512 devices in a mesh: gx: 8 (over z), gy: 8 (over x, core), gz: 8 (over y).
Axes of the slice: x: 4, y: 8, z: 8, core: 2. Of those that a mesh axis runs over, the one named last changes fastest.
Arguments:
- density: float32 [64, 64, 1024], P('gz', 'gy', 'gx'), may hold values from 0.9 to 1.1
- velocity: float32 [3, 64, 64, 1024], P(None, 'gz', 'gy', 'gx'), may hold values from -1.25 to 1.25
- solid: int32 [64, 64, 1024], P('gz', 'gy', 'gx'), may hold values from 0 to 1, as said below
- owner_map: int32 [8, 8, 8, 64, 1], P('gx', 'gy', 'gz'), may hold values from 0 to 63; in each aligned block of 64 rows (0 to 63, 64 to 127, ..., all dimensions but the last counted through in order) at most 2 rows name the same one
- slot_map: int32 [8, 8, 8, 64, 1], P('gx', 'gy', 'gz'), may hold values from 0 to 15
Outputs:
- final_moments: float32 [10, 64, 64, 1024], P(None, 'gz', 'gy', 'gx')
- relaxation: float32 [64, 64, 1024], P('gz', 'gy', 'gx')
- coarse_sums: float32 [8, 8, 8, 16, 160], P('gx', 'gy', 'gz')
The draws below stay inside these ranges and needn't reach their ends.
Inputs may be any that keep to these rules, and one draw needn't show every extreme that they name: 1 marks a solid cell; every cell of the vertical layer 0 is solid, and above it a column is solid below a building height that is constant over footprints of 4 spanwise by 4 streamwise columns. `owner_map`: of the 64 fine blocks of one device, at most 2 name the same owner.
All inputs are finite; a program needn't handle non-finite values.
Results may differ from the reference program's by a relative error of at most 0.0001.
Values sent between devices are 32-bit elements; how exact they have to be, the bound alone decides.
No kernel may reach another device: no remote copies, remote signals or barrier semaphores. Data moves between devices by JAX's collectives and lax.ppermute only.
A program may use at most 64 MiB of HBM per device.

```python
import math
import jax
import jax.numpy as jnp
import numpy as np
from jax import lax

CX = 128
CY = 8
CZ = 8
ITERS = 2
NSUB = 64
SLOTS = 16
CAP = 2
SUBCELLS = 16
NX = 1024
NY = 64
NZ = 64
N_GX = 8
N_GY = 8
N_GZ = 8


def draw_solid(key, part):
    key = jax.random.fold_in(key, 11)
    heights = jax.random.randint(key, (NY // 4, NX // 4), 0, max(NZ // 4, 4))
    columns = jnp.repeat(jnp.repeat(heights, 4, axis=0), 4, axis=1)
    levels = jnp.arange(NZ, dtype=jnp.int32)
    solid_cells = (levels[:, None, None] < columns[None, :, :]) | (levels[:, None, None] == 0)
    return solid_cells.astype(jnp.int32)


def with_ends(entries, own_key, smallest, top_value):
    longest = entries.shape.index(max(entries.shape))
    spots = []
    for shift in (0, 1):
        where = [jax.random.randint(jax.random.fold_in(own_key, axis), (), 0, length) for axis, length in enumerate(entries.shape)]
        where[longest] = (where[longest] + shift) % entries.shape[longest]
        spots.append(tuple(where))
    return entries.at[spots[0]].set(smallest).at[spots[1]].set(top_value)


def block_scale(stream_key, shape, split, low, top_value):
    factor_of = 1.0
    for dim, parts in split:
        draws = jax.random.uniform(jax.random.fold_in(jax.random.fold_in(stream_key, 6), dim), (parts,), jnp.float32, low / len(split), top_value / len(split))
        factor_of = factor_of * jnp.repeat(jnp.exp(draws), shape[dim] // parts).reshape((-1,) + (1,) * (len(shape) - 1 - dim))
    return factor_of


def deal_out(stream_key, own, number, rows, number_of, top, limit, lean):
    ranking = jax.random.permutation(stream_key, number_of)
    packed, usual = shares(number_of, rows * top, limit, lean, True), shares(number_of, rows * top, limit, lean, False)
    places = jnp.arange(number_of)

    def named(tallies, turn):
        used = int((tallies > 0).sum())
        fixed = max(1, used // 4)
        moved = fixed + (places - fixed + turn * (used - fixed)) % max(1, number_of - fixed)
        return jnp.zeros((number_of,), jnp.int32).at[ranking[jnp.where(places < fixed, places, moved)]].set(jnp.asarray(tallies, jnp.int32))

    tallies = jnp.where(number % 4 == 0, named(packed, number // 4), named(usual, number - number // 4 - 1))
    mixed = jax.random.permutation(jax.random.fold_in(own, 3), number_of)
    giver, receiver = mixed[0:number_of // 2 * 2:2], mixed[1:number_of // 2 * 2:2]
    margin = jnp.minimum(tallies[giver] - 1, limit - tallies[receiver]) // 2
    margin = jnp.where((giver == ranking[0]) | (receiver == ranking[0]) | (tallies[receiver] == 0), 0, jnp.maximum(margin, 0))
    moved = jax.random.randint(jax.random.fold_in(own, 4), (number_of // 2,), 0, 1 << 20) % (margin + 1)
    tallies = tallies.at[giver].add(-moved).at[receiver].add(moved)
    labels = jnp.searchsorted(jnp.cumsum(tallies), jnp.arange(rows * top), side="right").astype(jnp.int32)
    grid = labels.reshape(top, rows).T
    grid = grid[jax.random.permutation(jax.random.fold_in(own, 1), rows)]
    turn = jax.random.randint(jax.random.fold_in(own, 2), (rows, 1), 0, top)
    return jnp.take_along_axis(grid, (jnp.arange(top)[None, :] + turn) % top, axis=1)


def shares(number_of, total, bound, skew, full):
    weights = [(1 << 20) // math.isqrt(rank ** skew) + 1 for rank in range(1, number_of + 1)]
    largest = bound if full else min(bound, max(-(-total // number_of), total * weights[0] // sum(weights)))
    least = 1 if total - largest >= number_of - 1 else 0
    holding, surplus = [largest] + [least] * (number_of - 1), total - largest - least * (number_of - 1)
    while surplus > 0:
        free = [i for i in range(1, number_of) if holding[i] < largest] or [i for i in range(1, number_of) if holding[i] < bound]
        whole, left = sum([weights[i] for i in free]), surplus
        for i in free:
            extra = min(bound - holding[i], max(1, left * weights[i] // whole), surplus)
            holding[i] = holding[i] + extra
            surplus = surplus - extra
    return np.array(holding)


def normal_values(key, shape, spread, bound, cuts=(), held_as=jnp.bfloat16):
    factor_of = block_scale(key, shape, cuts, -0.22, 0.18) if cuts else 1.0
    drawn = jax.random.normal(key, shape, jnp.float32) * spread * factor_of
    return jnp.minimum(jnp.maximum(drawn, -bound), bound).astype(held_as)


def setup_inputs(seed: int = 0) -> dict:
    arg_keys = jax.random.split(jax.random.key(seed), 6)
    density = jnp.clip(0.9 + 0.20000005 * jax.random.uniform(arg_keys[0], (NZ, NY, NX), jnp.float32) ** block_scale(arg_keys[0], (NZ, NY, NX), ((0, 8), (1, 8), (2, 8)), -0.2, 0.2), 0.9, 1.1)
    velocity = normal_values(arg_keys[1], (3, NZ, NY, NX), 0.08, 1.25, ((1, 8), (2, 8), (3, 8)), jnp.float32)
    solid = draw_solid(jax.random.fold_in(arg_keys[5], 71), 0)
    owner_map_keys = jax.random.split(jax.random.fold_in(arg_keys[3], 1), N_GX * N_GY * N_GZ * NSUB // NSUB)
    owner_map_turns = jax.random.permutation(jax.random.fold_in(arg_keys[3], 3), N_GX * N_GY * N_GZ * NSUB // NSUB)
    owner_map = jax.vmap(lambda own, number: deal_out(jax.random.fold_in(arg_keys[3], 2), own, number, NSUB, N_GY * N_GZ, 1, CAP, 2))(owner_map_keys, owner_map_turns).reshape((N_GX, N_GY, N_GZ, NSUB, 1))
    slot_map = with_ends(jax.random.randint(arg_keys[4], (N_GX, N_GY, N_GZ, NSUB, 1), 0, SLOTS), jax.random.fold_in(arg_keys[4], 1), 0, SLOTS - 1).astype(jnp.int32)
    return dict(density=density, velocity=velocity, solid=solid, owner_map=owner_map, slot_map=slot_map)


WALE_COEFF = 0.5
BASE_VISCOSITY = 0.01
WALE_FLOOR = 1e-10
STRESS_PAIRS = ((0, 0), (1, 1), (2, 2), (0, 1), (0, 2), (1, 2))

def lattice_tables():
    directions = np.array([[0, 0, 0], [1, 0, 0], [-1, 0, 0], [0, 1, 0], [0, -1, 0], [0, 0, 1], [0, 0, -1], [1, 1, 0], [-1, -1, 0], [1, -1, 0], [-1, 1, 0], [1, 0, 1], [-1, 0, -1], [1, 0, -1], [-1, 0, 1], [0, 1, 1], [0, -1, -1], [0, 1, -1], [0, -1, 1]])
    recon_table = np.zeros((19, 10))
    moment_table = np.zeros((10, 19))
    for number in range(19):
        vector = directions[number]
        square = float(np.dot(vector, vector))
        weight = 1.0 / 3.0 if square == 0 else 1.0 / 18.0 if square == 1 else 1.0 / 36.0
        recon_table[number, 0] = weight * (1.0 - 1.5 * (square - 1.0))
        recon_table[number, 1:4] = 3.0 * weight * vector
        moment_table[0, number] = 1.0
        moment_table[1:4, number] = vector
        for column, stress_pair in enumerate(STRESS_PAIRS):
            left_axis, right_axis = stress_pair
            product = float(vector[left_axis] * vector[right_axis])
            moment_table[4 + column, number] = product
            if left_axis == right_axis:
                recon_table[number, 4 + column] = 4.5 * weight * (product - 1.0 / 3.0)
            else:
                recon_table[number, 4 + column] = 9.0 * weight * product
    return (directions, jnp.asarray(recon_table, jnp.float32), jnp.asarray(moment_table, jnp.float32))

def initial_state(density, velocity, fluid):
    momentum = density * velocity * fluid
    members = [density, momentum[0], momentum[1], momentum[2]]
    for left_axis, right_axis in STRESS_PAIRS:
        balance = momentum[left_axis] * momentum[right_axis] / density
        if left_axis == right_axis:
            balance = balance + density / 3.0
        members.append(balance)
    return jnp.stack(members)

def interior(padded, along, offset):
    window = [slice(None)] + [slice(1, padded.shape[1 + dimension] - 1) for dimension in range(3)]
    window[1 + along] = slice(1 + offset, padded.shape[1 + along] - 1 + offset)
    return padded[tuple(window)]

def wale_relaxation(padded):
    forward = [interior(padded, along, 1) for along in range(3)]
    backward = [interior(padded, along, -1) for along in range(3)]
    gradient = [[0.5 * (forward[column_axis][row_axis] - backward[column_axis][row_axis]) for column_axis in range(3)] for row_axis in range(3)]
    squared = [[gradient[row_axis][0] * gradient[0][column_axis] + gradient[row_axis][1] * gradient[1][column_axis] + gradient[row_axis][2] * gradient[2][column_axis] for column_axis in range(3)] for row_axis in range(3)]
    trace_sq = squared[0][0] + squared[1][1] + squared[2][2]
    strain_norm = 0.0
    deviator_norm = 0.0
    for row_axis in range(3):
        for column_axis in range(3):
            strain = 0.5 * (gradient[row_axis][column_axis] + gradient[column_axis][row_axis])
            deviator = 0.5 * (squared[row_axis][column_axis] + squared[column_axis][row_axis])
            if row_axis == column_axis:
                deviator = deviator - trace_sq / 3.0
            strain_norm = strain_norm + strain * strain
            deviator_norm = deviator_norm + deviator * deviator
    root_dev = jnp.sqrt(deviator_norm)
    eddy_viscosity = WALE_COEFF * WALE_COEFF * deviator_norm * root_dev / (strain_norm * strain_norm * jnp.sqrt(strain_norm) + deviator_norm * jnp.sqrt(root_dev) + WALE_FLOOR)
    return 0.5 + 3.0 * (BASE_VISCOSITY + eddy_viscosity)

def collide(state, relaxation):
    density = state[0]
    momentum = state[1:4]
    retained = 1.0 - 1.0 / relaxation
    members = [density, momentum[0], momentum[1], momentum[2]]
    for column, stress_pair in enumerate(STRESS_PAIRS):
        left_axis, right_axis = stress_pair
        balance = momentum[left_axis] * momentum[right_axis] / density
        if left_axis == right_axis:
            balance = balance + density / 3.0
        members.append(balance + retained * (state[4 + column] - balance))
    return jnp.stack(members)

def stream(post_pad, directions, recon_table, moment_table):
    size_a = post_pad.shape[1] - 2
    size_b = post_pad.shape[2] - 2
    size_c = post_pad.shape[3] - 2
    populations = jnp.einsum('qm,mxyz->qxyz', recon_table, post_pad, precision=lax.Precision.HIGHEST)
    pieces = []
    for number in range(19):
        start_a = 1 - int(directions[number][0])
        start_b = 1 - int(directions[number][1])
        start_c = 1 - int(directions[number][2])
        pieces.append(populations[number, start_a:start_a + size_a, start_b:start_b + size_b, start_c:start_c + size_c])
    moved = jnp.stack(pieces)
    return jnp.einsum('mq,qxyz->mxyz', moment_table, moved, precision=lax.Precision.HIGHEST)

def rest_solids(state, fluid):
    density = state[0]
    members = [density, state[1] * fluid, state[2] * fluid, state[3] * fluid]
    for column, stress_pair in enumerate(STRESS_PAIRS):
        if stress_pair[0] == stress_pair[1]:
            members.append(fluid * state[4 + column] + (1.0 - fluid) * density / 3.0)
        else:
            members.append(fluid * state[4 + column])
    return jnp.stack(members)

def wrap_pad(field):
    return jnp.pad(field, ((0, 0), (1, 1), (1, 1), (1, 1)), mode='wrap')

def reference(density, velocity, solid, owner_map, slot_map):
    fluid = 1.0 - solid.astype(jnp.float32)
    directions, recon_table, moment_table = lattice_tables()
    state = initial_state(density, velocity, fluid)
    relaxation = density
    for step in range(ITERS):
        speed = state[1:4] / state[0]
        relaxation = wale_relaxation(wrap_pad(speed))
        post = collide(state, relaxation)
        state = rest_solids(stream(wrap_pad(post), directions, recon_table, moment_table), fluid)
    restricted = state.reshape(10, NZ // 2, 2, NY // 2, 2, NX // 2, 2).mean(axis=(2, 4, 6))
    layer_count = CX // (2 * NSUB)
    blocks = restricted.reshape(10, N_GZ, CZ // 2, N_GY, CY // 2, N_GX, NSUB, layer_count)
    blocks = blocks.transpose(5, 3, 1, 6, 0, 2, 4, 7).reshape(N_GX, N_GY * N_GZ * NSUB, 10 * SUBCELLS)
    target = owner_map.reshape(N_GX, -1) * SLOTS + slot_map.reshape(N_GX, -1)
    slot_ids = jnp.arange(N_GY * N_GZ * SLOTS, dtype=jnp.int32)
    placing = (slot_ids[None, :, None] == target[:, None, :]).astype(jnp.float32)
    coarse = jnp.einsum('grs,gsc->grc', placing, blocks, precision=lax.Precision.HIGHEST)
    return (state, relaxation, coarse.reshape(N_GX, N_GY, N_GZ, SLOTS, 10 * SUBCELLS))
```

```python
import jax
import jax.numpy as jnp
from jax import lax
from jax.experimental import pallas as pl
from jax.experimental.pallas import tpu as pltpu
from jax.sharding import PartitionSpec as P

SLOTS = 16
WALE_COEFF = 0.5
BASE_VISCOSITY = 0.01
WALE_FLOOR = 1e-10
VMEM = pl.BlockSpec(memory_space=pltpu.VMEM)
PARAMS = pltpu.CompilerParams(vmem_limit_bytes=48 * 1024 * 1024)


def f32(*shape):
    return jax.ShapeDtypeStruct(shape, jnp.float32)


def roll(value, shift, axis):
    size = value.shape[axis]
    if isinstance(shift, int):
        shift = shift % size
        if shift == 0:
            return value
    return pltpu.roll(value, shift, axis)


def is_even(axis):
    return lax.rem(lax.axis_index(axis), 2) == 0


def swap(high_face, low_face, axis):
    count = lax.axis_size(axis)
    first = [(i, i ^ 1) for i in range(count)]
    second = [(i, (((i + 1) % count) ^ 1) - 1 if ((i + 1) % count) ^ 1 else count - 1) for i in range(count)]
    return lax.ppermute(high_face, axis, first), lax.ppermute(low_face, axis, second)


def pack_vertical(density, velocity, solid, first, second):
    even = is_even("gz")
    for out, upper in ((first, even), (second, jnp.logical_not(even))):
        planes = pl.ds(jnp.where(upper, 4, 0), 4)
        fluid = 1.0 - solid[planes].astype(jnp.float32)
        out[0] = density[planes]
        for axis in range(3):
            out[1 + axis] = velocity[axis, planes] * fluid
        out[4] = fluid


def pack_spanwise(density, velocity, solid, got_first, got_second, planes, first, second):
    even_z = is_even("gz")
    even_y = is_even("gy")
    fluid = 1.0 - solid[...].astype(jnp.float32)
    planes[0, 4:12] = density[...]
    for axis in range(3):
        planes[1 + axis, 4:12] = velocity[axis] * fluid
    planes[4, 4:12] = fluid
    for field in range(5):
        planes[field, 12:16] = jnp.where(even_z, got_first[field], got_second[field])
        planes[field, 0:4] = jnp.where(even_z, got_second[field], got_first[field])
    front = lax.broadcasted_iota(jnp.int32, (8, 128), 0) < 4
    for field in range(5):
        for pair in range(8):
            one = planes[field, 2 * pair]
            two = planes[field, 2 * pair + 1]
            high = jnp.where(front, roll(one, 4, 0), two)
            low = jnp.where(front, one, roll(two, 4, 0))
            first[field, pair] = jnp.where(even_y, high, low)
            second[field, pair] = jnp.where(even_y, low, high)


def pack_streamwise(planes, got_first, got_second, window, strip, first, second):
    even_y = is_even("gy")
    even_x = is_even("gx")
    front = lax.broadcasted_iota(jnp.int32, (8, 128), 0) < 4
    lane = lax.broadcasted_iota(jnp.int32, (16, 128), 1)
    group, spot = lane // 16, lane % 16
    for field in range(5):
        for pair in range(8):
            above = jnp.where(even_y, got_first[field, pair], got_second[field, pair])
            below = jnp.where(even_y, got_second[field, pair], got_first[field, pair])
            window[field, 2 * pair, 0:8] = planes[field, 2 * pair]
            window[field, 2 * pair + 1, 0:8] = planes[field, 2 * pair + 1]
            window[field, 2 * pair, 8:16] = jnp.where(front, above, roll(below, 4, 0))
            window[field, 2 * pair + 1, 8:16] = jnp.where(front, roll(above, 4, 0), below)
    quarter = lax.broadcasted_iota(jnp.int32, (8, 128), 1) % 16 // 4
    for field in range(5):
        to_right = jnp.zeros((8, 128), jnp.float32)
        to_left = jnp.zeros((8, 128), jnp.float32)
        for half in range(2):
            own = jnp.zeros((16, 128), jnp.float32)
            for number in range(8):
                cells = window[field, 2 * number + half]
                here = group == number
                own = jnp.where(here & (spot < 4), roll(cells, 16 * number + 4, 1), own)
                own = jnp.where(here & (spot >= 12), roll(cells, 16 * number + 12, 1), own)
            strip[field, half] = own
            for part in range(2):
                place = 2 * half + part
                rows = own[8 * part : 8 * part + 8]
                to_right = jnp.where(quarter == place, roll(rows, 4 * place, 1), to_right)
                to_left = jnp.where(quarter == place, roll(rows, 4 * place - 12, 1), to_left)
        first[field] = jnp.where(even_x, to_right, to_left)
        second[field] = jnp.where(even_x, to_left, to_right)


def wale(doubled):
    (g00, g01, g02), (g10, g11, g12), (g20, g21, g22) = doubled
    s01, s02, s12 = g01 + g10, g02 + g20, g12 + g21
    q0, q1, q2 = g00 * g00, g11 * g11, g22 * g22
    strain = 0.25 * ((q0 + q1 + q2) + 0.5 * (s01 * s01 + s02 * s02 + s12 * s12))
    p01, p02, p12 = g01 * g10, g02 * g20, g12 * g21
    d0, d1, d2 = q0 + (p01 + p02), q1 + (p01 + p12), q2 + (p02 + p12)
    third = (d0 + d1 + d2) * (1.0 / 3.0)
    d0, d1, d2 = d0 - third, d1 - third, d2 - third
    d01 = (g00 + g11) * s01 + (g02 * g21 + g12 * g20)
    d02 = (g00 + g22) * s02 + (g01 * g12 + g21 * g10)
    d12 = (g11 + g22) * s12 + (g10 * g02 + g20 * g01)
    deviator = 0.0625 * ((d0 * d0 + d1 * d1 + d2 * d2) + 0.5 * (d01 * d01 + d02 * d02 + d12 * d12))
    root = jnp.sqrt(deviator)
    eddy = (WALE_COEFF * WALE_COEFF) * deviator * root / (
        strain * strain * jnp.sqrt(strain) + deviator * jnp.sqrt(root) + WALE_FLOOR
    )
    return 0.5 + 3.0 * (BASE_VISCOSITY + eddy)


def collide(momentum, speed, stress, relaxation):
    retained = 1.0 - 1.0 / relaxation
    post = []
    for column, (one, two) in enumerate(((0, 0), (1, 1), (2, 2), (0, 1), (0, 2), (1, 2))):
        balance = momentum[one] * speed[two]
        post.append(balance + retained * (stress[column] - balance))
    return post


def leaving(density, momentum, post):
    t36 = density * (1.0 / 36.0) - (post[0] + post[1] + post[2]) * (1.0 / 24.0)
    az, ay, ax = (0.125 * post[k] for k in range(3))
    rzy, rzx, ryx = (0.25 * post[k] for k in range(3, 6))
    nz, ny, nx = ((1.0 / 12.0) * momentum[k] for k in range(3))
    bz, by, bx = t36 + az, t36 + ay, t36 + ax

    def edges(base, cross, one, two):
        plus, minus = base + cross, base - cross
        both, apart = one + two, one - two
        return plus + both, plus - both, minus + apart, minus - apart

    def up(value):
        return roll(value, 1, 0)

    def down(value):
        return roll(value, -1, 0)

    zpp, zmm, zpm, zmp = edges(bz + ay, rzy, nz, ny)
    y_zp = (up(zpp), down(zpm))
    y_zm = (up(zmp), down(zmm))
    xpp, xmm, xpm, xmp = edges(bz + ax, rzx, nz, nx)
    ypp, ymm, ypm, ymp = edges(by + ax, ryx, ny, nx)
    y_plus, y_minus = up(2.0 * (by + ny)), down(2.0 * (by - ny))
    ypp, ymp = up(ypp), down(ymp)
    ypm, ymm = up(ypm), down(ymm)
    x_plus, x_minus = 2.0 * (bx + nx), 2.0 * (bx - nx)
    syy_plus, syy_minus = ypp + ymp, ypm + ymm
    right = (x_plus + syy_plus, ypp - ymp, syy_plus, xpp, xmp)
    left = (x_minus + syy_minus, ypm - ymm, syy_minus, xpm, xmm)
    stay = (12.0 * t36, y_plus, y_minus, 2.0 * (bz + nz), y_zp, 2.0 * (bz - nz), y_zm)
    return stay, right, left


def plane_sums(stay, right, left):
    rest, y_plus, y_minus, z_plus, y_zp, z_minus, y_zm = stay
    syy = y_plus + y_minus
    sxx = right[0] + left[0]
    sums = [
        (rest + syy) + sxx,
        (y_plus - y_minus) + (right[1] + left[1]),
        right[0] - left[0],
        syy + (right[2] + left[2]),
        sxx,
        right[1] - left[1],
    ]
    for face, (one, two), plus, minus in ((z_plus, y_zp, right[3], left[3]), (z_minus, y_zm, right[4], left[4])):
        yy, xx = one + two, plus + minus
        sums += [face + (yy + xx), one - two, plus - minus, yy, xx]
    return sums


def gather_state(here, below, above, fluid):
    density = here[0] + (below[0] + above[0])
    third = density * (1.0 / 3.0)
    momentum = [
        fluid * (below[0] - above[0]),
        fluid * (here[1] + (below[1] + above[1])),
        fluid * (here[2] + (below[2] + above[2])),
    ]
    stress = [
        fluid * ((below[0] + above[0]) - third),
        fluid * ((here[3] + (below[3] + above[3])) - third),
        fluid * ((here[4] + (below[4] + above[4])) - third),
        fluid * (below[1] - above[1]),
        fluid * (below[2] - above[2]),
        fluid * here[5],
    ]
    return density, momentum, stress, third


def two_steps(
    window, own_strip, got_first, got_second, owners, slots, moments, relaxation_out, outgoing,
    state, sums, strip, strip_sums, edge, pooled,
):
    even_x = is_even("gx")
    lane = lax.broadcasted_iota(jnp.int32, (16, 128), 1)
    spot = lane % 16
    first_lane, last_lane = lane == 0, lane == 127
    quarter = lax.broadcasted_iota(jnp.int32, (8, 128), 1) % 16 // 4

    for field in range(5):
        from_right = jnp.where(even_x, got_first[field], got_second[field])
        from_left = jnp.where(even_x, got_second[field], got_first[field])
        for half in range(2):
            for part in range(2):
                place = 2 * half + part
                rows = slice(8 * part, 8 * part + 8)
                own = own_strip[field, half, rows]
                own = jnp.where(quarter == 1, roll(from_right, 4 - 4 * place, 1), own)
                strip[field, half, rows] = jnp.where(quarter == 2, roll(from_left, 8 - 4 * place, 1), own)

    def first_state(ref, where):
        density = ref[(0,) + where]
        speed = [ref[(1 + k,) + where] for k in range(3)]
        momentum = [density * speed[k] for k in range(3)]
        stress = [
            momentum[one] * speed[two] for one, two in ((0, 0), (1, 1), (2, 2), (0, 1), (0, 2), (1, 2))
        ]
        return density, speed, momentum, stress

    def strip_above(ref, number, half):
        return ref[number, 1] if half == 0 else roll(ref[number, 0], -16, 1)

    def strip_below(ref, number, half):
        return ref[number, 0] if half == 1 else roll(ref[number, 1], 16, 1)

    def row_differences(speed):
        return [roll(value, -1, 0) - roll(value, 1, 0) for value in speed]

    def strip_pass(step, half):
        if step == 0:
            density, speed, momentum, stress = first_state(strip, (half,))
        else:
            density = strip[0, half]
            speed = [strip[1 + k, half] for k in range(3)]
            momentum = [strip[5 + k, half] for k in range(3)]
            stress = [strip[8 + k, half] for k in range(6)]
        dz = [strip_above(strip, 1 + k, half) - strip_below(strip, 1 + k, half) for k in range(3)]
        dy = row_differences(speed)
        dx = [roll(value, -1, 1) - roll(value, 1, 1) for value in speed]
        relaxation = wale([[dz[k], dy[k], dx[k]] for k in range(3)])
        stay, right, left = leaving(density, momentum, collide(momentum, speed, stress, relaxation))
        for k in range(5):
            edge[k, half] = right[k]
            edge[5 + k, half] = left[k]
        if step == 0:
            moved_right = [roll(value, 1, 1) for value in right]
            moved_left = [roll(value, -1, 1) for value in left]
            for k, value in enumerate(plane_sums(stay, moved_right, moved_left)):
                strip_sums[k, half] = value

    def from_left_lane(value, ref, number, half, turn):
        return jnp.where(first_lane, roll(ref[number, half], 117 - turn, 1), roll(value, 1, 1))

    def from_right_lane(value, ref, number, half, turn):
        return jnp.where(last_lane, roll(ref[number, half], 123 - turn, 1), roll(value, -1, 1))

    def plane_pass(step, plane, speeds):
        half, turn = lax.rem(plane, 2), lax.div(plane, 2) * 16
        if step == 0:
            density, speed, momentum, stress = first_state(window, (plane,))
        else:
            density = state[0, plane]
            speed = [state[1 + k, plane] for k in range(3)]
            momentum = [state[4 + k, plane] for k in range(3)]
            stress = [state[7 + k, plane] for k in range(6)]
        dz = [speeds[1 + k, plane + 1] - speeds[1 + k, plane - 1] for k in range(3)]
        dy = row_differences(speed)
        dx = [
            from_right_lane(speed[k], strip, 1 + k, half, turn) - from_left_lane(speed[k], strip, 1 + k, half, turn)
            for k in range(3)
        ]
        relaxation = wale([[dz[k], dy[k], dx[k]] for k in range(3)])
        stay, right, left = leaving(density, momentum, collide(momentum, speed, stress, relaxation))
        return relaxation, stay, right, left, half, turn

    def move_lanes(right, left, half, turn):
        moved_right = [from_left_lane(value, edge, k, half, turn) for k, value in enumerate(right)]
        moved_left = [from_right_lane(value, edge, 5 + k, half, turn) for k, value in enumerate(left)]
        return moved_right, moved_left

    for half in range(2):
        strip_pass(0, half)

    def first_sums(plane, carry):
        _, stay, right, left, half, turn = plane_pass(0, plane, window)
        moved_right, moved_left = move_lanes(right, left, half, turn)
        for k, value in enumerate(plane_sums(stay, moved_right, moved_left)):
            sums[k, plane] = value
        return carry

    lax.fori_loop(1, 15, first_sums, 0)

    def first_gather(plane, carry):
        density, momentum, stress, _ = gather_state(
            [sums[k, plane] for k in range(6)],
            [sums[6 + k, plane - 1] for k in range(5)],
            [sums[11 + k, plane + 1] for k in range(5)],
            window[4, plane],
        )
        inverse = 1.0 / density
        state[0, plane] = density
        for k in range(3):
            state[1 + k, plane] = momentum[k] * inverse
            state[4 + k, plane] = momentum[k]
        for k in range(6):
            state[7 + k, plane] = stress[k]
        return carry

    lax.fori_loop(2, 14, first_gather, 0)

    for half in range(2):
        density, momentum, stress, _ = gather_state(
            [strip_sums[k, half] for k in range(6)],
            [strip_below(strip_sums, 6 + k, half) for k in range(5)],
            [strip_above(strip_sums, 11 + k, half) for k in range(5)],
            strip[4, half],
        )
        inverse = 1.0 / density
        strip[0, half] = density
        for k in range(3):
            strip[1 + k, half] = momentum[k] * inverse
            strip[5 + k, half] = momentum[k]
        for k in range(6):
            strip[8 + k, half] = stress[k]
    for half in range(2):
        strip_pass(1, half)

    def second_sums(plane, carry):
        relaxation, stay, right, left, half, turn = plane_pass(1, plane, state)
        moved_right, moved_left = move_lanes(right, left, half, turn)
        for k, value in enumerate(plane_sums(stay, moved_right, moved_left)):
            sums[k, plane] = value

        @pl.when((plane >= 4) & (plane < 12))
        def _():
            relaxation_out[plane - 4] = relaxation[0:8]

        return carry

    lax.fori_loop(3, 13, second_sums, 0)

    def second_gather(pair, carry):
        total = None
        for side in range(2):
            low = 2 * pair + side
            plane = low + 4
            density, momentum, stress, third = gather_state(
                [sums[k, plane, 0:8] for k in range(6)],
                [sums[6 + k, plane - 1, 0:8] for k in range(5)],
                [sums[11 + k, plane + 1, 0:8] for k in range(5)],
                window[4, plane, 0:8],
            )
            members = [density] + momentum + [stress[k] + third for k in range(3)] + stress[3:]
            for k in range(10):
                moments[k, low] = members[k]
            total = members if total is None else [one + two for one, two in zip(total, members)]
        for k in range(10):
            pooled[pl.ds(pl.multiple_of(k * 32 + pair * 8, 8), 8), :] = total[k]
        return carry

    lax.fori_loop(0, 4, second_gather, 0)

    blocks = 0.125 * (pooled[pl.ds(0, 160, stride=2), :] + pooled[pl.ds(1, 160, stride=2), :])
    owner_row = owners[0:1, :]
    lanes_a = lax.broadcasted_iota(jnp.int32, (128, 128), 0)
    lanes_b = lax.broadcasted_iota(jnp.int32, (128, 128), 1)
    owner_column = jnp.transpose(jnp.broadcast_to(owner_row, (128, 128)))
    earlier = (owner_column == owner_row) & (lanes_a // 2 < lanes_b // 2)
    rank = jnp.sum(earlier.astype(jnp.float32), axis=0, keepdims=True) * 0.5
    position = owner_row * 2 + rank.astype(jnp.int32)
    placing = (lanes_a == position).astype(jnp.float32)
    tags = 0.5 * (slots[0:1, :] + 1).astype(jnp.float32)
    payload = jnp.concatenate([blocks, jnp.broadcast_to(tags, (8, 128))], axis=0)
    outgoing[...] = lax.dot_general(
        placing, payload, (((1,), (1,)), ((), ())),
        precision=lax.Precision.HIGHEST, preferred_element_type=jnp.float32,
    )


def sum_slots(arrived, coarse):
    rows = arrived.shape[0]
    slot = lax.broadcasted_iota(jnp.int32, (rows, SLOTS), 1).astype(jnp.float32)
    chosen = (arrived[:, 160:161] == slot + 1.0).astype(jnp.float32)
    coarse[...] = lax.dot_general(
        chosen, arrived[:, 0:160], (((0,), (0,)), ((), ())),
        precision=lax.Precision.HIGHEST, preferred_element_type=jnp.float32,
    )


def call(kernel, outs, name, scratch=()):
    return pl.pallas_call(
        kernel,
        out_shape=outs,
        scratch_shapes=list(scratch),
        compiler_params=PARAMS,
        name=name,
    )


def per_device(density, velocity, solid, owner_map, slot_map):
    first, second = call(pack_vertical, (f32(5, 4, 8, 128),) * 2, "pack_vertical")(density, velocity, solid)
    first, second = swap(first, second, "gz")
    planes, first, second = call(
        pack_spanwise, (f32(5, 16, 8, 128), f32(5, 8, 8, 128), f32(5, 8, 8, 128)), "pack_spanwise"
    )(density, velocity, solid, first, second)
    first, second = swap(first, second, "gy")
    window, strip, first, second = call(
        pack_streamwise,
        (f32(5, 16, 16, 128), f32(5, 2, 16, 128), f32(5, 8, 128), f32(5, 8, 128)),
        "pack_streamwise",
    )(planes, first, second)
    first, second = swap(first, second, "gx")
    owners = jnp.broadcast_to(jnp.repeat(owner_map.reshape(1, 64), 2, axis=1), (8, 128))
    slots = jnp.broadcast_to(jnp.repeat(slot_map.reshape(1, 64), 2, axis=1), (8, 128))
    moments, relaxation, outgoing = call(
        two_steps,
        (f32(10, 8, 8, 128), f32(8, 8, 128), f32(128, 168)),
        "two_steps",
        (
            pltpu.VMEM((13, 16, 16, 128), jnp.float32),
            pltpu.VMEM((16, 16, 16, 128), jnp.float32),
            pltpu.VMEM((14, 2, 16, 128), jnp.float32),
            pltpu.VMEM((16, 2, 16, 128), jnp.float32),
            pltpu.VMEM((10, 2, 16, 128), jnp.float32),
            pltpu.VMEM((320, 128), jnp.float32),
        ),
    )(window, strip, first, second, owners, slots)
    arrived = lax.all_to_all(
        outgoing.reshape(64, 2, 168), ("gy", "gz"), split_axis=0, concat_axis=0, tiled=True
    )
    coarse = call(sum_slots, f32(SLOTS, 160), "sum_slots")(arrived.reshape(128, 168))
    return moments, relaxation, coarse.reshape(1, 1, 1, SLOTS, 160)


def solution(mesh):
    return jax.shard_map(
        per_device,
        mesh=mesh,
        in_specs=(
            P("gz", "gy", "gx"),
            P(None, "gz", "gy", "gx"),
            P("gz", "gy", "gx"),
            P("gx", "gy", "gz", None, None),
            P("gx", "gy", "gz", None, None),
        ),
        out_specs=(P(None, "gz", "gy", "gx"), P("gz", "gy", "gx"), P("gx", "gy", "gz", None, None)),
        check_vma=False,
    )
```

```python
import jax
import jax.numpy as jnp
from jax import lax
from jax.experimental import pallas as pl
from jax.experimental.pallas import tpu as pltpu
from jax.sharding import PartitionSpec as P

SLOTS = 16
SPAN_Y = 8
SPAN_Z = 8
WALE_COEFF = 0.5
BASE_VISCOSITY = 0.01
WALE_FLOOR = 1e-10


def f32(*shape):
    return jax.ShapeDtypeStruct(shape, jnp.float32)


def roll(value, shift, axis):
    size = value.shape[axis]
    if isinstance(shift, int):
        shift = shift % size
        if shift == 0:
            return value
    return pltpu.roll(value, shift, axis)


def is_even(axis):
    return lax.rem(lax.axis_index(axis), 2) == 0


def swap(near, far, axis):
    count = lax.axis_size(axis)
    near_pairs = [(i, i ^ 1) for i in range(count)]
    far_pairs = [(i, (i + 1) % count if i % 2 else (i - 1) % count) for i in range(count)]
    far = lax.ppermute(far, axis, far_pairs)
    return lax.ppermute(near, axis, near_pairs), far


def pack_vertical(fields, near, far):
    even = is_even("gz")
    for field in range(5):
        near[field] = jnp.where(even, fields[field, 4:8], fields[field, 0:4])
        far[field] = jnp.where(even, fields[field, 0:4], fields[field, 4:8])


def pack_spanwise(fields, got_far, got_near, planes, near, far):
    even_z = is_even("gz")
    even_y = is_even("gy")
    front = lax.broadcasted_iota(jnp.int32, (8, 128), 0) < 4
    for field in range(5):
        planes[field, 4:12] = fields[field]
        planes[field, 12:16] = jnp.where(even_z, got_near[field], got_far[field])
        planes[field, 0:4] = jnp.where(even_z, got_far[field], got_near[field])
        for pair in range(8):
            one = planes[field, 2 * pair]
            two = planes[field, 2 * pair + 1]
            high = jnp.where(front, roll(one, 4, 0), two)
            low = jnp.where(front, one, roll(two, 4, 0))
            near[field, pair] = jnp.where(even_y, high, low)
            far[field, pair] = jnp.where(even_y, low, high)


def pack_streamwise(planes, got_far, got_near, window, faces, near, far):
    even_y = is_even("gy")
    even_x = is_even("gx")
    front = lax.broadcasted_iota(jnp.int32, (8, 128), 0) < 4
    lane = lax.broadcasted_iota(jnp.int32, (8, 128), 1)
    for field in range(5):
        own = [jnp.zeros((8, 128), jnp.float32) for _ in range(2)]
        for pair in range(8):
            above = jnp.where(even_y, got_near[field, pair], got_far[field, pair])
            below = jnp.where(even_y, got_far[field, pair], got_near[field, pair])
            outer = (jnp.where(front, above, roll(below, 4, 0)), jnp.where(front, roll(above, 4, 0), below))
            for side in range(2):
                plane = 2 * pair + side
                inner = planes[field, plane]
                window[field, plane, 0:8] = inner
                window[field, plane, 8:16] = outer[side]
                here = lane // 8 == plane
                own[0] = jnp.where(here, roll(inner, 8 * plane + 4, 1), own[0])
                own[1] = jnp.where(here, roll(outer[side], 8 * plane + 4, 1), own[1])
        faces[field, 0] = own[0]
        faces[field, 1] = own[1]
        even_spot = lane % 8 < 4
        to_right = jnp.where(even_spot, own[0], roll(own[1], 4, 1))
        to_left = jnp.where(even_spot, roll(own[0], -4, 1), own[1])
        near[field] = jnp.where(even_x, to_right, to_left)
        far[field] = jnp.where(even_x, to_left, to_right)


def place_blocks(owners_in, slots_in, placing, tags, owners, slots, arrived):
    copies = [
        pltpu.make_async_copy(source, target, arrived.at[number])
        for number, (source, target) in enumerate(((owners_in, owners), (slots_in, slots)))
    ]
    for copy in copies:
        copy.start()
    for copy in copies:
        copy.wait()
    row = lax.broadcasted_iota(jnp.int32, (64, 128), 0)
    block = lax.broadcasted_iota(jnp.int32, (64, 128), 1) // 2
    diagonal = lax.broadcasted_iota(jnp.int32, (64, 64), 0) == lax.broadcasted_iota(jnp.int32, (64, 64), 1)
    owner_column = jnp.sum(jnp.where(diagonal, owners[...].astype(jnp.float32), 0.0), axis=1, keepdims=True)
    slot_column = jnp.sum(jnp.where(diagonal, slots[...].astype(jnp.float32), 0.0), axis=1, keepdims=True)
    owner_row = jnp.sum(jnp.where(row == block, owner_column, 0.0), axis=0, keepdims=True)
    slot = jnp.sum(jnp.where(row == block, slot_column, 0.0), axis=0, keepdims=True)
    earlier = (owner_column == owner_row) & (row < block)
    owner = owner_row.astype(jnp.int32)
    rank = jnp.sum(jnp.where(earlier, 1.0, 0.0), axis=0, keepdims=True).astype(jnp.int32)
    position = (lax.rem(owner, SPAN_Z) * SPAN_Y + lax.div(owner, SPAN_Z)) * 2 + rank
    rows = lax.broadcasted_iota(jnp.int32, (128, 128), 0)
    placing[...] = (rows == position).astype(jnp.float32)
    tags[...] = jnp.broadcast_to(0.5 * (slot + 1.0), (16, 128))


def pick(chosen, values, contract):
    chosen = chosen.astype(jnp.bfloat16)
    total = None
    for _ in range(3):
        part = values.astype(jnp.bfloat16)
        values = values - part.astype(jnp.float32)
        product = lax.dot_general(chosen, part, (contract, ((), ())), preferred_element_type=jnp.float32)
        total = product if total is None else total + product
    return total


def wale(doubled):
    (g00, g01, g02), (g10, g11, g12), (g20, g21, g22) = doubled
    s01, s02, s12 = g01 + g10, g02 + g20, g12 + g21
    q0, q1, q2 = g00 * g00, g11 * g11, g22 * g22
    strain = 0.25 * ((q0 + q1 + q2) + 0.5 * (s01 * s01 + s02 * s02 + s12 * s12))
    p01, p02, p12 = g01 * g10, g02 * g20, g12 * g21
    d0, d1, d2 = q0 + (p01 + p02), q1 + (p01 + p12), q2 + (p02 + p12)
    third = (d0 + d1 + d2) * (1.0 / 3.0)
    d0, d1, d2 = d0 - third, d1 - third, d2 - third
    d01 = (g00 + g11) * s01 + (g02 * g21 + g12 * g20)
    d02 = (g00 + g22) * s02 + (g01 * g12 + g21 * g10)
    d12 = (g11 + g22) * s12 + (g10 * g02 + g20 * g01)
    deviator = 0.0625 * ((d0 * d0 + d1 * d1 + d2 * d2) + 0.5 * (d01 * d01 + d02 * d02 + d12 * d12))
    root = jnp.sqrt(deviator)
    eddy = (WALE_COEFF * WALE_COEFF) * deviator * root / (
        strain * strain * jnp.sqrt(strain) + deviator * jnp.sqrt(root) + WALE_FLOOR
    )
    return 0.5 + 3.0 * (BASE_VISCOSITY + eddy)


def collide(momentum, speed, stress, relaxation):
    retained = 1.0 - 1.0 / relaxation
    post = []
    for column, (one, two) in enumerate(((0, 0), (1, 1), (2, 2), (0, 1), (0, 2), (1, 2))):
        balance = momentum[one] * speed[two]
        post.append(balance + retained * (stress[column] - balance))
    return post


def leaving(density, momentum, post):
    t36 = density * (1.0 / 36.0) - (post[0] + post[1] + post[2]) * (1.0 / 24.0)
    az, ay, ax = (0.125 * post[k] for k in range(3))
    rzy, rzx, ryx = (0.25 * post[k] for k in range(3, 6))
    nz, ny, nx = ((1.0 / 12.0) * momentum[k] for k in range(3))
    bz, by, bx = t36 + az, t36 + ay, t36 + ax

    def edges(base, cross, one, two):
        plus, minus = base + cross, base - cross
        both, apart = one + two, one - two
        return plus + both, plus - both, minus + apart, minus - apart

    def up(value):
        return roll(value, 1, 0)

    def down(value):
        return roll(value, -1, 0)

    zpp, zmm, zpm, zmp = edges(bz + ay, rzy, nz, ny)
    y_zp = (up(zpp), down(zpm))
    y_zm = (up(zmp), down(zmm))
    xpp, xmm, xpm, xmp = edges(bz + ax, rzx, nz, nx)
    ypp, ymm, ypm, ymp = edges(by + ax, ryx, ny, nx)
    y_plus, y_minus = up(2.0 * (by + ny)), down(2.0 * (by - ny))
    ypp, ymp = up(ypp), down(ymp)
    ypm, ymm = up(ypm), down(ymm)
    x_plus, x_minus = 2.0 * (bx + nx), 2.0 * (bx - nx)
    syy_plus, syy_minus = ypp + ymp, ypm + ymm
    right = (x_plus + syy_plus, ypp - ymp, syy_plus, xpp, xmp)
    left = (x_minus + syy_minus, ypm - ymm, syy_minus, xpm, xmm)
    stay = (12.0 * t36, y_plus, y_minus, 2.0 * (bz + nz), y_zp, 2.0 * (bz - nz), y_zm)
    return stay, right, left


def plane_sums(stay, right, left):
    rest, y_plus, y_minus, z_plus, y_zp, z_minus, y_zm = stay
    syy = y_plus + y_minus
    sxx = right[0] + left[0]
    sums = [
        (rest + syy) + sxx,
        (y_plus - y_minus) + (right[1] + left[1]),
        right[0] - left[0],
        syy + (right[2] + left[2]),
        sxx,
        right[1] - left[1],
    ]
    for face, (one, two), plus, minus in ((z_plus, y_zp, right[3], left[3]), (z_minus, y_zm, right[4], left[4])):
        yy, xx = one + two, plus + minus
        sums += [face + (yy + xx), one - two, plus - minus, yy, xx]
    return sums


def gather_state(here, below, above, fluid):
    density = here[0] + (below[0] + above[0])
    third = density * (1.0 / 3.0)
    momentum = [
        fluid * (below[0] - above[0]),
        fluid * (here[1] + (below[1] + above[1])),
        fluid * (here[2] + (below[2] + above[2])),
    ]
    stress = [
        fluid * ((below[0] + above[0]) - third),
        fluid * ((here[3] + (below[3] + above[3])) - third),
        fluid * ((here[4] + (below[4] + above[4])) - third),
        fluid * (below[1] - above[1]),
        fluid * (below[2] - above[2]),
        fluid * here[5],
    ]
    return density, momentum, stress, third


def two_steps(
    window, faces, got_far, got_near, placing, tags, moments, relaxation_out, outgoing,
    state, sums, strip, strip_sums, edge, pooled,
):
    even_x = is_even("gx")
    lane = lax.broadcasted_iota(jnp.int32, (16, 128), 1)
    first_lane, last_lane = lane == 0, lane == 127
    quarter = lax.broadcasted_iota(jnp.int32, (8, 128), 1) % 16 // 4

    for field in range(5):
        from_right = jnp.where(even_x, got_near[field], got_far[field])
        from_left = jnp.where(even_x, got_far[field], got_near[field])
        for half in range(2):
            for part in range(2):
                own = faces[field, part]
                turn = 8 * half + 4 * part
                cells = jnp.where(quarter == 0, roll(own, -8 * half, 1), roll(own, 8 - 8 * half, 1))
                cells = jnp.where(quarter == 1, roll(from_right, 4 - turn, 1), cells)
                strip[field, half, 8 * part : 8 * part + 8] = jnp.where(
                    quarter == 2, roll(from_left, 8 - turn, 1), cells
                )

    def first_state(ref, where):
        density = ref[(0,) + where]
        speed = [ref[(1 + k,) + where] for k in range(3)]
        momentum = [density * speed[k] for k in range(3)]
        stress = [
            momentum[one] * speed[two] for one, two in ((0, 0), (1, 1), (2, 2), (0, 1), (0, 2), (1, 2))
        ]
        return density, speed, momentum, stress

    def strip_above(ref, number, half):
        return ref[number, 1] if half == 0 else roll(ref[number, 0], -16, 1)

    def strip_below(ref, number, half):
        return ref[number, 0] if half == 1 else roll(ref[number, 1], 16, 1)

    def row_differences(speed):
        return [roll(value, -1, 0) - roll(value, 1, 0) for value in speed]

    def strip_pass(step, half):
        if step == 0:
            density, speed, momentum, stress = first_state(strip, (half,))
        else:
            density = strip[0, half]
            speed = [strip[1 + k, half] for k in range(3)]
            momentum = [strip[5 + k, half] for k in range(3)]
            stress = [strip[8 + k, half] for k in range(6)]
        dz = [strip_above(strip, 1 + k, half) - strip_below(strip, 1 + k, half) for k in range(3)]
        dy = row_differences(speed)
        dx = [roll(value, -1, 1) - roll(value, 1, 1) for value in speed]
        relaxation = wale([[dz[k], dy[k], dx[k]] for k in range(3)])
        stay, right, left = leaving(density, momentum, collide(momentum, speed, stress, relaxation))
        for k in range(5):
            edge[k, half] = right[k]
            edge[5 + k, half] = left[k]
        if step == 0:
            moved_right = [roll(value, 1, 1) for value in right]
            moved_left = [roll(value, -1, 1) for value in left]
            for k, value in enumerate(plane_sums(stay, moved_right, moved_left)):
                strip_sums[k, half] = value

    def from_left_lane(value, ref, number, half, turn):
        return jnp.where(first_lane, roll(ref[number, half], 117 - turn, 1), roll(value, 1, 1))

    def from_right_lane(value, ref, number, half, turn):
        return jnp.where(last_lane, roll(ref[number, half], 123 - turn, 1), roll(value, -1, 1))

    def plane_pass(step, plane, speeds):
        half, turn = plane % 2, plane // 2 * 16
        if step == 0:
            density, speed, momentum, stress = first_state(window, (plane,))
        else:
            density = state[0, plane]
            speed = [state[1 + k, plane] for k in range(3)]
            momentum = [state[4 + k, plane] for k in range(3)]
            stress = [state[7 + k, plane] for k in range(6)]
        dz = [speeds[1 + k, plane + 1] - speeds[1 + k, plane - 1] for k in range(3)]
        dy = row_differences(speed)
        dx = [
            from_right_lane(speed[k], strip, 1 + k, half, turn) - from_left_lane(speed[k], strip, 1 + k, half, turn)
            for k in range(3)
        ]
        relaxation = wale([[dz[k], dy[k], dx[k]] for k in range(3)])
        stay, right, left = leaving(density, momentum, collide(momentum, speed, stress, relaxation))
        return relaxation, stay, right, left, half, turn

    def move_lanes(right, left, half, turn):
        moved_right = [from_left_lane(value, edge, k, half, turn) for k, value in enumerate(right)]
        moved_left = [from_right_lane(value, edge, 5 + k, half, turn) for k, value in enumerate(left)]
        return moved_right, moved_left

    for half in range(2):
        strip_pass(0, half)

    for plane in range(1, 15):
        _, stay, right, left, half, turn = plane_pass(0, plane, window)
        moved_right, moved_left = move_lanes(right, left, half, turn)
        for k, value in enumerate(plane_sums(stay, moved_right, moved_left)):
            sums[k, plane] = value

    for plane in range(2, 14):
        density, momentum, stress, _ = gather_state(
            [sums[k, plane] for k in range(6)],
            [sums[6 + k, plane - 1] for k in range(5)],
            [sums[11 + k, plane + 1] for k in range(5)],
            window[4, plane],
        )
        inverse = 1.0 / density
        state[0, plane] = density
        for k in range(3):
            state[1 + k, plane] = momentum[k] * inverse
            state[4 + k, plane] = momentum[k]
        for k in range(6):
            state[7 + k, plane] = stress[k]

    for half in range(2):
        density, momentum, stress, _ = gather_state(
            [strip_sums[k, half] for k in range(6)],
            [strip_below(strip_sums, 6 + k, half) for k in range(5)],
            [strip_above(strip_sums, 11 + k, half) for k in range(5)],
            strip[4, half],
        )
        inverse = 1.0 / density
        strip[0, half] = density
        for k in range(3):
            strip[1 + k, half] = momentum[k] * inverse
            strip[5 + k, half] = momentum[k]
        for k in range(6):
            strip[8 + k, half] = stress[k]
    for half in range(2):
        strip_pass(1, half)

    for plane in range(3, 13):
        relaxation, stay, right, left, half, turn = plane_pass(1, plane, state)
        moved_right, moved_left = move_lanes(right, left, half, turn)
        for k, value in enumerate(plane_sums(stay, moved_right, moved_left)):
            sums[k, plane] = value
        if 4 <= plane < 12:
            relaxation_out[plane - 4] = relaxation[0:8]

    for pair in range(4):
        total = None
        for side in range(2):
            low = 2 * pair + side
            plane = low + 4
            density, momentum, stress, third = gather_state(
                [sums[k, plane, 0:8] for k in range(6)],
                [sums[6 + k, plane - 1, 0:8] for k in range(5)],
                [sums[11 + k, plane + 1, 0:8] for k in range(5)],
                window[4, plane, 0:8],
            )
            members = [density] + momentum + [stress[k] + third for k in range(3)] + stress[3:]
            for k in range(10):
                moments[k, low] = members[k]
            total = members if total is None else [one + two for one, two in zip(total, members)]
        for k in range(10):
            pooled[k * 32 + pair * 8 : k * 32 + pair * 8 + 8, :] = total[k]

    blocks = 0.125 * (pooled[pl.ds(0, 160, stride=2), :] + pooled[pl.ds(1, 160, stride=2), :])
    payload = jnp.concatenate([blocks, tags[...]], axis=0)
    outgoing[...] = pick(placing[...], payload, ((1,), (1,)))


def sum_by_slot(arrived, outgoing):
    row = lax.broadcasted_iota(jnp.int32, (128, 128), 0)
    column = lax.broadcasted_iota(jnp.int32, (128, 128), 1)
    tag = jnp.broadcast_to(arrived[:, 160:161], (128, 128))
    chosen = (column // SLOTS == row // 2 % SPAN_Y) & (tag == (column % SLOTS + 1).astype(jnp.float32))
    outgoing[...] = pick(chosen.astype(jnp.float32), arrived[:, 0:160], ((0,), (0,)))


def sum_senders(arrived, coarse):
    total = arrived[0]
    for sender in range(1, arrived.shape[0]):
        total = total + arrived[sender]
    coarse[...] = total


def call(kernel, outs, name, scratch=(), in_hbm=0, vmem=48):
    extra = {"in_specs": [pl.BlockSpec(memory_space=pltpu.HBM)] * in_hbm} if in_hbm else {}
    return pl.pallas_call(
        kernel, out_shape=outs, scratch_shapes=list(scratch), name=name,
        compiler_params=pltpu.CompilerParams(vmem_limit_bytes=vmem * 1024 * 1024), **extra
    )


def per_device(density, velocity, solid, owner_map, slot_map):
    placing, tags = call(
        place_blocks,
        (f32(128, 128), f32(16, 128)),
        "place_blocks",
        (pltpu.VMEM((1, 64), jnp.int32), pltpu.VMEM((1, 64), jnp.int32), pltpu.SemaphoreType.DMA((2,))),
        2,
    )(owner_map.reshape(1, 64), slot_map.reshape(1, 64))
    fluid = 1.0 - solid.astype(jnp.float32)
    fields = jnp.concatenate([density[None], velocity * fluid, fluid[None]])
    near, far = call(pack_vertical, (f32(5, 4, 8, 128),) * 2, "pack_vertical")(fields)
    near, far = swap(near, far, "gz")
    planes, near, far = call(
        pack_spanwise, (f32(5, 16, 8, 128), f32(5, 8, 8, 128), f32(5, 8, 8, 128)), "pack_spanwise"
    )(fields, far, near)
    near, far = swap(near, far, "gy")
    window, faces, near, far = call(
        pack_streamwise,
        (f32(5, 16, 16, 128), f32(5, 2, 8, 128), f32(5, 8, 128), f32(5, 8, 128)),
        "pack_streamwise",
    )(planes, far, near)
    near, far = swap(near, far, "gx")
    moments, relaxation, outgoing = call(
        two_steps,
        (f32(10, 8, 8, 128), f32(8, 8, 128), f32(128, 176)),
        "two_steps",
        (
            pltpu.VMEM((13, 16, 16, 128), jnp.float32),
            pltpu.VMEM((16, 16, 16, 128), jnp.float32),
            pltpu.VMEM((14, 2, 16, 128), jnp.float32),
            pltpu.VMEM((16, 2, 16, 128), jnp.float32),
            pltpu.VMEM((10, 2, 16, 128), jnp.float32),
            pltpu.VMEM((320, 128), jnp.float32),
        ),
    )(window, faces, far, near, placing, tags)
    arrived = lax.all_to_all(outgoing.reshape(SPAN_Z, 2 * SPAN_Y, 176), "gz", split_axis=0, concat_axis=0, tiled=True)
    outgoing = call(sum_by_slot, f32(128, 160), "sum_by_slot")(arrived.reshape(128, 176))
    arrived = lax.all_to_all(outgoing.reshape(SPAN_Y, SLOTS, 160), "gy", split_axis=0, concat_axis=0, tiled=True)
    coarse = call(sum_senders, f32(SLOTS, 160), "sum_senders")(arrived)
    return moments, relaxation, coarse.reshape(1, 1, 1, SLOTS, 160)


def solution(mesh):
    return jax.shard_map(
        per_device,
        mesh=mesh,
        in_specs=(
            P("gz", "gy", "gx"),
            P(None, "gz", "gy", "gx"),
            P("gz", "gy", "gx"),
            P("gx", "gy", "gz", None, None),
            P("gx", "gy", "gz", None, None),
        ),
        out_specs=(P(None, "gz", "gy", "gx"), P("gz", "gy", "gx"), P("gx", "gy", "gz", None, None)),
        check_vma=False,
    )
```

```python
import jax
import jax.numpy as jnp
from jax import lax
from jax.experimental import pallas as pl
from jax.experimental.pallas import tpu as pltpu
from jax.sharding import PartitionSpec as P

SLOTS = 16
OWNERS = 64
WALE_COEFF = 0.5
BASE_VISCOSITY = 0.01
WALE_FLOOR = 1e-10


def f32(*shape):
    return jax.ShapeDtypeStruct(shape, jnp.float32)


def roll(value, shift, axis):
    size = value.shape[axis]
    if isinstance(shift, int):
        shift = shift % size
        if shift == 0:
            return value
    return pltpu.roll(value, shift, axis)


def is_even(axis):
    return lax.rem(lax.axis_index(axis), 2) == 0


def swap(near, far, axis):
    count = lax.axis_size(axis)
    near_pairs = [(i, i ^ 1) for i in range(count)]
    far_pairs = [(i, (i + 1) % count if i % 2 else (i - 1) % count) for i in range(count)]
    far = lax.ppermute(far, axis, far_pairs)
    return lax.ppermute(near, axis, near_pairs), far


def ring(high, low, axis):
    count = lax.axis_size(axis)
    below = lax.ppermute(high, axis, [(i, (i + 1) % count) for i in range(count)])
    above = lax.ppermute(low, axis, [((i + 1) % count, i) for i in range(count)])
    return below, above


def pack_vertical(scalars, velocity, near, far):
    even = is_even("gz")
    for out, upper in ((near, even), (far, jnp.logical_not(even))):
        planes = pl.ds(jnp.where(upper, 4, 0), 4)
        fluid = scalars[1, planes]
        out[0] = scalars[0, planes]
        for axis in range(3):
            out[1 + axis] = velocity[axis, planes] * fluid
        out[4] = fluid


def pack_spanwise(scalars, velocity, got_far, got_near, planes, high, low):
    even_z = is_even("gz")
    front = lax.broadcasted_iota(jnp.int32, (8, 128), 0) < 4
    fluid = scalars[1]
    for field in range(5):
        inner = scalars[0] if field == 0 else fluid if field == 4 else velocity[field - 1] * fluid
        planes[field, 4:12] = inner
        planes[field, 12:16] = jnp.where(even_z, got_near[field], got_far[field])
        planes[field, 0:4] = jnp.where(even_z, got_far[field], got_near[field])
        for pair in range(8):
            one = planes[field, 2 * pair]
            two = planes[field, 2 * pair + 1]
            high[field, pair] = jnp.where(front, roll(one, 4, 0), two)
            low[field, pair] = jnp.where(front, one, roll(two, 4, 0))


def pack_streamwise(planes, got_below, got_above, window, faces, near, far):
    even_x = is_even("gx")
    front = lax.broadcasted_iota(jnp.int32, (8, 128), 0) < 4
    lane = lax.broadcasted_iota(jnp.int32, (8, 128), 1)
    for field in range(5):
        own = [jnp.zeros((8, 128), jnp.float32) for _ in range(2)]
        for pair in range(8):
            above, below = got_above[field, pair], got_below[field, pair]
            outer = (jnp.where(front, above, roll(below, 4, 0)), jnp.where(front, roll(above, 4, 0), below))
            for side in range(2):
                plane = 2 * pair + side
                inner = planes[field, plane]
                window[field, plane, 0:8] = inner
                window[field, plane, 8:16] = outer[side]
                here = lane // 8 == plane
                own[0] = jnp.where(here, roll(inner, 8 * plane + 4, 1), own[0])
                own[1] = jnp.where(here, roll(outer[side], 8 * plane + 4, 1), own[1])
        faces[field, 0] = own[0]
        faces[field, 1] = own[1]
        even_spot = lane % 8 < 4
        to_right = jnp.where(even_spot, own[0], roll(own[1], 4, 1))
        to_left = jnp.where(even_spot, roll(own[0], -4, 1), own[1])
        near[field] = jnp.where(even_x, to_right, to_left)
        far[field] = jnp.where(even_x, to_left, to_right)


def place_blocks(owners_in, slots_in, placing, tags, owners, slots, arrived):
    copies = [
        pltpu.make_async_copy(source, target, arrived.at[number])
        for number, (source, target) in enumerate(((owners_in, owners), (slots_in, slots)))
    ]
    for copy in copies:
        copy.start()
    for copy in copies:
        copy.wait()
    row = lax.broadcasted_iota(jnp.int32, (64, 128), 0)
    block = lax.broadcasted_iota(jnp.int32, (64, 128), 1) // 2
    diagonal = lax.broadcasted_iota(jnp.int32, (64, 64), 0) == lax.broadcasted_iota(jnp.int32, (64, 64), 1)
    owner_column = jnp.sum(jnp.where(diagonal, owners[...].astype(jnp.float32), 0.0), axis=1, keepdims=True)
    slot_column = jnp.sum(jnp.where(diagonal, slots[...].astype(jnp.float32), 0.0), axis=1, keepdims=True)
    owner_row = jnp.sum(jnp.where(row == block, owner_column, 0.0), axis=0, keepdims=True)
    slot = jnp.sum(jnp.where(row == block, slot_column, 0.0), axis=0, keepdims=True)
    earlier = (owner_column == owner_row) & (row < block)
    owner = owner_row.astype(jnp.int32)
    rank = jnp.sum(jnp.where(earlier, 1.0, 0.0), axis=0, keepdims=True).astype(jnp.int32)
    position = rank * OWNERS + owner
    rows = lax.broadcasted_iota(jnp.int32, (128, 128), 0)
    placing[...] = (rows == position).astype(jnp.float32)
    tags[...] = jnp.broadcast_to(0.5 * (slot + 1.0), (16, 128))


def pick(chosen, values, contract):
    chosen = chosen.astype(jnp.bfloat16)
    total = None
    for _ in range(3):
        part = values.astype(jnp.bfloat16)
        values = values - part.astype(jnp.float32)
        product = lax.dot_general(chosen, part, (contract, ((), ())), preferred_element_type=jnp.float32)
        total = product if total is None else total + product
    return total


def wale(doubled):
    (g00, g01, g02), (g10, g11, g12), (g20, g21, g22) = doubled
    s01, s02, s12 = g01 + g10, g02 + g20, g12 + g21
    q0, q1, q2 = g00 * g00, g11 * g11, g22 * g22
    strain = 0.25 * ((q0 + q1 + q2) + 0.5 * (s01 * s01 + s02 * s02 + s12 * s12))
    p01, p02, p12 = g01 * g10, g02 * g20, g12 * g21
    d0, d1, d2 = q0 + (p01 + p02), q1 + (p01 + p12), q2 + (p02 + p12)
    third = (d0 + d1 + d2) * (1.0 / 3.0)
    d0, d1, d2 = d0 - third, d1 - third, d2 - third
    d01 = (g00 + g11) * s01 + (g02 * g21 + g12 * g20)
    d02 = (g00 + g22) * s02 + (g01 * g12 + g21 * g10)
    d12 = (g11 + g22) * s12 + (g10 * g02 + g20 * g01)
    deviator = 0.0625 * ((d0 * d0 + d1 * d1 + d2 * d2) + 0.5 * (d01 * d01 + d02 * d02 + d12 * d12))
    root = jnp.sqrt(deviator)
    eddy = (WALE_COEFF * WALE_COEFF) * deviator * root / (
        strain * strain * jnp.sqrt(strain) + deviator * jnp.sqrt(root) + WALE_FLOOR
    )
    return 0.5 + 3.0 * (BASE_VISCOSITY + eddy)


def collide(momentum, speed, stress, relaxation):
    retained = 1.0 - 1.0 / relaxation
    post = []
    for column, (one, two) in enumerate(((0, 0), (1, 1), (2, 2), (0, 1), (0, 2), (1, 2))):
        balance = momentum[one] * speed[two]
        post.append(balance + retained * (stress[column] - balance))
    return post


def leaving(density, momentum, post):
    t36 = density * (1.0 / 36.0) - (post[0] + post[1] + post[2]) * (1.0 / 24.0)
    az, ay, ax = (0.125 * post[k] for k in range(3))
    rzy, rzx, ryx = (0.25 * post[k] for k in range(3, 6))
    nz, ny, nx = ((1.0 / 12.0) * momentum[k] for k in range(3))
    bz, by, bx = t36 + az, t36 + ay, t36 + ax

    def edges(base, cross, one, two):
        plus, minus = base + cross, base - cross
        both, apart = one + two, one - two
        return plus + both, plus - both, minus + apart, minus - apart

    def up(value):
        return roll(value, 1, 0)

    def down(value):
        return roll(value, -1, 0)

    zpp, zmm, zpm, zmp = edges(bz + ay, rzy, nz, ny)
    y_zp = (up(zpp), down(zpm))
    y_zm = (up(zmp), down(zmm))
    xpp, xmm, xpm, xmp = edges(bz + ax, rzx, nz, nx)
    ypp, ymm, ypm, ymp = edges(by + ax, ryx, ny, nx)
    y_plus, y_minus = up(2.0 * (by + ny)), down(2.0 * (by - ny))
    ypp, ymp = up(ypp), down(ymp)
    ypm, ymm = up(ypm), down(ymm)
    x_plus, x_minus = 2.0 * (bx + nx), 2.0 * (bx - nx)
    syy_plus, syy_minus = ypp + ymp, ypm + ymm
    right = (x_plus + syy_plus, ypp - ymp, syy_plus, xpp, xmp)
    left = (x_minus + syy_minus, ypm - ymm, syy_minus, xpm, xmm)
    stay = (12.0 * t36, y_plus, y_minus, 2.0 * (bz + nz), y_zp, 2.0 * (bz - nz), y_zm)
    return stay, right, left


def plane_sums(stay, right, left):
    rest, y_plus, y_minus, z_plus, y_zp, z_minus, y_zm = stay
    syy = y_plus + y_minus
    sxx = right[0] + left[0]
    sums = [
        (rest + syy) + sxx,
        (y_plus - y_minus) + (right[1] + left[1]),
        right[0] - left[0],
        syy + (right[2] + left[2]),
        sxx,
        right[1] - left[1],
    ]
    for face, (one, two), plus, minus in ((z_plus, y_zp, right[3], left[3]), (z_minus, y_zm, right[4], left[4])):
        yy, xx = one + two, plus + minus
        sums += [face + (yy + xx), one - two, plus - minus, yy, xx]
    return sums


def gather_state(here, below, above, fluid):
    density = here[0] + (below[0] + above[0])
    third = density * (1.0 / 3.0)
    momentum = [
        fluid * (below[0] - above[0]),
        fluid * (here[1] + (below[1] + above[1])),
        fluid * (here[2] + (below[2] + above[2])),
    ]
    stress = [
        fluid * ((below[0] + above[0]) - third),
        fluid * ((here[3] + (below[3] + above[3])) - third),
        fluid * ((here[4] + (below[4] + above[4])) - third),
        fluid * (below[1] - above[1]),
        fluid * (below[2] - above[2]),
        fluid * here[5],
    ]
    return density, momentum, stress, third


PAIRS = ((0, 0), (1, 1), (2, 2), (0, 1), (0, 2), (1, 2))


def first_state(ref, where):
    density = ref[(0,) + where]
    speed = [ref[(1 + k,) + where] for k in range(3)]
    momentum = [density * speed[k] for k in range(3)]
    stress = [momentum[one] * speed[two] for one, two in PAIRS]
    return density, speed, momentum, stress


def row_differences(speed):
    return [roll(value, -1, 0) - roll(value, 1, 0) for value in speed]


def lane_differences(speed):
    return [roll(value, -1, 1) - roll(value, 1, 1) for value in speed]


def step_one(window, state, sums):
    for plane in range(1, 15):
        density, speed, momentum, stress = first_state(window, (plane,))
        dz = [window[1 + k, plane + 1] - window[1 + k, plane - 1] for k in range(3)]
        dy = row_differences(speed)
        dx = lane_differences(speed)
        relaxation = wale([[dz[k], dy[k], dx[k]] for k in range(3)])
        stay, right, left = leaving(density, momentum, collide(momentum, speed, stress, relaxation))
        right = [roll(value, 1, 1) for value in right]
        left = [roll(value, -1, 1) for value in left]
        for k, value in enumerate(plane_sums(stay, right, left)):
            sums[k, plane] = value
    for plane in range(2, 14):
        density, momentum, stress, _ = gather_state(
            [sums[k, plane] for k in range(6)],
            [sums[6 + k, plane - 1] for k in range(5)],
            [sums[11 + k, plane + 1] for k in range(5)],
            window[4, plane],
        )
        for k, value in enumerate([density] + momentum + stress):
            state[k, plane - 2] = value


def step_two(
    window, state_one, faces, got_far, got_near, placing, tags, moments, relaxation_out, outgoing,
    state, sums, strip, strip_sums, edge, pooled,
):
    even_x = is_even("gx")
    lane = lax.broadcasted_iota(jnp.int32, (16, 128), 1)
    first_lane, last_lane = lane == 0, lane == 127
    first_two, last_two = lane < 2, lane >= 126
    quarter = lax.broadcasted_iota(jnp.int32, (8, 128), 1) % 16 // 4

    for field in range(5):
        from_right = jnp.where(even_x, got_near[field], got_far[field])
        from_left = jnp.where(even_x, got_far[field], got_near[field])
        for half in range(2):
            for part in range(2):
                own = faces[field, part]
                turn = 8 * half + 4 * part
                cells = jnp.where(quarter == 0, roll(own, -8 * half, 1), roll(own, 8 - 8 * half, 1))
                cells = jnp.where(quarter == 1, roll(from_right, 4 - turn, 1), cells)
                strip[field, half, 8 * part : 8 * part + 8] = jnp.where(
                    quarter == 2, roll(from_left, 8 - turn, 1), cells
                )

    def strip_above(ref, number, half):
        return ref[number, 1] if half == 0 else roll(ref[number, 0], -16, 1)

    def strip_below(ref, number, half):
        return ref[number, 0] if half == 1 else roll(ref[number, 1], 16, 1)

    def strip_pass(step, half):
        if step == 0:
            density, speed, momentum, stress = first_state(strip, (half,))
        else:
            density = strip[0, half]
            speed = [strip[1 + k, half] for k in range(3)]
            momentum = [strip[5 + k, half] for k in range(3)]
            stress = [strip[8 + k, half] for k in range(6)]
        dz = [strip_above(strip, 1 + k, half) - strip_below(strip, 1 + k, half) for k in range(3)]
        dy = row_differences(speed)
        dx = lane_differences(speed)
        relaxation = wale([[dz[k], dy[k], dx[k]] for k in range(3)])
        return leaving(density, momentum, collide(momentum, speed, stress, relaxation))

    for half in range(2):
        stay, right, left = strip_pass(0, half)
        right = [roll(value, 1, 1) for value in right]
        left = [roll(value, -1, 1) for value in left]
        for k, value in enumerate(plane_sums(stay, right, left)):
            strip_sums[k, half] = value
    for half in range(2):
        density, momentum, stress, _ = gather_state(
            [strip_sums[k, half] for k in range(6)],
            [strip_below(strip_sums, 6 + k, half) for k in range(5)],
            [strip_above(strip_sums, 11 + k, half) for k in range(5)],
            strip[4, half],
        )
        inverse = 1.0 / density
        strip[0, half] = density
        for k in range(3):
            strip[1 + k, half] = momentum[k] * inverse
            strip[5 + k, half] = momentum[k]
        for k in range(6):
            strip[8 + k, half] = stress[k]

    for plane in range(2, 14):
        half, turn = plane % 2, plane // 2 * 16
        members = []
        for k, number in enumerate((0, 5, 6, 7, 8, 9, 10, 11, 12, 13)):
            value = jnp.where(first_two, roll(strip[number, half], -12 - turn, 1), state_one[k, plane - 2])
            members.append(jnp.where(last_two, roll(strip[number, half], 124 - turn, 1), value))
        inverse = 1.0 / members[0]
        for k in range(3):
            members.append(members[1 + k] * inverse)
        for k in range(13):
            state[k, plane] = members[k]

    for half in range(2):
        _, right, left = strip_pass(1, half)
        for k in range(5):
            edge[k, half] = right[k]
            edge[5 + k, half] = left[k]

    for plane in range(3, 13):
        half, turn = plane % 2, plane // 2 * 16

        def from_left_lane(value, ref, number):
            return jnp.where(first_lane, roll(ref[number, half], 117 - turn, 1), roll(value, 1, 1))

        def from_right_lane(value, ref, number):
            return jnp.where(last_lane, roll(ref[number, half], 123 - turn, 1), roll(value, -1, 1))

        density = state[0, plane]
        momentum = [state[1 + k, plane] for k in range(3)]
        stress = [state[4 + k, plane] for k in range(6)]
        speed = [state[10 + k, plane] for k in range(3)]
        dz = [state[10 + k, plane + 1] - state[10 + k, plane - 1] for k in range(3)]
        dy = row_differences(speed)
        dx = [
            from_right_lane(speed[k], strip, 1 + k) - from_left_lane(speed[k], strip, 1 + k)
            for k in range(3)
        ]
        relaxation = wale([[dz[k], dy[k], dx[k]] for k in range(3)])
        stay, right, left = leaving(density, momentum, collide(momentum, speed, stress, relaxation))
        right = [from_left_lane(value, edge, k) for k, value in enumerate(right)]
        left = [from_right_lane(value, edge, 5 + k) for k, value in enumerate(left)]
        for k, value in enumerate(plane_sums(stay, right, left)):
            sums[k, plane] = value[0:8]
        if 4 <= plane < 12:
            relaxation_out[plane - 4] = relaxation[0:8]

    for pair in range(4):
        total = None
        for low in (2 * pair, 2 * pair + 1):
            plane = low + 4
            density, momentum, stress, third = gather_state(
                [sums[k, plane] for k in range(6)],
                [sums[6 + k, plane - 1] for k in range(5)],
                [sums[11 + k, plane + 1] for k in range(5)],
                window[4, plane, 0:8],
            )
            members = [density] + momentum + [stress[k] + third for k in range(3)] + stress[3:]
            for k in range(10):
                moments[k, low] = members[k]
            total = members if total is None else [one + two for one, two in zip(total, members)]
        for k in range(10):
            pooled[k * 32 + pair * 8 : k * 32 + pair * 8 + 8, :] = total[k]

    blocks = 0.125 * (pooled[pl.ds(0, 160, stride=2), :] + pooled[pl.ds(1, 160, stride=2), :])
    payload = jnp.concatenate(
        [blocks, jnp.zeros((32, 128), jnp.float32), tags[...], jnp.zeros((48, 128), jnp.float32)], axis=0
    )
    placed = pick(placing[...], payload, ((1,), (1,)))
    outgoing[:, 0:128] = placed[0:OWNERS, 0:128]
    outgoing[:, 128:256] = placed[0:OWNERS, 128:256] + roll(placed[OWNERS:, 128:256], 32, 1)
    outgoing[:, 256:384] = placed[OWNERS:, 0:128]


def sum_slots(arrived, coarse):
    slot = lax.broadcasted_iota(jnp.int32, (OWNERS, 128), 1).astype(jnp.float32)
    one = (arrived[:, 192:193] == slot + 1.0).astype(jnp.float32)
    two = (arrived[:, 224:225] == slot + 1.0).astype(jnp.float32)
    ones = pick(one, arrived[:, 0:256], ((0,), (0,)))[0:SLOTS]
    twos = pick(two, arrived[:, 128:384], ((0,), (0,)))[0:SLOTS]
    coarse[:, 0:128] = ones[:, 0:128] + twos[:, 128:256]
    coarse[:, 128:160] = (ones[:, 128:256] + roll(twos[:, 0:128], -32, 1))[:, 0:32]


def call(kernel, outs, name, scratch=(), in_hbm=0, vmem=48):
    extra = {"in_specs": [pl.BlockSpec(memory_space=pltpu.HBM)] * in_hbm} if in_hbm else {}
    return pl.pallas_call(
        kernel, out_shape=outs, scratch_shapes=list(scratch), name=name,
        compiler_params=pltpu.CompilerParams(vmem_limit_bytes=vmem * 1024 * 1024), **extra
    )


def per_device(density, velocity, solid, owner_map, slot_map):
    placing, tags = call(
        place_blocks,
        (f32(128, 128), f32(16, 128)),
        "place_blocks",
        (pltpu.VMEM((1, 64), jnp.int32), pltpu.VMEM((1, 64), jnp.int32), pltpu.SemaphoreType.DMA((2,))),
        2,
    )(owner_map.reshape(1, 64), slot_map.reshape(1, 64))
    scalars = jnp.concatenate([density[None], 1.0 - solid[None].astype(jnp.float32)])
    near, far = call(pack_vertical, (f32(5, 4, 8, 128),) * 2, "pack_vertical")(scalars, velocity)
    near, far = swap(near, far, "gz")
    planes, high, low = call(
        pack_spanwise, (f32(5, 16, 8, 128), f32(5, 8, 8, 128), f32(5, 8, 8, 128)), "pack_spanwise"
    )(scalars, velocity, far, near)
    below, above = ring(high, low, "gy")
    window, faces, near, far = call(
        pack_streamwise,
        (f32(5, 16, 16, 128), f32(5, 2, 8, 128), f32(5, 8, 128), f32(5, 8, 128)),
        "pack_streamwise",
    )(planes, below, above)
    near, far = swap(near, far, "gx")
    state = call(
        step_one, f32(10, 12, 16, 128), "step_one", (pltpu.VMEM((16, 16, 16, 128), jnp.float32),)
    )(window)
    moments, relaxation, outgoing = call(
        step_two,
        (f32(10, 8, 8, 128), f32(8, 8, 128), f32(OWNERS, 384)),
        "step_two",
        (
            pltpu.VMEM((13, 16, 16, 128), jnp.float32),
            pltpu.VMEM((16, 16, 8, 128), jnp.float32),
            pltpu.VMEM((14, 2, 16, 128), jnp.float32),
            pltpu.VMEM((16, 2, 16, 128), jnp.float32),
            pltpu.VMEM((10, 2, 16, 128), jnp.float32),
            pltpu.VMEM((320, 128), jnp.float32),
        ),
    )(window, state, faces, far, near, placing, tags)
    arrived = lax.all_to_all(
        outgoing.reshape(OWNERS, 1, 384), ("gy", "gz"), split_axis=0, concat_axis=0, tiled=True
    )
    coarse = call(sum_slots, f32(SLOTS, 160), "sum_slots")(arrived.reshape(OWNERS, 384))
    return moments, relaxation, coarse.reshape(1, 1, 1, SLOTS, 160)


def solution(mesh):
    return jax.shard_map(
        per_device,
        mesh=mesh,
        in_specs=(
            P("gz", "gy", "gx"),
            P(None, "gz", "gy", "gx"),
            P("gz", "gy", "gx"),
            P("gx", "gy", "gz", None, None),
            P("gx", "gy", "gz", None, None),
        ),
        out_specs=(P(None, "gz", "gy", "gx"), P("gz", "gy", "gx"), P("gx", "gy", "gz", None, None)),
        check_vma=False,
    )
```

```python
import jax
import jax.numpy as jnp
from jax import lax
from jax.experimental import pallas as pl
from jax.experimental.pallas import tpu as pltpu
from jax.sharding import PartitionSpec as P

SLOTS = 16
OWNERS = 64
WALE_COEFF = 0.5
BASE_VISCOSITY = 0.01
WALE_FLOOR = 1e-10


def f32(*shape):
    return jax.ShapeDtypeStruct(shape, jnp.float32)


def roll(value, shift, axis):
    size = value.shape[axis]
    if isinstance(shift, int):
        shift = shift % size
        if shift == 0:
            return value
    return pltpu.roll(value, shift, axis)


def is_even(axis):
    return lax.rem(lax.axis_index(axis), 2) == 0


def ring(high, low, axis):
    count = lax.axis_size(axis)
    below = lax.ppermute(high, axis, [(i, (i + 1) % count) for i in range(count)])
    above = lax.ppermute(low, axis, [((i + 1) % count, i) for i in range(count)])
    return below, above


def vertical_rings(one, two):
    span_y, span_z = lax.axis_size("gy"), lax.axis_size("gz")
    places = [(y, z) for y in range(span_y) for z in range(span_z)]

    def pairs(sense):
        return [
            (y * span_z + z, y * span_z + (z + (sense if y % 2 == 0 else -sense)) % span_z) for y, z in places
        ]

    return lax.ppermute(one, ("gy", "gz"), pairs(1)), lax.ppermute(two, ("gy", "gz"), pairs(-1))


def streamwise_swaps(one, two):
    span_x, span_y = lax.axis_size("gx"), lax.axis_size("gy")
    places = [(x, y) for x in range(span_x) for y in range(span_y)]

    def pairs(shift):
        return [
            (x * span_y + y, (x + (1 if (x + y + shift) % 2 == 0 else -1)) % span_x * span_y + y)
            for x, y in places
        ]

    return lax.ppermute(one, ("gx", "gy"), pairs(0)), lax.ppermute(two, ("gx", "gy"), pairs(1))


def pack_vertical(scalars, velocity, one, two):
    even = is_even("gy")
    for out, upper in ((one, even), (two, jnp.logical_not(even))):
        planes = pl.ds(jnp.where(upper, 4, 0), 4)
        fluid = scalars[1, planes]
        out[0] = scalars[0, planes]
        for axis in range(3):
            out[1 + axis] = velocity[axis, planes] * fluid
        out[4] = fluid


def pack_spanwise(scalars, velocity, got_one, got_two, placing, planes, high, low):
    del placing
    even = is_even("gy")
    front = lax.broadcasted_iota(jnp.int32, (8, 128), 0) < 4
    fluid = scalars[1]
    for field in range(5):
        inner = scalars[0] if field == 0 else fluid if field == 4 else velocity[field - 1] * fluid
        planes[field, 4:12] = inner
        planes[field, 12:16] = jnp.where(even, got_two[field], got_one[field])
        planes[field, 0:4] = jnp.where(even, got_one[field], got_two[field])
        for pair in range(8):
            one = planes[field, 2 * pair]
            two = planes[field, 2 * pair + 1]
            high[field, pair] = jnp.where(front, roll(one, 4, 0), two)
            low[field, pair] = jnp.where(front, one, roll(two, 4, 0))


def pack_streamwise(planes, got_below, got_above, window, faces, one, two):
    rightward = is_even("gx") == is_even("gy")
    front = lax.broadcasted_iota(jnp.int32, (8, 128), 0) < 4
    lane = lax.broadcasted_iota(jnp.int32, (8, 128), 1)
    for field in range(5):
        own = [jnp.zeros((8, 128), jnp.float32) for _ in range(2)]
        for pair in range(8):
            above, below = got_above[field, pair], got_below[field, pair]
            outer = (jnp.where(front, above, roll(below, 4, 0)), jnp.where(front, roll(above, 4, 0), below))
            for side in range(2):
                plane = 2 * pair + side
                inner = planes[field, plane]
                window[field, plane, 0:8] = inner
                window[field, plane, 8:16] = outer[side]
                here = lane // 8 == plane
                own[0] = jnp.where(here, roll(inner, 8 * plane + 4, 1), own[0])
                own[1] = jnp.where(here, roll(outer[side], 8 * plane + 4, 1), own[1])
        faces[field, 0] = own[0]
        faces[field, 1] = own[1]
        even_spot = lane % 8 < 4
        to_right = jnp.where(even_spot, own[0], roll(own[1], 4, 1))
        to_left = jnp.where(even_spot, roll(own[0], -4, 1), own[1])
        one[field] = jnp.where(rightward, to_right, to_left)
        two[field] = jnp.where(rightward, to_left, to_right)


def place_blocks(owners_in, slots_in, placing, tags, owners, slots, arrived):
    copies = [
        pltpu.make_async_copy(source, target, arrived.at[number])
        for number, (source, target) in enumerate(((owners_in, owners), (slots_in, slots)))
    ]
    for copy in copies:
        copy.start()
    for copy in copies:
        copy.wait()
    row = lax.broadcasted_iota(jnp.int32, (64, 128), 0)
    block = lax.broadcasted_iota(jnp.int32, (64, 128), 1) // 2
    diagonal = lax.broadcasted_iota(jnp.int32, (64, 64), 0) == lax.broadcasted_iota(jnp.int32, (64, 64), 1)
    owner_column = jnp.sum(jnp.where(diagonal, owners[...].astype(jnp.float32), 0.0), axis=1, keepdims=True)
    slot_column = jnp.sum(jnp.where(diagonal, slots[...].astype(jnp.float32), 0.0), axis=1, keepdims=True)
    owner_row = jnp.sum(jnp.where(row == block, owner_column, 0.0), axis=0, keepdims=True)
    slot = jnp.sum(jnp.where(row == block, slot_column, 0.0), axis=0, keepdims=True)
    earlier = (owner_column == owner_row) & (row < block)
    owner = owner_row.astype(jnp.int32)
    rank = jnp.sum(jnp.where(earlier, 1.0, 0.0), axis=0, keepdims=True).astype(jnp.int32)
    position = rank * OWNERS + owner
    rows = lax.broadcasted_iota(jnp.int32, (128, 128), 0)
    placing[...] = (rows == position).astype(jnp.float32)
    tags[...] = jnp.broadcast_to(0.5 * (slot + 1.0), (16, 128))


def pick(chosen, values, contract):
    chosen = chosen.astype(jnp.bfloat16)
    total = None
    for _ in range(3):
        part = values.astype(jnp.bfloat16)
        values = values - part.astype(jnp.float32)
        product = lax.dot_general(chosen, part, (contract, ((), ())), preferred_element_type=jnp.float32)
        total = product if total is None else total + product
    return total


def wale(doubled):
    (g00, g01, g02), (g10, g11, g12), (g20, g21, g22) = doubled
    s01, s02, s12 = g01 + g10, g02 + g20, g12 + g21
    q0, q1, q2 = g00 * g00, g11 * g11, g22 * g22
    strain = 0.25 * ((q0 + q1 + q2) + 0.5 * (s01 * s01 + s02 * s02 + s12 * s12))
    p01, p02, p12 = g01 * g10, g02 * g20, g12 * g21
    d0, d1, d2 = q0 + (p01 + p02), q1 + (p01 + p12), q2 + (p02 + p12)
    third = (d0 + d1 + d2) * (1.0 / 3.0)
    d0, d1, d2 = d0 - third, d1 - third, d2 - third
    d01 = (g00 + g11) * s01 + (g02 * g21 + g12 * g20)
    d02 = (g00 + g22) * s02 + (g01 * g12 + g21 * g10)
    d12 = (g11 + g22) * s12 + (g10 * g02 + g20 * g01)
    deviator = 0.0625 * ((d0 * d0 + d1 * d1 + d2 * d2) + 0.5 * (d01 * d01 + d02 * d02 + d12 * d12))
    root = jnp.sqrt(deviator)
    eddy = (WALE_COEFF * WALE_COEFF) * deviator * root / (
        strain * strain * jnp.sqrt(strain) + deviator * jnp.sqrt(root) + WALE_FLOOR
    )
    return 0.5 + 3.0 * (BASE_VISCOSITY + eddy)


def collide(momentum, speed, stress, relaxation):
    retained = 1.0 - 1.0 / relaxation
    post = []
    for column, (one, two) in enumerate(((0, 0), (1, 1), (2, 2), (0, 1), (0, 2), (1, 2))):
        balance = momentum[one] * speed[two]
        post.append(balance + retained * (stress[column] - balance))
    return post


def leaving(density, momentum, post):
    t36 = density * (1.0 / 36.0) - (post[0] + post[1] + post[2]) * (1.0 / 24.0)
    az, ay, ax = (0.125 * post[k] for k in range(3))
    rzy, rzx, ryx = (0.25 * post[k] for k in range(3, 6))
    nz, ny, nx = ((1.0 / 12.0) * momentum[k] for k in range(3))
    bz, by, bx = t36 + az, t36 + ay, t36 + ax

    def edges(base, cross, one, two):
        plus, minus = base + cross, base - cross
        both, apart = one + two, one - two
        return plus + both, plus - both, minus + apart, minus - apart

    def up(value):
        return roll(value, 1, 0)

    def down(value):
        return roll(value, -1, 0)

    zpp, zmm, zpm, zmp = edges(bz + ay, rzy, nz, ny)
    y_zp = (up(zpp), down(zpm))
    y_zm = (up(zmp), down(zmm))
    xpp, xmm, xpm, xmp = edges(bz + ax, rzx, nz, nx)
    ypp, ymm, ypm, ymp = edges(by + ax, ryx, ny, nx)
    y_plus, y_minus = up(2.0 * (by + ny)), down(2.0 * (by - ny))
    ypp, ymp = up(ypp), down(ymp)
    ypm, ymm = up(ypm), down(ymm)
    x_plus, x_minus = 2.0 * (bx + nx), 2.0 * (bx - nx)
    syy_plus, syy_minus = ypp + ymp, ypm + ymm
    right = (x_plus + syy_plus, ypp - ymp, syy_plus, xpp, xmp)
    left = (x_minus + syy_minus, ypm - ymm, syy_minus, xpm, xmm)
    stay = (12.0 * t36, y_plus, y_minus, 2.0 * (bz + nz), y_zp, 2.0 * (bz - nz), y_zm)
    return stay, right, left


def plane_sums(stay, right, left):
    rest, y_plus, y_minus, z_plus, y_zp, z_minus, y_zm = stay
    syy = y_plus + y_minus
    sxx = right[0] + left[0]
    sums = [
        (rest + syy) + sxx,
        (y_plus - y_minus) + (right[1] + left[1]),
        right[0] - left[0],
        syy + (right[2] + left[2]),
        sxx,
        right[1] - left[1],
    ]
    for face, (one, two), plus, minus in ((z_plus, y_zp, right[3], left[3]), (z_minus, y_zm, right[4], left[4])):
        yy, xx = one + two, plus + minus
        sums += [face + (yy + xx), one - two, plus - minus, yy, xx]
    return sums


def gather_state(here, below, above, fluid):
    density = here[0] + (below[0] + above[0])
    third = density * (1.0 / 3.0)
    momentum = [
        fluid * (below[0] - above[0]),
        fluid * (here[1] + (below[1] + above[1])),
        fluid * (here[2] + (below[2] + above[2])),
    ]
    stress = [
        fluid * ((below[0] + above[0]) - third),
        fluid * ((here[3] + (below[3] + above[3])) - third),
        fluid * ((here[4] + (below[4] + above[4])) - third),
        fluid * (below[1] - above[1]),
        fluid * (below[2] - above[2]),
        fluid * here[5],
    ]
    return density, momentum, stress, third


PAIRS = ((0, 0), (1, 1), (2, 2), (0, 1), (0, 2), (1, 2))


def first_state(ref, where):
    density = ref[(0,) + where]
    speed = [ref[(1 + k,) + where] for k in range(3)]
    momentum = [density * speed[k] for k in range(3)]
    stress = [momentum[one] * speed[two] for one, two in PAIRS]
    return density, speed, momentum, stress


def row_differences(speed):
    return [roll(value, -1, 0) - roll(value, 1, 0) for value in speed]


def lane_differences(speed):
    return [roll(value, -1, 1) - roll(value, 1, 1) for value in speed]


def step_one(window, state, sums):
    for plane in range(1, 15):
        density, speed, momentum, stress = first_state(window, (plane,))
        dz = [window[1 + k, plane + 1] - window[1 + k, plane - 1] for k in range(3)]
        dy = row_differences(speed)
        dx = lane_differences(speed)
        relaxation = wale([[dz[k], dy[k], dx[k]] for k in range(3)])
        stay, right, left = leaving(density, momentum, collide(momentum, speed, stress, relaxation))
        right = [roll(value, 1, 1) for value in right]
        left = [roll(value, -1, 1) for value in left]
        for k, value in enumerate(plane_sums(stay, right, left)):
            sums[k, plane] = value
    for plane in range(2, 14):
        density, momentum, stress, _ = gather_state(
            [sums[k, plane] for k in range(6)],
            [sums[6 + k, plane - 1] for k in range(5)],
            [sums[11 + k, plane + 1] for k in range(5)],
            window[4, plane],
        )
        for k, value in enumerate([density] + momentum + stress):
            state[k, plane - 2] = value


def step_two(
    window, state_one, faces, got_one, got_two, placing, tags, moments_out, relaxation_out, outgoing,
    state, sums, strip, strip_sums, edge, pooled, moments, relaxations, left_sems,
):
    rightward = is_even("gx") == is_even("gy")
    lane = lax.broadcasted_iota(jnp.int32, (16, 128), 1)
    first_lane, last_lane = lane == 0, lane == 127
    first_two, last_two = lane < 2, lane >= 126
    quarter = lax.broadcasted_iota(jnp.int32, (8, 128), 1) % 16 // 4

    for field in range(5):
        from_right = jnp.where(rightward, got_one[field], got_two[field])
        from_left = jnp.where(rightward, got_two[field], got_one[field])
        for half in range(2):
            for part in range(2):
                own = faces[field, part]
                turn = 8 * half + 4 * part
                cells = jnp.where(quarter == 0, roll(own, -8 * half, 1), roll(own, 8 - 8 * half, 1))
                cells = jnp.where(quarter == 1, roll(from_right, 4 - turn, 1), cells)
                strip[field, half, 8 * part : 8 * part + 8] = jnp.where(
                    quarter == 2, roll(from_left, 8 - turn, 1), cells
                )

    def strip_above(ref, number, half):
        return ref[number, 1] if half == 0 else roll(ref[number, 0], -16, 1)

    def strip_below(ref, number, half):
        return ref[number, 0] if half == 1 else roll(ref[number, 1], 16, 1)

    def strip_pass(step, half):
        if step == 0:
            density, speed, momentum, stress = first_state(strip, (half,))
        else:
            density = strip[0, half]
            speed = [strip[1 + k, half] for k in range(3)]
            momentum = [strip[5 + k, half] for k in range(3)]
            stress = [strip[8 + k, half] for k in range(6)]
        dz = [strip_above(strip, 1 + k, half) - strip_below(strip, 1 + k, half) for k in range(3)]
        dy = row_differences(speed)
        dx = lane_differences(speed)
        relaxation = wale([[dz[k], dy[k], dx[k]] for k in range(3)])
        return leaving(density, momentum, collide(momentum, speed, stress, relaxation))

    for half in range(2):
        stay, right, left = strip_pass(0, half)
        right = [roll(value, 1, 1) for value in right]
        left = [roll(value, -1, 1) for value in left]
        for k, value in enumerate(plane_sums(stay, right, left)):
            strip_sums[k, half] = value
    for half in range(2):
        density, momentum, stress, _ = gather_state(
            [strip_sums[k, half] for k in range(6)],
            [strip_below(strip_sums, 6 + k, half) for k in range(5)],
            [strip_above(strip_sums, 11 + k, half) for k in range(5)],
            strip[4, half],
        )
        inverse = 1.0 / density
        strip[0, half] = density
        for k in range(3):
            strip[1 + k, half] = momentum[k] * inverse
            strip[5 + k, half] = momentum[k]
        for k in range(6):
            strip[8 + k, half] = stress[k]

    for plane in range(2, 14):
        half, turn = plane % 2, plane // 2 * 16
        members = []
        for k, number in enumerate((0, 5, 6, 7, 8, 9, 10, 11, 12, 13)):
            value = jnp.where(first_two, roll(strip[number, half], -12 - turn, 1), state_one[k, plane - 2])
            members.append(jnp.where(last_two, roll(strip[number, half], 124 - turn, 1), value))
        inverse = 1.0 / members[0]
        for k in range(3):
            members.append(members[1 + k] * inverse)
        for k in range(13):
            state[k, plane] = members[k]

    for half in range(2):
        _, right, left = strip_pass(1, half)
        for k in range(5):
            edge[k, half] = right[k]
            edge[5 + k, half] = left[k]

    for plane in range(3, 13):
        half, turn = plane % 2, plane // 2 * 16

        def from_left_lane(value, ref, number):
            return jnp.where(first_lane, roll(ref[number, half], 117 - turn, 1), roll(value, 1, 1))

        def from_right_lane(value, ref, number):
            return jnp.where(last_lane, roll(ref[number, half], 123 - turn, 1), roll(value, -1, 1))

        density = state[0, plane]
        momentum = [state[1 + k, plane] for k in range(3)]
        stress = [state[4 + k, plane] for k in range(6)]
        speed = [state[10 + k, plane] for k in range(3)]
        dz = [state[10 + k, plane + 1] - state[10 + k, plane - 1] for k in range(3)]
        dy = row_differences(speed)
        dx = [
            from_right_lane(speed[k], strip, 1 + k) - from_left_lane(speed[k], strip, 1 + k)
            for k in range(3)
        ]
        relaxation = wale([[dz[k], dy[k], dx[k]] for k in range(3)])
        stay, right, left = leaving(density, momentum, collide(momentum, speed, stress, relaxation))
        right = [from_left_lane(value, edge, k) for k, value in enumerate(right)]
        left = [from_right_lane(value, edge, 5 + k) for k, value in enumerate(left)]
        for k, value in enumerate(plane_sums(stay, right, left)):
            sums[k, plane] = value[0:8]
        if 4 <= plane < 12:
            relaxations[plane - 4] = relaxation[0:8]
    copies = [pltpu.make_async_copy(relaxations, relaxation_out, left_sems.at[4])]
    copies[0].start()

    for pair in range(4):
        total = None
        for low in (2 * pair, 2 * pair + 1):
            plane = low + 4
            density, momentum, stress, third = gather_state(
                [sums[k, plane] for k in range(6)],
                [sums[6 + k, plane - 1] for k in range(5)],
                [sums[11 + k, plane + 1] for k in range(5)],
                window[4, plane, 0:8],
            )
            members = [density] + momentum + [stress[k] + third for k in range(3)] + stress[3:]
            for k in range(10):
                moments[k, low] = members[k]
            total = members if total is None else [one + two for one, two in zip(total, members)]
        for k in range(10):
            pooled[k * 32 + pair * 8 : k * 32 + pair * 8 + 8, :] = total[k]
        done = pl.ds(2 * pair, 2)
        copies.append(pltpu.make_async_copy(moments.at[:, done], moments_out.at[:, done], left_sems.at[pair]))
        copies[-1].start()

    blocks = 0.125 * (pooled[pl.ds(0, 160, stride=2), :] + pooled[pl.ds(1, 160, stride=2), :])
    payload = jnp.concatenate(
        [blocks, jnp.zeros((32, 128), jnp.float32), tags[...], jnp.zeros((48, 128), jnp.float32)], axis=0
    )
    placed = pick(placing[...], payload, ((1,), (1,)))
    outgoing[:, 0:128] = placed[0:OWNERS, 0:128]
    outgoing[:, 128:256] = placed[0:OWNERS, 128:256] + roll(placed[OWNERS:, 128:256], 32, 1)
    outgoing[:, 256:384] = placed[OWNERS:, 0:128]
    for copy in copies:
        copy.wait()


def sum_slots(arrived, coarse):
    slot = lax.broadcasted_iota(jnp.int32, (2 * OWNERS, SLOTS), 1).astype(jnp.float32)
    shared = arrived[:, 128:256]
    tag = jnp.concatenate([shared[:, 64:65], shared[:, 96:97]], axis=0)
    blocks = jnp.concatenate(
        [
            jnp.concatenate([arrived[:, 0:128], arrived[:, 256:384]], axis=0),
            jnp.concatenate([shared, roll(shared, -32, 1)], axis=0),
        ],
        axis=1,
    )
    total = pick((tag == slot + 1.0).astype(jnp.float32), blocks, ((0,), (0,)))
    coarse[...] = total[:, 0:160]


def call(kernel, outs, name, scratch=(), in_hbm=0, out_spaces=None):
    extra = {"in_specs": [pl.BlockSpec(memory_space=pltpu.HBM)] * in_hbm} if in_hbm else {}
    if out_spaces:
        extra["out_specs"] = tuple(pl.BlockSpec(memory_space=space) for space in out_spaces)
    return pl.pallas_call(
        kernel,
        out_shape=outs,
        scratch_shapes=list(scratch),
        name=name,
        compiler_params=pltpu.CompilerParams(vmem_limit_bytes=48 * 1024 * 1024),
        **extra,
    )


def per_device(density, velocity, solid, owner_map, slot_map):
    placing, tags = call(
        place_blocks,
        (f32(128, 128), f32(16, 128)),
        "place_blocks",
        (pltpu.VMEM((1, 64), jnp.int32), pltpu.VMEM((1, 64), jnp.int32), pltpu.SemaphoreType.DMA((2,))),
        2,
    )(owner_map.reshape(1, 64), slot_map.reshape(1, 64))
    scalars = jnp.concatenate([density[None], 1.0 - solid[None].astype(jnp.float32)])
    one, two = call(pack_vertical, (f32(5, 4, 8, 128),) * 2, "pack_vertical")(scalars, velocity)
    one, two = vertical_rings(one, two)
    planes, high, low = call(
        pack_spanwise, (f32(5, 16, 8, 128), f32(5, 8, 8, 128), f32(5, 8, 8, 128)), "pack_spanwise"
    )(scalars, velocity, one, two, placing)
    below, above = ring(high, low, "gy")
    window, faces, one, two = call(
        pack_streamwise,
        (f32(5, 16, 16, 128), f32(5, 2, 8, 128), f32(5, 8, 128), f32(5, 8, 128)),
        "pack_streamwise",
    )(planes, below, above)
    one, two = streamwise_swaps(one, two)
    state = call(
        step_one, f32(10, 12, 16, 128), "step_one", (pltpu.VMEM((16, 16, 16, 128), jnp.float32),)
    )(window)
    moments, relaxation, outgoing = call(
        step_two,
        (f32(10, 8, 8, 128), f32(8, 8, 128), f32(OWNERS, 384)),
        "step_two",
        (
            pltpu.VMEM((13, 16, 16, 128), jnp.float32),
            pltpu.VMEM((16, 16, 8, 128), jnp.float32),
            pltpu.VMEM((14, 2, 16, 128), jnp.float32),
            pltpu.VMEM((16, 2, 16, 128), jnp.float32),
            pltpu.VMEM((10, 2, 16, 128), jnp.float32),
            pltpu.VMEM((320, 128), jnp.float32),
            pltpu.VMEM((10, 8, 8, 128), jnp.float32),
            pltpu.VMEM((8, 8, 128), jnp.float32),
            pltpu.SemaphoreType.DMA((5,)),
        ),
        out_spaces=(pltpu.HBM, pltpu.HBM, pltpu.VMEM),
    )(window, state, faces, one, two, placing, tags)
    arrived = lax.all_to_all(
        outgoing.reshape(OWNERS, 1, 384), ("gy", "gz"), split_axis=0, concat_axis=0, tiled=True
    )
    coarse = call(sum_slots, f32(SLOTS, 160), "sum_slots")(arrived.reshape(OWNERS, 384))
    return moments, relaxation, coarse.reshape(1, 1, 1, SLOTS, 160)


def solution(mesh):
    return jax.shard_map(
        per_device,
        mesh=mesh,
        in_specs=(
            P("gz", "gy", "gx"),
            P(None, "gz", "gy", "gx"),
            P("gz", "gy", "gx"),
            P("gx", "gy", "gz", None, None),
            P("gx", "gy", "gz", None, None),
        ),
        out_specs=(P(None, "gz", "gy", "gx"), P("gz", "gy", "gx"), P("gx", "gy", "gz", None, None)),
        check_vma=False,
    )
```

```python
import jax
import jax.numpy as jnp
from jax import lax
from jax.experimental import pallas as pl
from jax.experimental.pallas import tpu as pltpu
from jax.sharding import PartitionSpec as P

SLOTS = 16
SPAN_Y = 8
SPAN_Z = 8
WALE_COEFF = 0.5
BASE_VISCOSITY = 0.01
WALE_FLOOR = 1e-10


def f32(*shape):
    return jax.ShapeDtypeStruct(shape, jnp.float32)


def roll(value, shift, axis):
    size = value.shape[axis]
    if isinstance(shift, int):
        shift = shift % size
        if shift == 0:
            return value
    return pltpu.roll(value, shift, axis)


def is_even(axis):
    return lax.rem(lax.axis_index(axis), 2) == 0


def ring(high, low, axis):
    count = lax.axis_size(axis)
    below = lax.ppermute(high, axis, [(i, (i + 1) % count) for i in range(count)])
    above = lax.ppermute(low, axis, [((i + 1) % count, i) for i in range(count)])
    return below, above


def swap(near, far, axis):
    count = lax.axis_size(axis)
    near_pairs = [(i, i ^ 1) for i in range(count)]
    far_pairs = [(i, (i + 1) % count if i % 2 else (i - 1) % count) for i in range(count)]
    far = lax.ppermute(far, axis, far_pairs)
    return lax.ppermute(near, axis, near_pairs), far


def pack_vertical(scalars, velocity, near, far):
    even = is_even("gz")
    for out, upper in ((near, even), (far, jnp.logical_not(even))):
        planes = pl.ds(jnp.where(upper, 4, 0), 4)
        fluid = scalars[1, planes]
        out[0] = scalars[0, planes]
        for axis in range(3):
            out[1 + axis] = velocity[axis, planes] * fluid
        out[4] = fluid


def pack_spanwise(scalars, velocity, got_far, got_near, placing, planes, high, low):
    del placing
    even = is_even("gz")
    front = lax.broadcasted_iota(jnp.int32, (8, 128), 0) < 4
    fluid = scalars[1]
    for field in range(5):
        inner = scalars[0] if field == 0 else fluid if field == 4 else velocity[field - 1] * fluid
        planes[field, 4:12] = inner
        planes[field, 12:16] = jnp.where(even, got_near[field], got_far[field])
        planes[field, 0:4] = jnp.where(even, got_far[field], got_near[field])
        for pair in range(8):
            one = planes[field, 2 * pair]
            two = planes[field, 2 * pair + 1]
            high[field, pair] = jnp.where(front, roll(one, 4, 0), two)
            low[field, pair] = jnp.where(front, one, roll(two, 4, 0))


def pack_streamwise(planes, got_below, got_above, window, faces, near, far):
    even_x = is_even("gx")
    front = lax.broadcasted_iota(jnp.int32, (8, 128), 0) < 4
    lane = lax.broadcasted_iota(jnp.int32, (8, 128), 1)
    for field in range(5):
        own = [jnp.zeros((8, 128), jnp.float32) for _ in range(2)]
        for pair in range(8):
            above, below = got_above[field, pair], got_below[field, pair]
            outer = (jnp.where(front, above, roll(below, 4, 0)), jnp.where(front, roll(above, 4, 0), below))
            for side in range(2):
                plane = 2 * pair + side
                inner = planes[field, plane]
                window[field, plane, 0:8] = inner
                window[field, plane, 8:16] = outer[side]
                here = lane // 8 == plane
                own[0] = jnp.where(here, roll(inner, 8 * plane + 4, 1), own[0])
                own[1] = jnp.where(here, roll(outer[side], 8 * plane + 4, 1), own[1])
        faces[field, 0] = own[0]
        faces[field, 1] = own[1]
        even_spot = lane % 8 < 4
        to_right = jnp.where(even_spot, own[0], roll(own[1], 4, 1))
        to_left = jnp.where(even_spot, roll(own[0], -4, 1), own[1])
        near[field] = jnp.where(even_x, to_right, to_left)
        far[field] = jnp.where(even_x, to_left, to_right)


def place_blocks(owners_in, slots_in, placing, tags, owners, slots, arrived):
    copies = [
        pltpu.make_async_copy(source, target, arrived.at[number])
        for number, (source, target) in enumerate(((owners_in, owners), (slots_in, slots)))
    ]
    for copy in copies:
        copy.start()
    for copy in copies:
        copy.wait()
    row = lax.broadcasted_iota(jnp.int32, (64, 128), 0)
    block = lax.broadcasted_iota(jnp.int32, (64, 128), 1) // 2
    diagonal = lax.broadcasted_iota(jnp.int32, (64, 64), 0) == lax.broadcasted_iota(jnp.int32, (64, 64), 1)
    owner_column = jnp.sum(jnp.where(diagonal, owners[...].astype(jnp.float32), 0.0), axis=1, keepdims=True)
    slot_column = jnp.sum(jnp.where(diagonal, slots[...].astype(jnp.float32), 0.0), axis=1, keepdims=True)
    owner_row = jnp.sum(jnp.where(row == block, owner_column, 0.0), axis=0, keepdims=True)
    slot = jnp.sum(jnp.where(row == block, slot_column, 0.0), axis=0, keepdims=True)
    earlier = (owner_column == owner_row) & (row < block)
    owner = owner_row.astype(jnp.int32)
    rank = jnp.sum(jnp.where(earlier, 1.0, 0.0), axis=0, keepdims=True).astype(jnp.int32)
    position = (lax.rem(owner, SPAN_Z) * SPAN_Y + lax.div(owner, SPAN_Z)) * 2 + rank
    rows = lax.broadcasted_iota(jnp.int32, (128, 128), 0)
    placing[...] = (rows == position).astype(jnp.float32)
    tags[...] = jnp.broadcast_to(0.5 * (slot + 1.0), (16, 128))


def pick(chosen, values, contract):
    chosen = chosen.astype(jnp.bfloat16)
    total = None
    for _ in range(3):
        part = values.astype(jnp.bfloat16)
        values = values - part.astype(jnp.float32)
        product = lax.dot_general(chosen, part, (contract, ((), ())), preferred_element_type=jnp.float32)
        total = product if total is None else total + product
    return total


def wale(doubled):
    (g00, g01, g02), (g10, g11, g12), (g20, g21, g22) = doubled
    s01, s02, s12 = g01 + g10, g02 + g20, g12 + g21
    q0, q1, q2 = g00 * g00, g11 * g11, g22 * g22
    strain = 0.25 * ((q0 + q1 + q2) + 0.5 * (s01 * s01 + s02 * s02 + s12 * s12))
    p01, p02, p12 = g01 * g10, g02 * g20, g12 * g21
    d0, d1, d2 = q0 + (p01 + p02), q1 + (p01 + p12), q2 + (p02 + p12)
    third = (d0 + d1 + d2) * (1.0 / 3.0)
    d0, d1, d2 = d0 - third, d1 - third, d2 - third
    d01 = (g00 + g11) * s01 + (g02 * g21 + g12 * g20)
    d02 = (g00 + g22) * s02 + (g01 * g12 + g21 * g10)
    d12 = (g11 + g22) * s12 + (g10 * g02 + g20 * g01)
    deviator = 0.0625 * ((d0 * d0 + d1 * d1 + d2 * d2) + 0.5 * (d01 * d01 + d02 * d02 + d12 * d12))
    root = jnp.sqrt(deviator)
    eddy = (WALE_COEFF * WALE_COEFF) * deviator * root / (
        strain * strain * jnp.sqrt(strain) + deviator * jnp.sqrt(root) + WALE_FLOOR
    )
    return 0.5 + 3.0 * (BASE_VISCOSITY + eddy)


def collide(momentum, speed, stress, relaxation):
    retained = 1.0 - 1.0 / relaxation
    post = []
    for column, (one, two) in enumerate(((0, 0), (1, 1), (2, 2), (0, 1), (0, 2), (1, 2))):
        balance = momentum[one] * speed[two]
        post.append(balance + retained * (stress[column] - balance))
    return post


def leaving(density, momentum, post):
    t36 = density * (1.0 / 36.0) - (post[0] + post[1] + post[2]) * (1.0 / 24.0)
    az, ay, ax = (0.125 * post[k] for k in range(3))
    rzy, rzx, ryx = (0.25 * post[k] for k in range(3, 6))
    nz, ny, nx = ((1.0 / 12.0) * momentum[k] for k in range(3))
    bz, by, bx = t36 + az, t36 + ay, t36 + ax

    def edges(base, cross, one, two):
        plus, minus = base + cross, base - cross
        both, apart = one + two, one - two
        return plus + both, plus - both, minus + apart, minus - apart

    def up(value):
        return roll(value, 1, 0)

    def down(value):
        return roll(value, -1, 0)

    zpp, zmm, zpm, zmp = edges(bz + ay, rzy, nz, ny)
    y_zp = (up(zpp), down(zpm))
    y_zm = (up(zmp), down(zmm))
    xpp, xmm, xpm, xmp = edges(bz + ax, rzx, nz, nx)
    ypp, ymm, ypm, ymp = edges(by + ax, ryx, ny, nx)
    y_plus, y_minus = up(2.0 * (by + ny)), down(2.0 * (by - ny))
    ypp, ymp = up(ypp), down(ymp)
    ypm, ymm = up(ypm), down(ymm)
    x_plus, x_minus = 2.0 * (bx + nx), 2.0 * (bx - nx)
    syy_plus, syy_minus = ypp + ymp, ypm + ymm
    right = (x_plus + syy_plus, ypp - ymp, syy_plus, xpp, xmp)
    left = (x_minus + syy_minus, ypm - ymm, syy_minus, xpm, xmm)
    stay = (12.0 * t36, y_plus, y_minus, 2.0 * (bz + nz), y_zp, 2.0 * (bz - nz), y_zm)
    return stay, right, left


def plane_sums(stay, right, left):
    rest, y_plus, y_minus, z_plus, y_zp, z_minus, y_zm = stay
    syy = y_plus + y_minus
    sxx = right[0] + left[0]
    sums = [
        (rest + syy) + sxx,
        (y_plus - y_minus) + (right[1] + left[1]),
        right[0] - left[0],
        syy + (right[2] + left[2]),
        sxx,
        right[1] - left[1],
    ]
    for face, (one, two), plus, minus in ((z_plus, y_zp, right[3], left[3]), (z_minus, y_zm, right[4], left[4])):
        yy, xx = one + two, plus + minus
        sums += [face + (yy + xx), one - two, plus - minus, yy, xx]
    return sums


def gather_state(here, below, above, fluid):
    density = here[0] + (below[0] + above[0])
    third = density * (1.0 / 3.0)
    momentum = [
        fluid * (below[0] - above[0]),
        fluid * (here[1] + (below[1] + above[1])),
        fluid * (here[2] + (below[2] + above[2])),
    ]
    stress = [
        fluid * ((below[0] + above[0]) - third),
        fluid * ((here[3] + (below[3] + above[3])) - third),
        fluid * ((here[4] + (below[4] + above[4])) - third),
        fluid * (below[1] - above[1]),
        fluid * (below[2] - above[2]),
        fluid * here[5],
    ]
    return density, momentum, stress, third


PAIRS = ((0, 0), (1, 1), (2, 2), (0, 1), (0, 2), (1, 2))


def first_state(ref, where):
    density = ref[(0,) + where]
    speed = [ref[(1 + k,) + where] for k in range(3)]
    momentum = [density * speed[k] for k in range(3)]
    stress = [momentum[one] * speed[two] for one, two in PAIRS]
    return density, speed, momentum, stress


def row_differences(speed):
    return [roll(value, -1, 0) - roll(value, 1, 0) for value in speed]


def lane_differences(speed):
    return [roll(value, -1, 1) - roll(value, 1, 1) for value in speed]


def step_one(window, state, sums):
    for plane in range(1, 15):
        density, speed, momentum, stress = first_state(window, (plane,))
        dz = [window[1 + k, plane + 1] - window[1 + k, plane - 1] for k in range(3)]
        dy = row_differences(speed)
        dx = lane_differences(speed)
        relaxation = wale([[dz[k], dy[k], dx[k]] for k in range(3)])
        stay, right, left = leaving(density, momentum, collide(momentum, speed, stress, relaxation))
        right = [roll(value, 1, 1) for value in right]
        left = [roll(value, -1, 1) for value in left]
        for k, value in enumerate(plane_sums(stay, right, left)):
            sums[k, plane] = value
    for plane in range(2, 14):
        density, momentum, stress, _ = gather_state(
            [sums[k, plane] for k in range(6)],
            [sums[6 + k, plane - 1] for k in range(5)],
            [sums[11 + k, plane + 1] for k in range(5)],
            window[4, plane],
        )
        for k, value in enumerate([density] + momentum + stress):
            state[k, plane - 2] = value


def step_two(
    window, state_one, faces, got_far, got_near, placing, tags, moments_out, relaxation_out, outgoing,
    state, sums, strip, strip_sums, edge, pooled, moments, relaxations, left_sems,
):
    even_x = is_even("gx")
    lane = lax.broadcasted_iota(jnp.int32, (16, 128), 1)
    first_lane, last_lane = lane == 0, lane == 127
    first_two, last_two = lane < 2, lane >= 126
    quarter = lax.broadcasted_iota(jnp.int32, (8, 128), 1) % 16 // 4

    for field in range(5):
        from_right = jnp.where(even_x, got_near[field], got_far[field])
        from_left = jnp.where(even_x, got_far[field], got_near[field])
        for half in range(2):
            for part in range(2):
                own = faces[field, part]
                turn = 8 * half + 4 * part
                cells = jnp.where(quarter == 0, roll(own, -8 * half, 1), roll(own, 8 - 8 * half, 1))
                cells = jnp.where(quarter == 1, roll(from_right, 4 - turn, 1), cells)
                strip[field, half, 8 * part : 8 * part + 8] = jnp.where(
                    quarter == 2, roll(from_left, 8 - turn, 1), cells
                )

    def strip_above(ref, number, half):
        return ref[number, 1] if half == 0 else roll(ref[number, 0], -16, 1)

    def strip_below(ref, number, half):
        return ref[number, 0] if half == 1 else roll(ref[number, 1], 16, 1)

    def strip_pass(step, half):
        if step == 0:
            density, speed, momentum, stress = first_state(strip, (half,))
        else:
            density = strip[0, half]
            speed = [strip[1 + k, half] for k in range(3)]
            momentum = [strip[5 + k, half] for k in range(3)]
            stress = [strip[8 + k, half] for k in range(6)]
        dz = [strip_above(strip, 1 + k, half) - strip_below(strip, 1 + k, half) for k in range(3)]
        dy = row_differences(speed)
        dx = lane_differences(speed)
        relaxation = wale([[dz[k], dy[k], dx[k]] for k in range(3)])
        return leaving(density, momentum, collide(momentum, speed, stress, relaxation))

    for half in range(2):
        stay, right, left = strip_pass(0, half)
        right = [roll(value, 1, 1) for value in right]
        left = [roll(value, -1, 1) for value in left]
        for k, value in enumerate(plane_sums(stay, right, left)):
            strip_sums[k, half] = value
    for half in range(2):
        density, momentum, stress, _ = gather_state(
            [strip_sums[k, half] for k in range(6)],
            [strip_below(strip_sums, 6 + k, half) for k in range(5)],
            [strip_above(strip_sums, 11 + k, half) for k in range(5)],
            strip[4, half],
        )
        inverse = 1.0 / density
        strip[0, half] = density
        for k in range(3):
            strip[1 + k, half] = momentum[k] * inverse
            strip[5 + k, half] = momentum[k]
        for k in range(6):
            strip[8 + k, half] = stress[k]

    for plane in range(2, 14):
        half, turn = plane % 2, plane // 2 * 16
        members = []
        for k, number in enumerate((0, 5, 6, 7, 8, 9, 10, 11, 12, 13)):
            value = jnp.where(first_two, roll(strip[number, half], -12 - turn, 1), state_one[k, plane - 2])
            members.append(jnp.where(last_two, roll(strip[number, half], 124 - turn, 1), value))
        inverse = 1.0 / members[0]
        for k in range(3):
            members.append(members[1 + k] * inverse)
        for k in range(13):
            state[k, plane] = members[k]

    for half in range(2):
        _, right, left = strip_pass(1, half)
        for k in range(5):
            edge[k, half] = right[k]
            edge[5 + k, half] = left[k]

    for plane in range(3, 13):
        half, turn = plane % 2, plane // 2 * 16

        def from_left_lane(value, ref, number):
            return jnp.where(first_lane, roll(ref[number, half], 117 - turn, 1), roll(value, 1, 1))

        def from_right_lane(value, ref, number):
            return jnp.where(last_lane, roll(ref[number, half], 123 - turn, 1), roll(value, -1, 1))

        density = state[0, plane]
        momentum = [state[1 + k, plane] for k in range(3)]
        stress = [state[4 + k, plane] for k in range(6)]
        speed = [state[10 + k, plane] for k in range(3)]
        dz = [state[10 + k, plane + 1] - state[10 + k, plane - 1] for k in range(3)]
        dy = row_differences(speed)
        dx = [
            from_right_lane(speed[k], strip, 1 + k) - from_left_lane(speed[k], strip, 1 + k)
            for k in range(3)
        ]
        relaxation = wale([[dz[k], dy[k], dx[k]] for k in range(3)])
        stay, right, left = leaving(density, momentum, collide(momentum, speed, stress, relaxation))
        right = [from_left_lane(value, edge, k) for k, value in enumerate(right)]
        left = [from_right_lane(value, edge, 5 + k) for k, value in enumerate(left)]
        for k, value in enumerate(plane_sums(stay, right, left)):
            sums[k, plane] = value[0:8]
        if 4 <= plane < 12:
            relaxations[plane - 4] = relaxation[0:8]
    copies = [pltpu.make_async_copy(relaxations, relaxation_out, left_sems.at[4])]
    copies[0].start()

    for pair in range(4):
        total = None
        for low in (2 * pair, 2 * pair + 1):
            plane = low + 4
            density, momentum, stress, third = gather_state(
                [sums[k, plane] for k in range(6)],
                [sums[6 + k, plane - 1] for k in range(5)],
                [sums[11 + k, plane + 1] for k in range(5)],
                window[4, plane, 0:8],
            )
            members = [density] + momentum + [stress[k] + third for k in range(3)] + stress[3:]
            for k in range(10):
                moments[k, low] = members[k]
            total = members if total is None else [one + two for one, two in zip(total, members)]
        for k in range(10):
            pooled[k * 32 + pair * 8 : k * 32 + pair * 8 + 8, :] = total[k]
        done = pl.ds(2 * pair, 2)
        copies.append(pltpu.make_async_copy(moments.at[:, done], moments_out.at[:, done], left_sems.at[pair]))
        copies[-1].start()

    blocks = 0.125 * (pooled[pl.ds(0, 160, stride=2), :] + pooled[pl.ds(1, 160, stride=2), :])
    payload = jnp.concatenate([blocks, tags[...]], axis=0)
    outgoing[...] = pick(placing[...], payload, ((1,), (1,)))
    for copy in copies:
        copy.wait()


def sum_by_slot(arrived, sums):
    row = lax.broadcasted_iota(jnp.int32, (128, 128), 0)
    column = lax.broadcasted_iota(jnp.int32, (128, 128), 1)
    tag = jnp.broadcast_to(arrived[:, 160:161], (128, 128))
    chosen = (column // SLOTS == row // 2 % SPAN_Y) & (tag == (column % SLOTS + 1).astype(jnp.float32))
    sums[...] = pick(chosen.astype(jnp.float32), arrived[:, 0:160], ((0,), (0,)))


def call(kernel, outs, name, scratch=(), in_hbm=0, out_spaces=None):
    extra = {"in_specs": [pl.BlockSpec(memory_space=pltpu.HBM)] * in_hbm} if in_hbm else {}
    if out_spaces:
        extra["out_specs"] = tuple(pl.BlockSpec(memory_space=space) for space in out_spaces)
    return pl.pallas_call(
        kernel,
        out_shape=outs,
        scratch_shapes=list(scratch),
        name=name,
        compiler_params=pltpu.CompilerParams(vmem_limit_bytes=48 * 1024 * 1024),
        **extra,
    )


def per_device(density, velocity, solid, owner_map, slot_map):
    placing, tags = call(
        place_blocks,
        (f32(128, 128), f32(16, 128)),
        "place_blocks",
        (pltpu.VMEM((1, 64), jnp.int32), pltpu.VMEM((1, 64), jnp.int32), pltpu.SemaphoreType.DMA((2,))),
        2,
    )(owner_map.reshape(1, 64), slot_map.reshape(1, 64))
    scalars = jnp.concatenate([density[None], 1.0 - solid[None].astype(jnp.float32)])
    near, far = call(pack_vertical, (f32(5, 4, 8, 128),) * 2, "pack_vertical")(scalars, velocity)
    near, far = swap(near, far, "gz")
    planes, high, low = call(
        pack_spanwise, (f32(5, 16, 8, 128), f32(5, 8, 8, 128), f32(5, 8, 8, 128)), "pack_spanwise"
    )(scalars, velocity, far, near, placing)
    below, above = ring(high, low, "gy")
    window, faces, near, far = call(
        pack_streamwise,
        (f32(5, 16, 16, 128), f32(5, 2, 8, 128), f32(5, 8, 128), f32(5, 8, 128)),
        "pack_streamwise",
    )(planes, below, above)
    near, far = swap(near, far, "gx")
    state = call(
        step_one, f32(10, 12, 16, 128), "step_one", (pltpu.VMEM((16, 16, 16, 128), jnp.float32),)
    )(window)
    moments, relaxation, outgoing = call(
        step_two,
        (f32(10, 8, 8, 128), f32(8, 8, 128), f32(128, 176)),
        "step_two",
        (
            pltpu.VMEM((13, 16, 16, 128), jnp.float32),
            pltpu.VMEM((16, 16, 8, 128), jnp.float32),
            pltpu.VMEM((14, 2, 16, 128), jnp.float32),
            pltpu.VMEM((16, 2, 16, 128), jnp.float32),
            pltpu.VMEM((10, 2, 16, 128), jnp.float32),
            pltpu.VMEM((320, 128), jnp.float32),
            pltpu.VMEM((10, 8, 8, 128), jnp.float32),
            pltpu.VMEM((8, 8, 128), jnp.float32),
            pltpu.SemaphoreType.DMA((5,)),
        ),
        out_spaces=(pltpu.HBM, pltpu.HBM, pltpu.VMEM),
    )(window, state, faces, far, near, placing, tags)
    arrived = lax.all_to_all(
        outgoing.reshape(SPAN_Z, 2 * SPAN_Y, 176), "gz", split_axis=0, concat_axis=0, tiled=True
    )
    sums = call(sum_by_slot, f32(128, 160), "sum_by_slot")(arrived.reshape(128, 176))
    coarse = lax.psum_scatter(sums, "gy", scatter_dimension=0, tiled=True)
    return moments, relaxation, coarse.reshape(1, 1, 1, SLOTS, 160)


def solution(mesh):
    return jax.shard_map(
        per_device,
        mesh=mesh,
        in_specs=(
            P("gz", "gy", "gx"),
            P(None, "gz", "gy", "gx"),
            P("gz", "gy", "gx"),
            P("gx", "gy", "gz", None, None),
            P("gx", "gy", "gz", None, None),
        ),
        out_specs=(P(None, "gz", "gy", "gx"), P("gz", "gy", "gx"), P("gx", "gy", "gz", None, None)),
        check_vma=False,
    )
```

```python
import jax
import jax.numpy as jnp
from jax import lax
from jax.experimental import pallas as pl
from jax.experimental.pallas import tpu as pltpu
from jax.sharding import PartitionSpec as P

SLOTS = 16
OWNERS = 64
WALE_COEFF = 0.5
BASE_VISCOSITY = 0.01
WALE_FLOOR = 1e-10


def f32(*shape):
    return jax.ShapeDtypeStruct(shape, jnp.float32)


def roll(value, shift, axis):
    size = value.shape[axis]
    if isinstance(shift, int):
        shift = shift % size
        if shift == 0:
            return value
    return pltpu.roll(value, shift, axis)


def is_even(axis):
    return lax.rem(lax.axis_index(axis), 2) == 0


def ring(high, low, axis):
    count = lax.axis_size(axis)
    below = lax.ppermute(high, axis, [(i, (i + 1) % count) for i in range(count)])
    above = lax.ppermute(low, axis, [((i + 1) % count, i) for i in range(count)])
    return below, above


def swap(near, far, axis):
    count = lax.axis_size(axis)
    near_pairs = [(i, i ^ 1) for i in range(count)]
    far_pairs = [(i, (i + 1) % count if i % 2 else (i - 1) % count) for i in range(count)]
    far = lax.ppermute(far, axis, far_pairs)
    return lax.ppermute(near, axis, near_pairs), far


def pack_vertical(scalars, velocity, near, far):
    even = is_even("gz")
    for out, upper in ((near, even), (far, jnp.logical_not(even))):

        def face(depth):
            return pl.ds(jnp.where(upper, 8 - depth, 0), depth)

        for axis in range(3):
            out[4 * axis : 4 * axis + 4] = velocity[axis, face(4)] * scalars[1, face(4)]
        out[12:15] = scalars[0, face(3)]
        out[15:17] = scalars[1, face(2)]


def pack_spanwise(scalars, velocity, got_far, got_near, placing, planes, high, low):
    del placing
    even = is_even("gz")
    row = lax.broadcasted_iota(jnp.int32, (8, 128), 0)
    front = row < 4

    def got_above(first, last):
        return jnp.where(even, got_near[first:last], got_far[first:last])

    def got_below(first, last):
        return jnp.where(even, got_far[first:last], got_near[first:last])

    fluid = scalars[1]
    planes[0, 4:12] = scalars[0]
    planes[0, 12:15] = got_above(12, 15)
    planes[0, 1:4] = got_below(12, 15)
    planes[0, 15] = jnp.ones((8, 128), jnp.float32)
    planes[0, 0] = jnp.ones((8, 128), jnp.float32)
    for axis in range(3):
        planes[1 + axis, 4:12] = velocity[axis] * fluid
        planes[1 + axis, 12:16] = got_above(4 * axis, 4 * axis + 4)
        planes[1 + axis, 0:4] = got_below(4 * axis, 4 * axis + 4)
    planes[4, 4:12] = fluid
    planes[4, 12:14] = got_above(15, 17)
    planes[4, 2:4] = got_below(15, 17)
    planes[4, 14:16] = jnp.zeros((2, 8, 128), jnp.float32)
    planes[4, 0:2] = jnp.zeros((2, 8, 128), jnp.float32)

    def pack(place, field, one, two):
        one, two = planes[field, one], planes[field, two]
        high[place] = jnp.where(front, roll(one, 4, 0), two)
        low[place] = jnp.where(front, one, roll(two, 4, 0))

    for axis in range(3):
        for pair in range(8):
            pack(8 * axis + pair, 1 + axis, 2 * pair, 2 * pair + 1)
    for pair in range(7):
        pack(24 + pair, 0, 2 * pair + 1, 2 * pair + 2)
    for place in range(3):
        upper, lower = None, None
        for part in range(4):
            cells = planes[4, 2 + 4 * place + part]
            moved_high, moved_low = roll(cells, 2 * part + 2, 0), roll(cells, 2 * part, 0)
            upper = moved_high if part == 0 else jnp.where(row // 2 == part, moved_high, upper)
            lower = moved_low if part == 0 else jnp.where(row // 2 == part, moved_low, lower)
        high[31 + place] = upper
        low[31 + place] = lower


def pack_streamwise(planes, got_below, got_above, window, faces, near, far):
    even_x = is_even("gx")
    row = lax.broadcasted_iota(jnp.int32, (8, 128), 0)
    front = row < 4
    lane = lax.broadcasted_iota(jnp.int32, (8, 128), 1)

    def outer_rows(field, plane):
        if field == 4:
            if not 2 <= plane < 14:
                return jnp.zeros((8, 128), jnp.float32)
            place, part = 31 + (plane - 2) // 4, (plane - 2) % 4
            below = jnp.where(row >= 6, roll(got_below[place], 6 - 2 * part, 0), 0.0)
            return jnp.where(row < 2, roll(got_above[place], -2 * part, 0), below)
        if field == 0:
            if not 1 <= plane < 15:
                return jnp.ones((8, 128), jnp.float32)
            place, second = 24 + (plane - 1) // 2, (plane - 1) % 2
        else:
            place, second = 8 * (field - 1) + plane // 2, plane % 2
        above, below = got_above[place], got_below[place]
        if second:
            return jnp.where(front, roll(above, 4, 0), below)
        return jnp.where(front, above, roll(below, 4, 0))

    for field in range(5):
        own = [jnp.zeros((8, 128), jnp.float32) for _ in range(2)]
        for plane in range(16):
            inner, outer = planes[field, plane], outer_rows(field, plane)
            window[field, plane, 0:8] = inner
            window[field, plane, 8:16] = outer
            here = lane // 8 == plane
            own[0] = jnp.where(here, roll(inner, 8 * plane + 4, 1), own[0])
            own[1] = jnp.where(here, roll(outer, 8 * plane + 4, 1), own[1])
        faces[field, 0] = own[0]
        faces[field, 1] = own[1]
        even_spot = lane % 8 < 4
        to_right = jnp.where(even_spot, own[0], roll(own[1], 4, 1))
        to_left = jnp.where(even_spot, roll(own[0], -4, 1), own[1])
        near[field] = jnp.where(even_x, to_right, to_left)
        far[field] = jnp.where(even_x, to_left, to_right)


def place_blocks(owners_in, slots_in, placing, tags, owners, slots, arrived):
    copies = [
        pltpu.make_async_copy(source, target, arrived.at[number])
        for number, (source, target) in enumerate(((owners_in, owners), (slots_in, slots)))
    ]
    for copy in copies:
        copy.start()
    for copy in copies:
        copy.wait()
    row = lax.broadcasted_iota(jnp.int32, (64, 128), 0)
    block = lax.broadcasted_iota(jnp.int32, (64, 128), 1) // 2
    diagonal = lax.broadcasted_iota(jnp.int32, (64, 64), 0) == lax.broadcasted_iota(jnp.int32, (64, 64), 1)
    owner_column = jnp.sum(jnp.where(diagonal, owners[...].astype(jnp.float32), 0.0), axis=1, keepdims=True)
    slot_column = jnp.sum(jnp.where(diagonal, slots[...].astype(jnp.float32), 0.0), axis=1, keepdims=True)
    owner_row = jnp.sum(jnp.where(row == block, owner_column, 0.0), axis=0, keepdims=True)
    slot = jnp.sum(jnp.where(row == block, slot_column, 0.0), axis=0, keepdims=True)
    earlier = (owner_column == owner_row) & (row < block)
    owner = owner_row.astype(jnp.int32)
    rank = jnp.sum(jnp.where(earlier, 1.0, 0.0), axis=0, keepdims=True).astype(jnp.int32)
    position = rank * OWNERS + owner
    rows = lax.broadcasted_iota(jnp.int32, (128, 128), 0)
    placing[...] = (rows == position).astype(jnp.float32)
    tags[...] = jnp.broadcast_to(0.5 * (slot + 1.0), (16, 128))


def pick(chosen, values, contract):
    chosen = chosen.astype(jnp.bfloat16)
    total = None
    for _ in range(3):
        part = values.astype(jnp.bfloat16)
        values = values - part.astype(jnp.float32)
        product = lax.dot_general(chosen, part, (contract, ((), ())), preferred_element_type=jnp.float32)
        total = product if total is None else total + product
    return total


def wale(doubled):
    (g00, g01, g02), (g10, g11, g12), (g20, g21, g22) = doubled
    s01, s02, s12 = g01 + g10, g02 + g20, g12 + g21
    q0, q1, q2 = g00 * g00, g11 * g11, g22 * g22
    strain = 0.25 * ((q0 + q1 + q2) + 0.5 * (s01 * s01 + s02 * s02 + s12 * s12))
    p01, p02, p12 = g01 * g10, g02 * g20, g12 * g21
    d0, d1, d2 = q0 + (p01 + p02), q1 + (p01 + p12), q2 + (p02 + p12)
    third = (d0 + d1 + d2) * (1.0 / 3.0)
    d0, d1, d2 = d0 - third, d1 - third, d2 - third
    d01 = (g00 + g11) * s01 + (g02 * g21 + g12 * g20)
    d02 = (g00 + g22) * s02 + (g01 * g12 + g21 * g10)
    d12 = (g11 + g22) * s12 + (g10 * g02 + g20 * g01)
    deviator = 0.0625 * ((d0 * d0 + d1 * d1 + d2 * d2) + 0.5 * (d01 * d01 + d02 * d02 + d12 * d12))
    root = jnp.sqrt(deviator)
    eddy = (WALE_COEFF * WALE_COEFF) * deviator * root / (
        strain * strain * jnp.sqrt(strain) + deviator * jnp.sqrt(root) + WALE_FLOOR
    )
    return 0.5 + 3.0 * (BASE_VISCOSITY + eddy)


def collide(momentum, speed, stress, relaxation):
    retained = 1.0 - 1.0 / relaxation
    post = []
    for column, (one, two) in enumerate(((0, 0), (1, 1), (2, 2), (0, 1), (0, 2), (1, 2))):
        balance = momentum[one] * speed[two]
        post.append(balance + retained * (stress[column] - balance))
    return post


def leaving(density, momentum, post):
    t36 = density * (1.0 / 36.0) - (post[0] + post[1] + post[2]) * (1.0 / 24.0)
    az, ay, ax = (0.125 * post[k] for k in range(3))
    rzy, rzx, ryx = (0.25 * post[k] for k in range(3, 6))
    nz, ny, nx = ((1.0 / 12.0) * momentum[k] for k in range(3))
    bz, by, bx = t36 + az, t36 + ay, t36 + ax

    def edges(base, cross, one, two):
        plus, minus = base + cross, base - cross
        both, apart = one + two, one - two
        return plus + both, plus - both, minus + apart, minus - apart

    def up(value):
        return roll(value, 1, 0)

    def down(value):
        return roll(value, -1, 0)

    zpp, zmm, zpm, zmp = edges(bz + ay, rzy, nz, ny)
    y_zp = (up(zpp), down(zpm))
    y_zm = (up(zmp), down(zmm))
    xpp, xmm, xpm, xmp = edges(bz + ax, rzx, nz, nx)
    ypp, ymm, ypm, ymp = edges(by + ax, ryx, ny, nx)
    y_plus, y_minus = up(2.0 * (by + ny)), down(2.0 * (by - ny))
    ypp, ymp = up(ypp), down(ymp)
    ypm, ymm = up(ypm), down(ymm)
    x_plus, x_minus = 2.0 * (bx + nx), 2.0 * (bx - nx)
    syy_plus, syy_minus = ypp + ymp, ypm + ymm
    right = (x_plus + syy_plus, ypp - ymp, syy_plus, xpp, xmp)
    left = (x_minus + syy_minus, ypm - ymm, syy_minus, xpm, xmm)
    stay = (12.0 * t36, y_plus, y_minus, 2.0 * (bz + nz), y_zp, 2.0 * (bz - nz), y_zm)
    return stay, right, left


def plane_sums(stay, right, left):
    rest, y_plus, y_minus, z_plus, y_zp, z_minus, y_zm = stay
    syy = y_plus + y_minus
    sxx = right[0] + left[0]
    sums = [
        (rest + syy) + sxx,
        (y_plus - y_minus) + (right[1] + left[1]),
        right[0] - left[0],
        syy + (right[2] + left[2]),
        sxx,
        right[1] - left[1],
    ]
    for face, (one, two), plus, minus in ((z_plus, y_zp, right[3], left[3]), (z_minus, y_zm, right[4], left[4])):
        yy, xx = one + two, plus + minus
        sums += [face + (yy + xx), one - two, plus - minus, yy, xx]
    return sums


def gather_state(here, below, above, fluid):
    density = here[0] + (below[0] + above[0])
    third = density * (1.0 / 3.0)
    momentum = [
        fluid * (below[0] - above[0]),
        fluid * (here[1] + (below[1] + above[1])),
        fluid * (here[2] + (below[2] + above[2])),
    ]
    stress = [
        fluid * ((below[0] + above[0]) - third),
        fluid * ((here[3] + (below[3] + above[3])) - third),
        fluid * ((here[4] + (below[4] + above[4])) - third),
        fluid * (below[1] - above[1]),
        fluid * (below[2] - above[2]),
        fluid * here[5],
    ]
    return density, momentum, stress, third


PAIRS = ((0, 0), (1, 1), (2, 2), (0, 1), (0, 2), (1, 2))


def first_state(ref, where):
    density = ref[(0,) + where]
    speed = [ref[(1 + k,) + where] for k in range(3)]
    momentum = [density * speed[k] for k in range(3)]
    stress = [momentum[one] * speed[two] for one, two in PAIRS]
    return density, speed, momentum, stress


def row_differences(speed):
    return [roll(value, -1, 0) - roll(value, 1, 0) for value in speed]


def lane_differences(speed):
    return [roll(value, -1, 1) - roll(value, 1, 1) for value in speed]


def step_one(window, state, sums):
    for plane in range(1, 15):
        density, speed, momentum, stress = first_state(window, (plane,))
        dz = [window[1 + k, plane + 1] - window[1 + k, plane - 1] for k in range(3)]
        dy = row_differences(speed)
        dx = lane_differences(speed)
        relaxation = wale([[dz[k], dy[k], dx[k]] for k in range(3)])
        stay, right, left = leaving(density, momentum, collide(momentum, speed, stress, relaxation))
        right = [roll(value, 1, 1) for value in right]
        left = [roll(value, -1, 1) for value in left]
        for k, value in enumerate(plane_sums(stay, right, left)):
            sums[k, plane] = value
    for plane in range(2, 14):
        density, momentum, stress, _ = gather_state(
            [sums[k, plane] for k in range(6)],
            [sums[6 + k, plane - 1] for k in range(5)],
            [sums[11 + k, plane + 1] for k in range(5)],
            window[4, plane],
        )
        for k, value in enumerate([density] + momentum + stress):
            state[k, plane - 2] = value


def step_two(
    window, state_one, faces, got_far, got_near, placing, tags, moments_out, relaxation_out, outgoing,
    state, sums, strip, strip_sums, edge, pooled, moments, relaxations, left_sems,
):
    even_x = is_even("gx")
    lane = lax.broadcasted_iota(jnp.int32, (16, 128), 1)
    first_lane, last_lane = lane == 0, lane == 127
    first_two, last_two = lane < 2, lane >= 126
    quarter = lax.broadcasted_iota(jnp.int32, (8, 128), 1) % 16 // 4

    for field in range(5):
        from_right = jnp.where(even_x, got_near[field], got_far[field])
        from_left = jnp.where(even_x, got_far[field], got_near[field])
        for half in range(2):
            for part in range(2):
                own = faces[field, part]
                turn = 8 * half + 4 * part
                cells = jnp.where(quarter == 0, roll(own, -8 * half, 1), roll(own, 8 - 8 * half, 1))
                cells = jnp.where(quarter == 1, roll(from_right, 4 - turn, 1), cells)
                strip[field, half, 8 * part : 8 * part + 8] = jnp.where(
                    quarter == 2, roll(from_left, 8 - turn, 1), cells
                )

    def strip_above(ref, number, half):
        return ref[number, 1] if half == 0 else roll(ref[number, 0], -16, 1)

    def strip_below(ref, number, half):
        return ref[number, 0] if half == 1 else roll(ref[number, 1], 16, 1)

    def strip_pass(step, half):
        if step == 0:
            density, speed, momentum, stress = first_state(strip, (half,))
        else:
            density = strip[0, half]
            speed = [strip[1 + k, half] for k in range(3)]
            momentum = [strip[5 + k, half] for k in range(3)]
            stress = [strip[8 + k, half] for k in range(6)]
        dz = [strip_above(strip, 1 + k, half) - strip_below(strip, 1 + k, half) for k in range(3)]
        dy = row_differences(speed)
        dx = lane_differences(speed)
        relaxation = wale([[dz[k], dy[k], dx[k]] for k in range(3)])
        return leaving(density, momentum, collide(momentum, speed, stress, relaxation))

    for half in range(2):
        stay, right, left = strip_pass(0, half)
        right = [roll(value, 1, 1) for value in right]
        left = [roll(value, -1, 1) for value in left]
        for k, value in enumerate(plane_sums(stay, right, left)):
            strip_sums[k, half] = value
    for half in range(2):
        density, momentum, stress, _ = gather_state(
            [strip_sums[k, half] for k in range(6)],
            [strip_below(strip_sums, 6 + k, half) for k in range(5)],
            [strip_above(strip_sums, 11 + k, half) for k in range(5)],
            strip[4, half],
        )
        inverse = 1.0 / density
        strip[0, half] = density
        for k in range(3):
            strip[1 + k, half] = momentum[k] * inverse
            strip[5 + k, half] = momentum[k]
        for k in range(6):
            strip[8 + k, half] = stress[k]

    for plane in range(2, 14):
        half, turn = plane % 2, plane // 2 * 16
        members = []
        for k, number in enumerate((0, 5, 6, 7, 8, 9, 10, 11, 12, 13)):
            value = jnp.where(first_two, roll(strip[number, half], -12 - turn, 1), state_one[k, plane - 2])
            members.append(jnp.where(last_two, roll(strip[number, half], 124 - turn, 1), value))
        inverse = 1.0 / members[0]
        for k in range(3):
            members.append(members[1 + k] * inverse)
        for k in range(13):
            state[k, plane] = members[k]

    for half in range(2):
        _, right, left = strip_pass(1, half)
        for k in range(5):
            edge[k, half] = right[k]
            edge[5 + k, half] = left[k]

    for plane in range(3, 13):
        half, turn = plane % 2, plane // 2 * 16

        def from_left_lane(value, ref, number):
            return jnp.where(first_lane, roll(ref[number, half], 117 - turn, 1), roll(value, 1, 1))

        def from_right_lane(value, ref, number):
            return jnp.where(last_lane, roll(ref[number, half], 123 - turn, 1), roll(value, -1, 1))

        density = state[0, plane]
        momentum = [state[1 + k, plane] for k in range(3)]
        stress = [state[4 + k, plane] for k in range(6)]
        speed = [state[10 + k, plane] for k in range(3)]
        dz = [state[10 + k, plane + 1] - state[10 + k, plane - 1] for k in range(3)]
        dy = row_differences(speed)
        dx = [
            from_right_lane(speed[k], strip, 1 + k) - from_left_lane(speed[k], strip, 1 + k)
            for k in range(3)
        ]
        relaxation = wale([[dz[k], dy[k], dx[k]] for k in range(3)])
        stay, right, left = leaving(density, momentum, collide(momentum, speed, stress, relaxation))
        right = [from_left_lane(value, edge, k) for k, value in enumerate(right)]
        left = [from_right_lane(value, edge, 5 + k) for k, value in enumerate(left)]
        for k, value in enumerate(plane_sums(stay, right, left)):
            sums[k, plane] = value[0:8]
        if 4 <= plane < 12:
            relaxations[plane - 4] = relaxation[0:8]
    copies = [pltpu.make_async_copy(relaxations, relaxation_out, left_sems.at[4])]
    copies[0].start()

    for pair in range(4):
        total = None
        for low in (2 * pair, 2 * pair + 1):
            plane = low + 4
            density, momentum, stress, third = gather_state(
                [sums[k, plane] for k in range(6)],
                [sums[6 + k, plane - 1] for k in range(5)],
                [sums[11 + k, plane + 1] for k in range(5)],
                window[4, plane, 0:8],
            )
            members = [density] + momentum + [stress[k] + third for k in range(3)] + stress[3:]
            for k in range(10):
                moments[k, low] = members[k]
            total = members if total is None else [one + two for one, two in zip(total, members)]
        for k in range(10):
            pooled[k * 32 + pair * 8 : k * 32 + pair * 8 + 8, :] = total[k]
        done = pl.ds(2 * pair, 2)
        copies.append(pltpu.make_async_copy(moments.at[:, done], moments_out.at[:, done], left_sems.at[pair]))
        copies[-1].start()

    blocks = 0.125 * (pooled[pl.ds(0, 160, stride=2), :] + pooled[pl.ds(1, 160, stride=2), :])
    payload = jnp.concatenate(
        [blocks, jnp.zeros((32, 128), jnp.float32), tags[...], jnp.zeros((48, 128), jnp.float32)], axis=0
    )
    placed = pick(placing[...], payload, ((1,), (1,)))
    outgoing[:, 0:128] = placed[0:OWNERS, 0:128]
    outgoing[:, 128:256] = placed[0:OWNERS, 128:256] + roll(placed[OWNERS:, 128:256], 32, 1)
    outgoing[:, 256:384] = placed[OWNERS:, 0:128]
    for copy in copies:
        copy.wait()


def sum_slots(arrived, coarse):
    slot = lax.broadcasted_iota(jnp.int32, (2 * OWNERS, SLOTS), 1).astype(jnp.float32)
    shared = arrived[:, 128:256]
    tag = jnp.concatenate([shared[:, 64:65], shared[:, 96:97]], axis=0)
    blocks = jnp.concatenate(
        [
            jnp.concatenate([arrived[:, 0:128], arrived[:, 256:384]], axis=0),
            jnp.concatenate([shared, roll(shared, -32, 1)], axis=0),
        ],
        axis=1,
    )
    total = pick((tag == slot + 1.0).astype(jnp.float32), blocks, ((0,), (0,)))
    coarse[...] = total[:, 0:160]


def call(kernel, outs, name, scratch=(), in_hbm=0, out_spaces=None):
    extra = {"in_specs": [pl.BlockSpec(memory_space=pltpu.HBM)] * in_hbm} if in_hbm else {}
    if out_spaces:
        extra["out_specs"] = tuple(pl.BlockSpec(memory_space=space) for space in out_spaces)
    return pl.pallas_call(
        kernel,
        out_shape=outs,
        scratch_shapes=list(scratch),
        name=name,
        compiler_params=pltpu.CompilerParams(vmem_limit_bytes=48 * 1024 * 1024),
        **extra,
    )


def per_device(density, velocity, solid, owner_map, slot_map):
    placing, tags = call(
        place_blocks,
        (f32(128, 128), f32(16, 128)),
        "place_blocks",
        (pltpu.VMEM((1, 64), jnp.int32), pltpu.VMEM((1, 64), jnp.int32), pltpu.SemaphoreType.DMA((2,))),
        2,
    )(owner_map.reshape(1, 64), slot_map.reshape(1, 64))
    scalars = jnp.concatenate([density[None], 1.0 - solid[None].astype(jnp.float32)])
    near, far = call(pack_vertical, (f32(17, 8, 128),) * 2, "pack_vertical")(scalars, velocity)
    near, far = swap(near, far, "gz")
    planes, high, low = call(
        pack_spanwise, (f32(5, 16, 8, 128), f32(34, 8, 128), f32(34, 8, 128)), "pack_spanwise"
    )(scalars, velocity, far, near, placing)
    below, above = ring(high, low, "gy")
    window, faces, near, far = call(
        pack_streamwise,
        (f32(5, 16, 16, 128), f32(5, 2, 8, 128), f32(5, 8, 128), f32(5, 8, 128)),
        "pack_streamwise",
    )(planes, below, above)
    near, far = swap(near, far, "gx")
    state = call(
        step_one, f32(10, 12, 16, 128), "step_one", (pltpu.VMEM((16, 16, 16, 128), jnp.float32),)
    )(window)
    moments, relaxation, outgoing = call(
        step_two,
        (f32(10, 8, 8, 128), f32(8, 8, 128), f32(OWNERS, 384)),
        "step_two",
        (
            pltpu.VMEM((13, 16, 16, 128), jnp.float32),
            pltpu.VMEM((16, 16, 8, 128), jnp.float32),
            pltpu.VMEM((14, 2, 16, 128), jnp.float32),
            pltpu.VMEM((16, 2, 16, 128), jnp.float32),
            pltpu.VMEM((10, 2, 16, 128), jnp.float32),
            pltpu.VMEM((320, 128), jnp.float32),
            pltpu.VMEM((10, 8, 8, 128), jnp.float32),
            pltpu.VMEM((8, 8, 128), jnp.float32),
            pltpu.SemaphoreType.DMA((5,)),
        ),
        out_spaces=(pltpu.HBM, pltpu.HBM, pltpu.VMEM),
    )(window, state, faces, far, near, placing, tags)
    arrived = lax.all_to_all(
        outgoing.reshape(OWNERS, 1, 384), ("gy", "gz"), split_axis=0, concat_axis=0, tiled=True
    )
    coarse = call(sum_slots, f32(SLOTS, 160), "sum_slots")(arrived.reshape(OWNERS, 384))
    return moments, relaxation, coarse.reshape(1, 1, 1, SLOTS, 160)


def solution(mesh):
    return jax.shard_map(
        per_device,
        mesh=mesh,
        in_specs=(
            P("gz", "gy", "gx"),
            P(None, "gz", "gy", "gx"),
            P("gz", "gy", "gx"),
            P("gx", "gy", "gz", None, None),
            P("gx", "gy", "gz", None, None),
        ),
        out_specs=(P(None, "gz", "gy", "gx"), P("gz", "gy", "gx"), P("gx", "gy", "gz", None, None)),
        check_vma=False,
    )
```

```python
import jax
import jax.numpy as jnp
from jax import lax
from jax.experimental import pallas as pl
from jax.experimental.pallas import tpu as pltpu
from jax.sharding import PartitionSpec as P

SLOTS = 16
OWNERS = 64
WALE_COEFF = 0.5
BASE_VISCOSITY = 0.01
WALE_FLOOR = 1e-10


def f32(*shape):
    return jax.ShapeDtypeStruct(shape, jnp.float32)


def roll(value, shift, axis):
    size = value.shape[axis]
    if isinstance(shift, int):
        shift = shift % size
        if shift == 0:
            return value
    return pltpu.roll(value, shift, axis)


def is_even(axis):
    return lax.rem(lax.axis_index(axis), 2) == 0


def ring(high, low, axis):
    count = lax.axis_size(axis)
    below = lax.ppermute(high, axis, [(i, (i + 1) % count) for i in range(count)])
    above = lax.ppermute(low, axis, [((i + 1) % count, i) for i in range(count)])
    return below, above


def swap(near, far, axis):
    count = lax.axis_size(axis)
    near_pairs = [(i, i ^ 1) for i in range(count)]
    far_pairs = [(i, (i + 1) % count if i % 2 else (i - 1) % count) for i in range(count)]
    far = lax.ppermute(far, axis, far_pairs)
    return lax.ppermute(near, axis, near_pairs), far


def pack_vertical(scalars, velocity, near, far):
    even = is_even("gz")
    for out, upper in ((near, even), (far, jnp.logical_not(even))):

        def face(depth):
            return pl.ds(jnp.where(upper, 8 - depth, 0), depth)

        for axis in range(3):
            out[4 * axis : 4 * axis + 4] = velocity[axis, face(4)] * scalars[1, face(4)]
        out[12:15] = scalars[0, face(3)]
        out[15:17] = scalars[1, face(2)]


def pack_spanwise(scalars, velocity, got_far, got_near, placing, planes, high, low):
    del placing
    even = is_even("gz")
    row = lax.broadcasted_iota(jnp.int32, (8, 128), 0)
    front = row < 4

    def got_above(first, last):
        return jnp.where(even, got_near[first:last], got_far[first:last])

    def got_below(first, last):
        return jnp.where(even, got_far[first:last], got_near[first:last])

    fluid = scalars[1]
    planes[0, 4:12] = scalars[0]
    planes[0, 12:15] = got_above(12, 15)
    planes[0, 1:4] = got_below(12, 15)
    planes[0, 15] = jnp.ones((8, 128), jnp.float32)
    planes[0, 0] = jnp.ones((8, 128), jnp.float32)
    for axis in range(3):
        planes[1 + axis, 4:12] = velocity[axis] * fluid
        planes[1 + axis, 12:16] = got_above(4 * axis, 4 * axis + 4)
        planes[1 + axis, 0:4] = got_below(4 * axis, 4 * axis + 4)
    planes[4, 4:12] = fluid
    planes[4, 12:14] = got_above(15, 17)
    planes[4, 2:4] = got_below(15, 17)
    planes[4, 14:16] = jnp.zeros((2, 8, 128), jnp.float32)
    planes[4, 0:2] = jnp.zeros((2, 8, 128), jnp.float32)

    def pack(place, field, one, two):
        one, two = planes[field, one], planes[field, two]
        high[place] = jnp.where(front, roll(one, 4, 0), two)
        low[place] = jnp.where(front, one, roll(two, 4, 0))

    for axis in range(3):
        for pair in range(8):
            pack(8 * axis + pair, 1 + axis, 2 * pair, 2 * pair + 1)
    for pair in range(7):
        pack(24 + pair, 0, 2 * pair + 1, 2 * pair + 2)
    for place in range(3):
        upper, lower = None, None
        for part in range(4):
            cells = planes[4, 2 + 4 * place + part]
            moved_high, moved_low = roll(cells, 2 * part + 2, 0), roll(cells, 2 * part, 0)
            upper = moved_high if part == 0 else jnp.where(row // 2 == part, moved_high, upper)
            lower = moved_low if part == 0 else jnp.where(row // 2 == part, moved_low, lower)
        high[31 + place] = upper
        low[31 + place] = lower


def pack_streamwise(planes, got_below, got_above, window, faces, right, left):
    row = lax.broadcasted_iota(jnp.int32, (8, 128), 0)
    front = row < 4
    lane = lax.broadcasted_iota(jnp.int32, (8, 128), 1)

    def outer_rows(field, plane):
        if field == 4:
            if not 2 <= plane < 14:
                return jnp.zeros((8, 128), jnp.float32)
            place, part = 31 + (plane - 2) // 4, (plane - 2) % 4
            below = jnp.where(row >= 6, roll(got_below[place], 6 - 2 * part, 0), 0.0)
            return jnp.where(row < 2, roll(got_above[place], -2 * part, 0), below)
        if field == 0:
            if not 1 <= plane < 15:
                return jnp.ones((8, 128), jnp.float32)
            place, second = 24 + (plane - 1) // 2, (plane - 1) % 2
        else:
            place, second = 8 * (field - 1) + plane // 2, plane % 2
        above, below = got_above[place], got_below[place]
        if second:
            return jnp.where(front, roll(above, 4, 0), below)
        return jnp.where(front, above, roll(below, 4, 0))

    for field in range(5):
        own = [jnp.zeros((8, 128), jnp.float32) for _ in range(2)]
        for plane in range(16):
            inner, outer = planes[field, plane], outer_rows(field, plane)
            window[field, plane, 0:8] = inner
            window[field, plane, 8:16] = outer
            here = lane // 8 == plane
            own[0] = jnp.where(here, roll(inner, 8 * plane + 4, 1), own[0])
            own[1] = jnp.where(here, roll(outer, 8 * plane + 4, 1), own[1])
        faces[field, 0] = own[0]
        faces[field, 1] = own[1]
        even_spot = lane % 8 < 4
        right[field] = jnp.where(even_spot, own[0], roll(own[1], 4, 1))
        left[field] = jnp.where(even_spot, roll(own[0], -4, 1), own[1])


def place_blocks(owners_in, slots_in, placing, tags, owners, slots, arrived):
    copies = [
        pltpu.make_async_copy(source, target, arrived.at[number])
        for number, (source, target) in enumerate(((owners_in, owners), (slots_in, slots)))
    ]
    for copy in copies:
        copy.start()
    for copy in copies:
        copy.wait()
    row = lax.broadcasted_iota(jnp.int32, (64, 128), 0)
    block = lax.broadcasted_iota(jnp.int32, (64, 128), 1) // 2
    diagonal = lax.broadcasted_iota(jnp.int32, (64, 64), 0) == lax.broadcasted_iota(jnp.int32, (64, 64), 1)
    owner_column = jnp.sum(jnp.where(diagonal, owners[...].astype(jnp.float32), 0.0), axis=1, keepdims=True)
    slot_column = jnp.sum(jnp.where(diagonal, slots[...].astype(jnp.float32), 0.0), axis=1, keepdims=True)
    owner_row = jnp.sum(jnp.where(row == block, owner_column, 0.0), axis=0, keepdims=True)
    slot = jnp.sum(jnp.where(row == block, slot_column, 0.0), axis=0, keepdims=True)
    earlier = (owner_column == owner_row) & (row < block)
    owner = owner_row.astype(jnp.int32)
    rank = jnp.sum(jnp.where(earlier, 1.0, 0.0), axis=0, keepdims=True).astype(jnp.int32)
    position = rank * OWNERS + owner
    rows = lax.broadcasted_iota(jnp.int32, (128, 128), 0)
    placing[...] = (rows == position).astype(jnp.float32)
    tags[...] = jnp.broadcast_to(0.5 * (slot + 1.0), (16, 128))


def pick(chosen, values, contract):
    chosen = chosen.astype(jnp.bfloat16)
    total = None
    for _ in range(3):
        part = values.astype(jnp.bfloat16)
        values = values - part.astype(jnp.float32)
        product = lax.dot_general(chosen, part, (contract, ((), ())), preferred_element_type=jnp.float32)
        total = product if total is None else total + product
    return total


def wale(doubled):
    (g00, g01, g02), (g10, g11, g12), (g20, g21, g22) = doubled
    s01, s02, s12 = g01 + g10, g02 + g20, g12 + g21
    q0, q1, q2 = g00 * g00, g11 * g11, g22 * g22
    strain = 0.25 * ((q0 + q1 + q2) + 0.5 * (s01 * s01 + s02 * s02 + s12 * s12))
    p01, p02, p12 = g01 * g10, g02 * g20, g12 * g21
    d0, d1, d2 = q0 + (p01 + p02), q1 + (p01 + p12), q2 + (p02 + p12)
    third = (d0 + d1 + d2) * (1.0 / 3.0)
    d0, d1, d2 = d0 - third, d1 - third, d2 - third
    d01 = (g00 + g11) * s01 + (g02 * g21 + g12 * g20)
    d02 = (g00 + g22) * s02 + (g01 * g12 + g21 * g10)
    d12 = (g11 + g22) * s12 + (g10 * g02 + g20 * g01)
    deviator = 0.0625 * ((d0 * d0 + d1 * d1 + d2 * d2) + 0.5 * (d01 * d01 + d02 * d02 + d12 * d12))
    root = jnp.sqrt(deviator)
    eddy = (WALE_COEFF * WALE_COEFF) * deviator * root / (
        strain * strain * jnp.sqrt(strain) + deviator * jnp.sqrt(root) + WALE_FLOOR
    )
    return 0.5 + 3.0 * (BASE_VISCOSITY + eddy)


def collide(momentum, speed, stress, relaxation):
    retained = 1.0 - 1.0 / relaxation
    post = []
    for column, (one, two) in enumerate(((0, 0), (1, 1), (2, 2), (0, 1), (0, 2), (1, 2))):
        balance = momentum[one] * speed[two]
        post.append(balance + retained * (stress[column] - balance))
    return post


def leaving(density, momentum, post):
    t36 = density * (1.0 / 36.0) - (post[0] + post[1] + post[2]) * (1.0 / 24.0)
    az, ay, ax = (0.125 * post[k] for k in range(3))
    rzy, rzx, ryx = (0.25 * post[k] for k in range(3, 6))
    nz, ny, nx = ((1.0 / 12.0) * momentum[k] for k in range(3))
    bz, by, bx = t36 + az, t36 + ay, t36 + ax

    def edges(base, cross, one, two):
        plus, minus = base + cross, base - cross
        both, apart = one + two, one - two
        return plus + both, plus - both, minus + apart, minus - apart

    def up(value):
        return roll(value, 1, 0)

    def down(value):
        return roll(value, -1, 0)

    zpp, zmm, zpm, zmp = edges(bz + ay, rzy, nz, ny)
    y_zp = (up(zpp), down(zpm))
    y_zm = (up(zmp), down(zmm))
    xpp, xmm, xpm, xmp = edges(bz + ax, rzx, nz, nx)
    ypp, ymm, ypm, ymp = edges(by + ax, ryx, ny, nx)
    y_plus, y_minus = up(2.0 * (by + ny)), down(2.0 * (by - ny))
    ypp, ymp = up(ypp), down(ymp)
    ypm, ymm = up(ypm), down(ymm)
    x_plus, x_minus = 2.0 * (bx + nx), 2.0 * (bx - nx)
    syy_plus, syy_minus = ypp + ymp, ypm + ymm
    right = (x_plus + syy_plus, ypp - ymp, syy_plus, xpp, xmp)
    left = (x_minus + syy_minus, ypm - ymm, syy_minus, xpm, xmm)
    stay = (12.0 * t36, y_plus, y_minus, 2.0 * (bz + nz), y_zp, 2.0 * (bz - nz), y_zm)
    return stay, right, left


def plane_sums(stay, right, left):
    rest, y_plus, y_minus, z_plus, y_zp, z_minus, y_zm = stay
    syy = y_plus + y_minus
    sxx = right[0] + left[0]
    sums = [
        (rest + syy) + sxx,
        (y_plus - y_minus) + (right[1] + left[1]),
        right[0] - left[0],
        syy + (right[2] + left[2]),
        sxx,
        right[1] - left[1],
    ]
    for face, (one, two), plus, minus in ((z_plus, y_zp, right[3], left[3]), (z_minus, y_zm, right[4], left[4])):
        yy, xx = one + two, plus + minus
        sums += [face + (yy + xx), one - two, plus - minus, yy, xx]
    return sums


def gather_state(here, below, above, fluid):
    density = here[0] + (below[0] + above[0])
    third = density * (1.0 / 3.0)
    momentum = [
        fluid * (below[0] - above[0]),
        fluid * (here[1] + (below[1] + above[1])),
        fluid * (here[2] + (below[2] + above[2])),
    ]
    stress = [
        fluid * ((below[0] + above[0]) - third),
        fluid * ((here[3] + (below[3] + above[3])) - third),
        fluid * ((here[4] + (below[4] + above[4])) - third),
        fluid * (below[1] - above[1]),
        fluid * (below[2] - above[2]),
        fluid * here[5],
    ]
    return density, momentum, stress, third


PAIRS = ((0, 0), (1, 1), (2, 2), (0, 1), (0, 2), (1, 2))


def first_state(ref, where):
    density = ref[(0,) + where]
    speed = [ref[(1 + k,) + where] for k in range(3)]
    momentum = [density * speed[k] for k in range(3)]
    stress = [momentum[one] * speed[two] for one, two in PAIRS]
    return density, speed, momentum, stress


def row_differences(speed):
    return [roll(value, -1, 0) - roll(value, 1, 0) for value in speed]


def lane_differences(speed):
    return [roll(value, -1, 1) - roll(value, 1, 1) for value in speed]


def step_one(window, state, sums):
    for plane in range(1, 15):
        density, speed, momentum, stress = first_state(window, (plane,))
        dz = [window[1 + k, plane + 1] - window[1 + k, plane - 1] for k in range(3)]
        dy = row_differences(speed)
        dx = lane_differences(speed)
        relaxation = wale([[dz[k], dy[k], dx[k]] for k in range(3)])
        stay, right, left = leaving(density, momentum, collide(momentum, speed, stress, relaxation))
        right = [roll(value, 1, 1) for value in right]
        left = [roll(value, -1, 1) for value in left]
        for k, value in enumerate(plane_sums(stay, right, left)):
            sums[k, plane] = value
    for plane in range(2, 14):
        density, momentum, stress, _ = gather_state(
            [sums[k, plane] for k in range(6)],
            [sums[6 + k, plane - 1] for k in range(5)],
            [sums[11 + k, plane + 1] for k in range(5)],
            window[4, plane],
        )
        for k, value in enumerate([density] + momentum + stress):
            state[k, plane - 2] = value


def step_two(
    window, state_one, faces, from_left, from_right, placing, tags, moments_out, relaxation_out, outgoing,
    state, sums, strip, strip_sums, edge, pooled, moments, relaxations, left_sems,
):
    lane = lax.broadcasted_iota(jnp.int32, (16, 128), 1)
    first_lane, last_lane = lane == 0, lane == 127
    first_two, last_two = lane < 2, lane >= 126
    quarter = lax.broadcasted_iota(jnp.int32, (8, 128), 1) % 16 // 4

    for field in range(5):
        got_right, got_left = from_right[field], from_left[field]
        for half in range(2):
            for part in range(2):
                own = faces[field, part]
                turn = 8 * half + 4 * part
                cells = jnp.where(quarter == 0, roll(own, -8 * half, 1), roll(own, 8 - 8 * half, 1))
                cells = jnp.where(quarter == 1, roll(got_right, 4 - turn, 1), cells)
                strip[field, half, 8 * part : 8 * part + 8] = jnp.where(
                    quarter == 2, roll(got_left, 8 - turn, 1), cells
                )

    def strip_above(ref, number, half):
        return ref[number, 1] if half == 0 else roll(ref[number, 0], -16, 1)

    def strip_below(ref, number, half):
        return ref[number, 0] if half == 1 else roll(ref[number, 1], 16, 1)

    def strip_pass(step, half):
        if step == 0:
            density, speed, momentum, stress = first_state(strip, (half,))
        else:
            density = strip[0, half]
            speed = [strip[1 + k, half] for k in range(3)]
            momentum = [strip[5 + k, half] for k in range(3)]
            stress = [strip[8 + k, half] for k in range(6)]
        dz = [strip_above(strip, 1 + k, half) - strip_below(strip, 1 + k, half) for k in range(3)]
        dy = row_differences(speed)
        dx = lane_differences(speed)
        relaxation = wale([[dz[k], dy[k], dx[k]] for k in range(3)])
        return leaving(density, momentum, collide(momentum, speed, stress, relaxation))

    for half in range(2):
        stay, right, left = strip_pass(0, half)
        right = [roll(value, 1, 1) for value in right]
        left = [roll(value, -1, 1) for value in left]
        for k, value in enumerate(plane_sums(stay, right, left)):
            strip_sums[k, half] = value
    for half in range(2):
        density, momentum, stress, _ = gather_state(
            [strip_sums[k, half] for k in range(6)],
            [strip_below(strip_sums, 6 + k, half) for k in range(5)],
            [strip_above(strip_sums, 11 + k, half) for k in range(5)],
            strip[4, half],
        )
        inverse = 1.0 / density
        strip[0, half] = density
        for k in range(3):
            strip[1 + k, half] = momentum[k] * inverse
            strip[5 + k, half] = momentum[k]
        for k in range(6):
            strip[8 + k, half] = stress[k]

    for plane in range(2, 14):
        half, turn = plane % 2, plane // 2 * 16
        members = []
        for k, number in enumerate((0, 5, 6, 7, 8, 9, 10, 11, 12, 13)):
            value = jnp.where(first_two, roll(strip[number, half], -12 - turn, 1), state_one[k, plane - 2])
            members.append(jnp.where(last_two, roll(strip[number, half], 124 - turn, 1), value))
        inverse = 1.0 / members[0]
        for k in range(3):
            members.append(members[1 + k] * inverse)
        for k in range(13):
            state[k, plane] = members[k]

    for half in range(2):
        _, right, left = strip_pass(1, half)
        for k in range(5):
            edge[k, half] = right[k]
            edge[5 + k, half] = left[k]

    for plane in range(3, 13):
        half, turn = plane % 2, plane // 2 * 16

        def from_left_lane(value, ref, number):
            return jnp.where(first_lane, roll(ref[number, half], 117 - turn, 1), roll(value, 1, 1))

        def from_right_lane(value, ref, number):
            return jnp.where(last_lane, roll(ref[number, half], 123 - turn, 1), roll(value, -1, 1))

        density = state[0, plane]
        momentum = [state[1 + k, plane] for k in range(3)]
        stress = [state[4 + k, plane] for k in range(6)]
        speed = [state[10 + k, plane] for k in range(3)]
        dz = [state[10 + k, plane + 1] - state[10 + k, plane - 1] for k in range(3)]
        dy = row_differences(speed)
        dx = [
            from_right_lane(speed[k], strip, 1 + k) - from_left_lane(speed[k], strip, 1 + k)
            for k in range(3)
        ]
        relaxation = wale([[dz[k], dy[k], dx[k]] for k in range(3)])
        stay, right, left = leaving(density, momentum, collide(momentum, speed, stress, relaxation))
        right = [from_left_lane(value, edge, k) for k, value in enumerate(right)]
        left = [from_right_lane(value, edge, 5 + k) for k, value in enumerate(left)]
        for k, value in enumerate(plane_sums(stay, right, left)):
            sums[k, plane] = value[0:8]
        if 4 <= plane < 12:
            relaxations[plane - 4] = relaxation[0:8]
    copies = [pltpu.make_async_copy(relaxations, relaxation_out, left_sems.at[4])]
    copies[0].start()

    for pair in range(4):
        total = None
        for low in (2 * pair, 2 * pair + 1):
            plane = low + 4
            density, momentum, stress, third = gather_state(
                [sums[k, plane] for k in range(6)],
                [sums[6 + k, plane - 1] for k in range(5)],
                [sums[11 + k, plane + 1] for k in range(5)],
                window[4, plane, 0:8],
            )
            members = [density] + momentum + [stress[k] + third for k in range(3)] + stress[3:]
            for k in range(10):
                moments[k, low] = members[k]
            total = members if total is None else [one + two for one, two in zip(total, members)]
        for k in range(10):
            pooled[k * 32 + pair * 8 : k * 32 + pair * 8 + 8, :] = total[k]
        done = pl.ds(2 * pair, 2)
        copies.append(pltpu.make_async_copy(moments.at[:, done], moments_out.at[:, done], left_sems.at[pair]))
        copies[-1].start()

    blocks = 0.125 * (pooled[pl.ds(0, 160, stride=2), :] + pooled[pl.ds(1, 160, stride=2), :])
    payload = jnp.concatenate(
        [blocks, jnp.zeros((32, 128), jnp.float32), tags[...], jnp.zeros((48, 128), jnp.float32)], axis=0
    )
    placed = pick(placing[...], payload, ((1,), (1,)))
    outgoing[:, 0:128] = placed[0:OWNERS, 0:128]
    outgoing[:, 128:256] = placed[0:OWNERS, 128:256] + roll(placed[OWNERS:, 128:256], 32, 1)
    outgoing[:, 256:384] = placed[OWNERS:, 0:128]
    for copy in copies:
        copy.wait()


def sum_slots(arrived, coarse):
    slot = lax.broadcasted_iota(jnp.int32, (2 * OWNERS, SLOTS), 1).astype(jnp.float32)
    shared = arrived[:, 128:256]
    tag = jnp.concatenate([shared[:, 64:65], shared[:, 96:97]], axis=0)
    blocks = jnp.concatenate(
        [
            jnp.concatenate([arrived[:, 0:128], arrived[:, 256:384]], axis=0),
            jnp.concatenate([shared, roll(shared, -32, 1)], axis=0),
        ],
        axis=1,
    )
    total = pick((tag == slot + 1.0).astype(jnp.float32), blocks, ((0,), (0,)))
    coarse[...] = total[:, 0:160]


def call(kernel, outs, name, scratch=(), in_hbm=0, out_spaces=None):
    extra = {"in_specs": [pl.BlockSpec(memory_space=pltpu.HBM)] * in_hbm} if in_hbm else {}
    if out_spaces:
        extra["out_specs"] = tuple(pl.BlockSpec(memory_space=space) for space in out_spaces)
    return pl.pallas_call(
        kernel,
        out_shape=outs,
        scratch_shapes=list(scratch),
        name=name,
        compiler_params=pltpu.CompilerParams(vmem_limit_bytes=48 * 1024 * 1024),
        **extra,
    )


def per_device(density, velocity, solid, owner_map, slot_map):
    placing, tags = call(
        place_blocks,
        (f32(128, 128), f32(16, 128)),
        "place_blocks",
        (pltpu.VMEM((1, 64), jnp.int32), pltpu.VMEM((1, 64), jnp.int32), pltpu.SemaphoreType.DMA((2,))),
        2,
    )(owner_map.reshape(1, 64), slot_map.reshape(1, 64))
    scalars = jnp.concatenate([density[None], 1.0 - solid[None].astype(jnp.float32)])
    near, far = call(pack_vertical, (f32(17, 8, 128),) * 2, "pack_vertical")(scalars, velocity)
    near, far = swap(near, far, "gz")
    planes, high, low = call(
        pack_spanwise, (f32(5, 16, 8, 128), f32(34, 8, 128), f32(34, 8, 128)), "pack_spanwise"
    )(scalars, velocity, far, near, placing)
    below, above = ring(high, low, "gy")
    window, faces, right, left = call(
        pack_streamwise,
        (f32(5, 16, 16, 128), f32(5, 2, 8, 128), f32(5, 8, 128), f32(5, 8, 128)),
        "pack_streamwise",
    )(planes, below, above)
    left, right = ring(right, left, "gx")
    state = call(
        step_one, f32(10, 12, 16, 128), "step_one", (pltpu.VMEM((16, 16, 16, 128), jnp.float32),)
    )(window)
    moments, relaxation, outgoing = call(
        step_two,
        (f32(10, 8, 8, 128), f32(8, 8, 128), f32(OWNERS, 384)),
        "step_two",
        (
            pltpu.VMEM((13, 16, 16, 128), jnp.float32),
            pltpu.VMEM((16, 16, 8, 128), jnp.float32),
            pltpu.VMEM((14, 2, 16, 128), jnp.float32),
            pltpu.VMEM((16, 2, 16, 128), jnp.float32),
            pltpu.VMEM((10, 2, 16, 128), jnp.float32),
            pltpu.VMEM((320, 128), jnp.float32),
            pltpu.VMEM((10, 8, 8, 128), jnp.float32),
            pltpu.VMEM((8, 8, 128), jnp.float32),
            pltpu.SemaphoreType.DMA((5,)),
        ),
        out_spaces=(pltpu.HBM, pltpu.HBM, pltpu.VMEM),
    )(window, state, faces, left, right, placing, tags)
    arrived = lax.all_to_all(
        outgoing.reshape(OWNERS, 1, 384), ("gy", "gz"), split_axis=0, concat_axis=0, tiled=True
    )
    coarse = call(sum_slots, f32(SLOTS, 160), "sum_slots")(arrived.reshape(OWNERS, 384))
    return moments, relaxation, coarse.reshape(1, 1, 1, SLOTS, 160)


def solution(mesh):
    return jax.shard_map(
        per_device,
        mesh=mesh,
        in_specs=(
            P("gz", "gy", "gx"),
            P(None, "gz", "gy", "gx"),
            P("gz", "gy", "gx"),
            P("gx", "gy", "gz", None, None),
            P("gx", "gy", "gz", None, None),
        ),
        out_specs=(P(None, "gz", "gy", "gx"), P("gz", "gy", "gx"), P("gx", "gy", "gz", None, None)),
        check_vma=False,
    )
```

```python
import jax
import jax.numpy as jnp
from jax import lax
from jax.experimental import pallas as pl
from jax.experimental.pallas import tpu as pltpu
from jax.sharding import PartitionSpec as P

SLOTS = 16
SPAN_Y = 8
SPAN_Z = 8
OWNERS = SPAN_Y * SPAN_Z
WALE_COEFF = 0.5
BASE_VISCOSITY = 0.01
WALE_FLOOR = 1e-10


def f32(*shape):
    return jax.ShapeDtypeStruct(shape, jnp.float32)


def roll(value, shift, axis):
    size = value.shape[axis]
    if isinstance(shift, int):
        shift = shift % size
        if shift == 0:
            return value
    return pltpu.roll(value, shift, axis)


def is_even(axis):
    return lax.rem(lax.axis_index(axis), 2) == 0


def from_lower(high, axis):
    count = lax.axis_size(axis)
    return lax.ppermute(high, axis, [(i, (i + 1) % count) for i in range(count)])


def from_upper(low, axis):
    count = lax.axis_size(axis)
    return lax.ppermute(low, axis, [((i + 1) % count, i) for i in range(count)])


def swap(near, far, axis):
    count = lax.axis_size(axis)
    near_pairs = [(i, i ^ 1) for i in range(count)]
    far_pairs = [(i, (i + 1) % count if i % 2 else (i - 1) % count) for i in range(count)]
    far = lax.ppermute(far, axis, far_pairs)
    return lax.ppermute(near, axis, near_pairs), far


def pack_vertical(scalars, velocity, near, far):
    even = is_even("gz")
    for out, upper in ((near, even), (far, jnp.logical_not(even))):

        def face(depth):
            return pl.ds(jnp.where(upper, 8 - depth, 0), depth)

        for axis in range(3):
            out[4 * axis : 4 * axis + 4] = velocity[axis, face(4)] * scalars[1, face(4)]
        out[12:15] = scalars[0, face(3)]
        out[15:17] = scalars[1, face(2)]


def pack_spanwise(scalars, velocity, got_far, got_near, placing, planes, high, low):
    del placing
    even = is_even("gz")
    row = lax.broadcasted_iota(jnp.int32, (8, 128), 0)
    front = row < 4

    def got_above(first, last):
        return jnp.where(even, got_near[first:last], got_far[first:last])

    def got_below(first, last):
        return jnp.where(even, got_far[first:last], got_near[first:last])

    fluid = scalars[1]
    planes[0, 4:12] = scalars[0]
    planes[0, 12:15] = got_above(12, 15)
    planes[0, 1:4] = got_below(12, 15)
    planes[0, 15] = jnp.ones((8, 128), jnp.float32)
    planes[0, 0] = jnp.ones((8, 128), jnp.float32)
    for axis in range(3):
        planes[1 + axis, 4:12] = velocity[axis] * fluid
        planes[1 + axis, 12:16] = got_above(4 * axis, 4 * axis + 4)
        planes[1 + axis, 0:4] = got_below(4 * axis, 4 * axis + 4)
    planes[4, 4:12] = fluid
    planes[4, 12:14] = got_above(15, 17)
    planes[4, 2:4] = got_below(15, 17)
    planes[4, 14:16] = jnp.zeros((2, 8, 128), jnp.float32)
    planes[4, 0:2] = jnp.zeros((2, 8, 128), jnp.float32)

    def pack(place, field, one, two):
        one, two = planes[field, one], planes[field, two]
        high[place] = jnp.where(front, roll(one, 4, 0), two)
        low[place] = jnp.where(front, one, roll(two, 4, 0))

    for axis in range(3):
        for pair in range(8):
            pack(8 * axis + pair, 1 + axis, 2 * pair, 2 * pair + 1)
    for pair in range(7):
        pack(24 + pair, 0, 2 * pair + 1, 2 * pair + 2)
    for place in range(3):
        upper, lower = None, None
        for part in range(4):
            cells = planes[4, 2 + 4 * place + part]
            moved_high, moved_low = roll(cells, 2 * part + 2, 0), roll(cells, 2 * part, 0)
            upper = moved_high if part == 0 else jnp.where(row // 2 == part, moved_high, upper)
            lower = moved_low if part == 0 else jnp.where(row // 2 == part, moved_low, lower)
        high[31 + place] = upper
        low[31 + place] = lower


def pack_streamwise(planes, got_above, got_below, window, faces, right, left):
    row = lax.broadcasted_iota(jnp.int32, (8, 128), 0)
    front = row < 4
    lane = lax.broadcasted_iota(jnp.int32, (8, 128), 1)

    def outer_rows(field, plane):
        if field == 4:
            if not 2 <= plane < 14:
                return jnp.zeros((8, 128), jnp.float32)
            place, part = 31 + (plane - 2) // 4, (plane - 2) % 4
            below = jnp.where(row >= 6, roll(got_below[place], 6 - 2 * part, 0), 0.0)
            return jnp.where(row < 2, roll(got_above[place], -2 * part, 0), below)
        if field == 0:
            if not 1 <= plane < 15:
                return jnp.ones((8, 128), jnp.float32)
            place, second = 24 + (plane - 1) // 2, (plane - 1) % 2
        else:
            place, second = 8 * (field - 1) + plane // 2, plane % 2
        above, below = got_above[place], got_below[place]
        if second:
            return jnp.where(front, roll(above, 4, 0), below)
        return jnp.where(front, above, roll(below, 4, 0))

    for field in range(5):
        own = [jnp.zeros((8, 128), jnp.float32) for _ in range(2)]
        for plane in range(16):
            inner, outer = planes[field, plane], outer_rows(field, plane)
            window[field, plane, 0:8] = inner
            window[field, plane, 8:16] = outer
            here = lane // 8 == plane
            own[0] = jnp.where(here, roll(inner, 8 * plane + 4, 1), own[0])
            own[1] = jnp.where(here, roll(outer, 8 * plane + 4, 1), own[1])
        faces[field, 0] = own[0]
        faces[field, 1] = own[1]
        even_spot = lane % 8 < 4
        right[field] = jnp.where(even_spot, own[0], roll(own[1], 4, 1))
        left[field] = jnp.where(even_spot, roll(own[0], -4, 1), own[1])


def place_blocks(owners_in, slots_in, placing, tags, owners, slots, arrived):
    copies = [
        pltpu.make_async_copy(source, target, arrived.at[number])
        for number, (source, target) in enumerate(((owners_in, owners), (slots_in, slots)))
    ]
    for copy in copies:
        copy.start()
    for copy in copies:
        copy.wait()
    row = lax.broadcasted_iota(jnp.int32, (64, 128), 0)
    block = lax.broadcasted_iota(jnp.int32, (64, 128), 1) // 2
    diagonal = lax.broadcasted_iota(jnp.int32, (64, 64), 0) == lax.broadcasted_iota(jnp.int32, (64, 64), 1)
    owner_column = jnp.sum(jnp.where(diagonal, owners[...].astype(jnp.float32), 0.0), axis=1, keepdims=True)
    slot_column = jnp.sum(jnp.where(diagonal, slots[...].astype(jnp.float32), 0.0), axis=1, keepdims=True)
    owner_row = jnp.sum(jnp.where(row == block, owner_column, 0.0), axis=0, keepdims=True)
    slot = jnp.sum(jnp.where(row == block, slot_column, 0.0), axis=0, keepdims=True)
    earlier = (owner_column == owner_row) & (row < block)
    owner = owner_row.astype(jnp.int32)
    rank = jnp.sum(jnp.where(earlier, 1.0, 0.0), axis=0, keepdims=True).astype(jnp.int32)
    position = rank * OWNERS + lax.rem(owner, SPAN_Z) * SPAN_Y + lax.div(owner, SPAN_Z)
    rows = lax.broadcasted_iota(jnp.int32, (128, 128), 0)
    placing[...] = (rows == position).astype(jnp.float32)
    tags[...] = jnp.broadcast_to(0.5 * (slot + 1.0), (16, 128))


def pick(chosen, values, contract):
    chosen = chosen.astype(jnp.bfloat16)
    total = None
    for _ in range(3):
        part = values.astype(jnp.bfloat16)
        values = values - part.astype(jnp.float32)
        product = lax.dot_general(chosen, part, (contract, ((), ())), preferred_element_type=jnp.float32)
        total = product if total is None else total + product
    return total


def wale(doubled):
    (g00, g01, g02), (g10, g11, g12), (g20, g21, g22) = doubled
    s01, s02, s12 = g01 + g10, g02 + g20, g12 + g21
    q0, q1, q2 = g00 * g00, g11 * g11, g22 * g22
    strain = 0.25 * ((q0 + q1 + q2) + 0.5 * (s01 * s01 + s02 * s02 + s12 * s12))
    p01, p02, p12 = g01 * g10, g02 * g20, g12 * g21
    d0, d1, d2 = q0 + (p01 + p02), q1 + (p01 + p12), q2 + (p02 + p12)
    third = (d0 + d1 + d2) * (1.0 / 3.0)
    d0, d1, d2 = d0 - third, d1 - third, d2 - third
    d01 = (g00 + g11) * s01 + (g02 * g21 + g12 * g20)
    d02 = (g00 + g22) * s02 + (g01 * g12 + g21 * g10)
    d12 = (g11 + g22) * s12 + (g10 * g02 + g20 * g01)
    deviator = 0.0625 * ((d0 * d0 + d1 * d1 + d2 * d2) + 0.5 * (d01 * d01 + d02 * d02 + d12 * d12))
    root = jnp.sqrt(deviator)
    eddy = (WALE_COEFF * WALE_COEFF) * deviator * root / (
        strain * strain * jnp.sqrt(strain) + deviator * jnp.sqrt(root) + WALE_FLOOR
    )
    return 0.5 + 3.0 * (BASE_VISCOSITY + eddy)


def collide(momentum, speed, stress, relaxation):
    retained = 1.0 - 1.0 / relaxation
    post = []
    for column, (one, two) in enumerate(((0, 0), (1, 1), (2, 2), (0, 1), (0, 2), (1, 2))):
        balance = momentum[one] * speed[two]
        post.append(balance + retained * (stress[column] - balance))
    return post


def leaving(density, momentum, post):
    t36 = density * (1.0 / 36.0) - (post[0] + post[1] + post[2]) * (1.0 / 24.0)
    az, ay, ax = (0.125 * post[k] for k in range(3))
    rzy, rzx, ryx = (0.25 * post[k] for k in range(3, 6))
    nz, ny, nx = ((1.0 / 12.0) * momentum[k] for k in range(3))
    bz, by, bx = t36 + az, t36 + ay, t36 + ax

    def edges(base, cross, one, two):
        plus, minus = base + cross, base - cross
        both, apart = one + two, one - two
        return plus + both, plus - both, minus + apart, minus - apart

    def up(value):
        return roll(value, 1, 0)

    def down(value):
        return roll(value, -1, 0)

    zpp, zmm, zpm, zmp = edges(bz + ay, rzy, nz, ny)
    y_zp = (up(zpp), down(zpm))
    y_zm = (up(zmp), down(zmm))
    xpp, xmm, xpm, xmp = edges(bz + ax, rzx, nz, nx)
    ypp, ymm, ypm, ymp = edges(by + ax, ryx, ny, nx)
    y_plus, y_minus = up(2.0 * (by + ny)), down(2.0 * (by - ny))
    ypp, ymp = up(ypp), down(ymp)
    ypm, ymm = up(ypm), down(ymm)
    x_plus, x_minus = 2.0 * (bx + nx), 2.0 * (bx - nx)
    syy_plus, syy_minus = ypp + ymp, ypm + ymm
    right = (x_plus + syy_plus, ypp - ymp, syy_plus, xpp, xmp)
    left = (x_minus + syy_minus, ypm - ymm, syy_minus, xpm, xmm)
    stay = (12.0 * t36, y_plus, y_minus, 2.0 * (bz + nz), y_zp, 2.0 * (bz - nz), y_zm)
    return stay, right, left


def plane_sums(stay, right, left):
    rest, y_plus, y_minus, z_plus, y_zp, z_minus, y_zm = stay
    syy = y_plus + y_minus
    sxx = right[0] + left[0]
    sums = [
        (rest + syy) + sxx,
        (y_plus - y_minus) + (right[1] + left[1]),
        right[0] - left[0],
        syy + (right[2] + left[2]),
        sxx,
        right[1] - left[1],
    ]
    for face, (one, two), plus, minus in ((z_plus, y_zp, right[3], left[3]), (z_minus, y_zm, right[4], left[4])):
        yy, xx = one + two, plus + minus
        sums += [face + (yy + xx), one - two, plus - minus, yy, xx]
    return sums


def gather_state(here, below, above, fluid):
    density = here[0] + (below[0] + above[0])
    third = density * (1.0 / 3.0)
    momentum = [
        fluid * (below[0] - above[0]),
        fluid * (here[1] + (below[1] + above[1])),
        fluid * (here[2] + (below[2] + above[2])),
    ]
    stress = [
        fluid * ((below[0] + above[0]) - third),
        fluid * ((here[3] + (below[3] + above[3])) - third),
        fluid * ((here[4] + (below[4] + above[4])) - third),
        fluid * (below[1] - above[1]),
        fluid * (below[2] - above[2]),
        fluid * here[5],
    ]
    return density, momentum, stress, third


PAIRS = ((0, 0), (1, 1), (2, 2), (0, 1), (0, 2), (1, 2))


def first_state(ref, where):
    density = ref[(0,) + where]
    speed = [ref[(1 + k,) + where] for k in range(3)]
    momentum = [density * speed[k] for k in range(3)]
    stress = [momentum[one] * speed[two] for one, two in PAIRS]
    return density, speed, momentum, stress


def row_differences(speed):
    return [roll(value, -1, 0) - roll(value, 1, 0) for value in speed]


def lane_differences(speed):
    return [roll(value, -1, 1) - roll(value, 1, 1) for value in speed]


def step_one(window, state, sums):
    for plane in range(1, 15):
        density, speed, momentum, stress = first_state(window, (plane,))
        dz = [window[1 + k, plane + 1] - window[1 + k, plane - 1] for k in range(3)]
        dy = row_differences(speed)
        dx = lane_differences(speed)
        relaxation = wale([[dz[k], dy[k], dx[k]] for k in range(3)])
        stay, right, left = leaving(density, momentum, collide(momentum, speed, stress, relaxation))
        right = [roll(value, 1, 1) for value in right]
        left = [roll(value, -1, 1) for value in left]
        for k, value in enumerate(plane_sums(stay, right, left)):
            sums[k, plane] = value
    for plane in range(2, 14):
        density, momentum, stress, _ = gather_state(
            [sums[k, plane] for k in range(6)],
            [sums[6 + k, plane - 1] for k in range(5)],
            [sums[11 + k, plane + 1] for k in range(5)],
            window[4, plane],
        )
        for k, value in enumerate([density] + momentum + stress):
            state[k, plane - 2] = value


def step_two(
    window, state_one, faces, from_left, from_right, placing, tags, moments_out, relaxation_out, outgoing,
    state, sums, strip, strip_sums, edge, pooled, moments, relaxations, left_sems,
):
    lane = lax.broadcasted_iota(jnp.int32, (16, 128), 1)
    first_lane, last_lane = lane == 0, lane == 127
    first_two, last_two = lane < 2, lane >= 126
    quarter = lax.broadcasted_iota(jnp.int32, (8, 128), 1) % 16 // 4

    for field in range(5):
        got_right, got_left = from_right[field], from_left[field]
        for half in range(2):
            for part in range(2):
                own = faces[field, part]
                turn = 8 * half + 4 * part
                cells = jnp.where(quarter == 0, roll(own, -8 * half, 1), roll(own, 8 - 8 * half, 1))
                cells = jnp.where(quarter == 1, roll(got_right, 4 - turn, 1), cells)
                strip[field, half, 8 * part : 8 * part + 8] = jnp.where(
                    quarter == 2, roll(got_left, 8 - turn, 1), cells
                )

    def strip_above(ref, number, half):
        return ref[number, 1] if half == 0 else roll(ref[number, 0], -16, 1)

    def strip_below(ref, number, half):
        return ref[number, 0] if half == 1 else roll(ref[number, 1], 16, 1)

    def strip_pass(step, half):
        if step == 0:
            density, speed, momentum, stress = first_state(strip, (half,))
        else:
            density = strip[0, half]
            speed = [strip[1 + k, half] for k in range(3)]
            momentum = [strip[5 + k, half] for k in range(3)]
            stress = [strip[8 + k, half] for k in range(6)]
        dz = [strip_above(strip, 1 + k, half) - strip_below(strip, 1 + k, half) for k in range(3)]
        dy = row_differences(speed)
        dx = lane_differences(speed)
        relaxation = wale([[dz[k], dy[k], dx[k]] for k in range(3)])
        return leaving(density, momentum, collide(momentum, speed, stress, relaxation))

    for half in range(2):
        stay, right, left = strip_pass(0, half)
        right = [roll(value, 1, 1) for value in right]
        left = [roll(value, -1, 1) for value in left]
        for k, value in enumerate(plane_sums(stay, right, left)):
            strip_sums[k, half] = value
    for half in range(2):
        density, momentum, stress, _ = gather_state(
            [strip_sums[k, half] for k in range(6)],
            [strip_below(strip_sums, 6 + k, half) for k in range(5)],
            [strip_above(strip_sums, 11 + k, half) for k in range(5)],
            strip[4, half],
        )
        inverse = 1.0 / density
        strip[0, half] = density
        for k in range(3):
            strip[1 + k, half] = momentum[k] * inverse
            strip[5 + k, half] = momentum[k]
        for k in range(6):
            strip[8 + k, half] = stress[k]

    for plane in range(2, 14):
        half, turn = plane % 2, plane // 2 * 16
        members = []
        for k, number in enumerate((0, 5, 6, 7, 8, 9, 10, 11, 12, 13)):
            value = jnp.where(first_two, roll(strip[number, half], -12 - turn, 1), state_one[k, plane - 2])
            members.append(jnp.where(last_two, roll(strip[number, half], 124 - turn, 1), value))
        inverse = 1.0 / members[0]
        for k in range(3):
            members.append(members[1 + k] * inverse)
        for k in range(13):
            state[k, plane] = members[k]

    for half in range(2):
        _, right, left = strip_pass(1, half)
        for k in range(5):
            edge[k, half] = right[k]
            edge[5 + k, half] = left[k]

    for plane in range(3, 13):
        half, turn = plane % 2, plane // 2 * 16

        def from_left_lane(value, ref, number):
            return jnp.where(first_lane, roll(ref[number, half], 117 - turn, 1), roll(value, 1, 1))

        def from_right_lane(value, ref, number):
            return jnp.where(last_lane, roll(ref[number, half], 123 - turn, 1), roll(value, -1, 1))

        density = state[0, plane]
        momentum = [state[1 + k, plane] for k in range(3)]
        stress = [state[4 + k, plane] for k in range(6)]
        speed = [state[10 + k, plane] for k in range(3)]
        dz = [state[10 + k, plane + 1] - state[10 + k, plane - 1] for k in range(3)]
        dy = row_differences(speed)
        dx = [
            from_right_lane(speed[k], strip, 1 + k) - from_left_lane(speed[k], strip, 1 + k)
            for k in range(3)
        ]
        relaxation = wale([[dz[k], dy[k], dx[k]] for k in range(3)])
        stay, right, left = leaving(density, momentum, collide(momentum, speed, stress, relaxation))
        right = [from_left_lane(value, edge, k) for k, value in enumerate(right)]
        left = [from_right_lane(value, edge, 5 + k) for k, value in enumerate(left)]
        for k, value in enumerate(plane_sums(stay, right, left)):
            sums[k, plane] = value[0:8]
        if 4 <= plane < 12:
            relaxations[plane - 4] = relaxation[0:8]
    copies = [pltpu.make_async_copy(relaxations, relaxation_out, left_sems.at[4])]
    copies[0].start()

    for pair in range(4):
        total = None
        for low in (2 * pair, 2 * pair + 1):
            plane = low + 4
            density, momentum, stress, third = gather_state(
                [sums[k, plane] for k in range(6)],
                [sums[6 + k, plane - 1] for k in range(5)],
                [sums[11 + k, plane + 1] for k in range(5)],
                window[4, plane, 0:8],
            )
            members = [density] + momentum + [stress[k] + third for k in range(3)] + stress[3:]
            for k in range(10):
                moments[k, low] = members[k]
            total = members if total is None else [one + two for one, two in zip(total, members)]
        for k in range(10):
            pooled[k * 32 + pair * 8 : k * 32 + pair * 8 + 8, :] = total[k]
        done = pl.ds(2 * pair, 2)
        copies.append(pltpu.make_async_copy(moments.at[:, done], moments_out.at[:, done], left_sems.at[pair]))
        copies[-1].start()

    blocks = 0.125 * (pooled[pl.ds(0, 160, stride=2), :] + pooled[pl.ds(1, 160, stride=2), :])
    payload = jnp.concatenate(
        [blocks, jnp.zeros((32, 128), jnp.float32), tags[...], jnp.zeros((48, 128), jnp.float32)], axis=0
    )
    placed = pick(placing[...], payload, ((1,), (1,)))
    outgoing[:, 0:128] = placed[0:OWNERS, 0:128]
    outgoing[:, 128:256] = placed[0:OWNERS, 128:256] + roll(placed[OWNERS:, 128:256], 32, 1)
    outgoing[:, 256:384] = placed[OWNERS:, 0:128]
    for copy in copies:
        copy.wait()


def sum_slots(arrived, coarse):
    slot = lax.broadcasted_iota(jnp.int32, (2 * OWNERS, SLOTS), 1).astype(jnp.float32)
    shared = arrived[:, 128:256]
    tag = jnp.concatenate([shared[:, 64:65], shared[:, 96:97]], axis=0)
    blocks = jnp.concatenate(
        [
            jnp.concatenate([arrived[:, 0:128], arrived[:, 256:384]], axis=0),
            jnp.concatenate([shared, roll(shared, -32, 1)], axis=0),
        ],
        axis=1,
    )
    total = pick((tag == slot + 1.0).astype(jnp.float32), blocks, ((0,), (0,)))
    coarse[...] = total[:, 0:160]


def call(kernel, outs, name, scratch=(), in_hbm=0, out_spaces=None):
    extra = {"in_specs": [pl.BlockSpec(memory_space=pltpu.HBM)] * in_hbm} if in_hbm else {}
    if out_spaces:
        extra["out_specs"] = tuple(pl.BlockSpec(memory_space=space) for space in out_spaces)
    return pl.pallas_call(
        kernel,
        out_shape=outs,
        scratch_shapes=list(scratch),
        name=name,
        compiler_params=pltpu.CompilerParams(vmem_limit_bytes=48 * 1024 * 1024),
        **extra,
    )


def per_device(density, velocity, solid, owner_map, slot_map):
    placing, tags = call(
        place_blocks,
        (f32(128, 128), f32(16, 128)),
        "place_blocks",
        (pltpu.VMEM((1, 64), jnp.int32), pltpu.VMEM((1, 64), jnp.int32), pltpu.SemaphoreType.DMA((2,))),
        2,
    )(owner_map.reshape(1, 64), slot_map.reshape(1, 64))
    scalars = jnp.concatenate([density[None], 1.0 - solid[None].astype(jnp.float32)])
    near, far = call(pack_vertical, (f32(17, 8, 128),) * 2, "pack_vertical")(scalars, velocity)
    near, far = swap(near, far, "gz")
    planes, high, low = call(
        pack_spanwise, (f32(5, 16, 8, 128), f32(34, 8, 128), f32(34, 8, 128)), "pack_spanwise"
    )(scalars, velocity, far, near, placing)
    above = from_upper(low, "gy")
    below = from_lower(high, "gy")
    window, faces, right, left = call(
        pack_streamwise,
        (f32(5, 16, 16, 128), f32(5, 2, 8, 128), f32(5, 8, 128), f32(5, 8, 128)),
        "pack_streamwise",
    )(planes, above, below)
    right, left = from_lower(right, "gx"), from_upper(left, "gx")
    state = call(
        step_one, f32(10, 12, 16, 128), "step_one", (pltpu.VMEM((16, 16, 16, 128), jnp.float32),)
    )(window)
    moments, relaxation, outgoing = call(
        step_two,
        (f32(10, 8, 8, 128), f32(8, 8, 128), f32(OWNERS, 384)),
        "step_two",
        (
            pltpu.VMEM((13, 16, 16, 128), jnp.float32),
            pltpu.VMEM((16, 16, 8, 128), jnp.float32),
            pltpu.VMEM((14, 2, 16, 128), jnp.float32),
            pltpu.VMEM((16, 2, 16, 128), jnp.float32),
            pltpu.VMEM((10, 2, 16, 128), jnp.float32),
            pltpu.VMEM((320, 128), jnp.float32),
            pltpu.VMEM((10, 8, 8, 128), jnp.float32),
            pltpu.VMEM((8, 8, 128), jnp.float32),
            pltpu.SemaphoreType.DMA((5,)),
        ),
        out_spaces=(pltpu.HBM, pltpu.HBM, pltpu.VMEM),
    )(window, state, faces, right, left, placing, tags)
    arrived = lax.all_to_all(
        outgoing.reshape(OWNERS, 1, 384), ("gz", "gy"), split_axis=0, concat_axis=0, tiled=True
    )
    coarse = call(sum_slots, f32(SLOTS, 160), "sum_slots")(arrived.reshape(OWNERS, 384))
    return moments, relaxation, coarse.reshape(1, 1, 1, SLOTS, 160)


def solution(mesh):
    return jax.shard_map(
        per_device,
        mesh=mesh,
        in_specs=(
            P("gz", "gy", "gx"),
            P(None, "gz", "gy", "gx"),
            P("gz", "gy", "gx"),
            P("gx", "gy", "gz", None, None),
            P("gx", "gy", "gz", None, None),
        ),
        out_specs=(P(None, "gz", "gy", "gx"), P("gz", "gy", "gx"), P("gx", "gy", "gz", None, None)),
        check_vma=False,
    )
```

```python
import jax
import jax.numpy as jnp
from jax import lax
from jax.experimental import pallas as pl
from jax.experimental.pallas import tpu as pltpu
from jax.sharding import PartitionSpec as P

SLOTS = 16
SPAN_Y = 8
SPAN_Z = 8
OWNERS = SPAN_Y * SPAN_Z
WALE_COEFF = 0.5
BASE_VISCOSITY = 0.01
WALE_FLOOR = 1e-10


def f32(*shape):
    return jax.ShapeDtypeStruct(shape, jnp.float32)


def roll(value, shift, axis):
    size = value.shape[axis]
    if isinstance(shift, int):
        shift = shift % size
        if shift == 0:
            return value
    return pltpu.roll(value, shift, axis)


def is_even(axis):
    return lax.rem(lax.axis_index(axis), 2) == 0


def from_lower(high, axis):
    count = lax.axis_size(axis)
    return lax.ppermute(high, axis, [(i, (i + 1) % count) for i in range(count)])


def from_upper(low, axis):
    count = lax.axis_size(axis)
    return lax.ppermute(low, axis, [((i + 1) % count, i) for i in range(count)])


def swap(near, far, axis):
    count = lax.axis_size(axis)
    near_pairs = [(i, i ^ 1) for i in range(count)]
    far_pairs = [(i, (i + 1) % count if i % 2 else (i - 1) % count) for i in range(count)]
    far = lax.ppermute(far, axis, far_pairs)
    return lax.ppermute(near, axis, near_pairs), far


def pack_vertical(scalars, velocity, near, far):
    even = is_even("gz")
    for out, upper in ((near, even), (far, jnp.logical_not(even))):

        def face(depth):
            return pl.ds(jnp.where(upper, 8 - depth, 0), depth)

        for axis in range(3):
            out[4 * axis : 4 * axis + 4] = velocity[axis, face(4)] * scalars[1, face(4)]
        out[12:15] = scalars[0, face(3)]
        out[15:17] = scalars[1, face(2)]


def pack_spanwise(scalars, velocity, got_far, got_near, placing, planes, high, low):
    del placing
    even = is_even("gz")
    row = lax.broadcasted_iota(jnp.int32, (8, 128), 0)
    front = row < 4

    def got_above(first, last):
        return jnp.where(even, got_near[first:last], got_far[first:last])

    def got_below(first, last):
        return jnp.where(even, got_far[first:last], got_near[first:last])

    fluid = scalars[1]
    planes[0, 4:12] = scalars[0]
    planes[0, 12:15] = got_above(12, 15)
    planes[0, 1:4] = got_below(12, 15)
    planes[0, 15] = jnp.ones((8, 128), jnp.float32)
    planes[0, 0] = jnp.ones((8, 128), jnp.float32)
    for axis in range(3):
        planes[1 + axis, 4:12] = velocity[axis] * fluid
        planes[1 + axis, 12:16] = got_above(4 * axis, 4 * axis + 4)
        planes[1 + axis, 0:4] = got_below(4 * axis, 4 * axis + 4)
    planes[4, 4:12] = fluid
    planes[4, 12:14] = got_above(15, 17)
    planes[4, 2:4] = got_below(15, 17)
    planes[4, 14:16] = jnp.zeros((2, 8, 128), jnp.float32)
    planes[4, 0:2] = jnp.zeros((2, 8, 128), jnp.float32)

    def pack(place, field, one, two):
        one, two = planes[field, one], planes[field, two]
        high[place] = jnp.where(front, roll(one, 4, 0), two)
        low[place] = jnp.where(front, one, roll(two, 4, 0))

    for axis in range(3):
        for pair in range(8):
            pack(8 * axis + pair, 1 + axis, 2 * pair, 2 * pair + 1)
    for pair in range(7):
        pack(24 + pair, 0, 2 * pair + 1, 2 * pair + 2)
    for place in range(3):
        upper, lower = None, None
        for part in range(4):
            cells = planes[4, 2 + 4 * place + part]
            moved_high, moved_low = roll(cells, 2 * part + 2, 0), roll(cells, 2 * part, 0)
            upper = moved_high if part == 0 else jnp.where(row // 2 == part, moved_high, upper)
            lower = moved_low if part == 0 else jnp.where(row // 2 == part, moved_low, lower)
        high[31 + place] = upper
        low[31 + place] = lower


def gather_faces(cells, plane, moved):
    lane = lax.broadcasted_iota(jnp.int32, (8, 128), 1)
    return jnp.where(lane // 8 == plane, roll(cells, 8 * plane + 4, 1), moved)


def pack_inner(planes, inner_faces):
    for field in range(5):
        moved = jnp.zeros((8, 128), jnp.float32)
        for plane in range(16):
            moved = gather_faces(planes[field, plane], plane, moved)
        inner_faces[field] = moved


def pack_streamwise(inner_faces, got_above, got_below, outer, faces, right, left):
    row = lax.broadcasted_iota(jnp.int32, (8, 128), 0)
    front = row < 4
    lane = lax.broadcasted_iota(jnp.int32, (8, 128), 1)

    def outer_rows(field, plane):
        if field == 4:
            if not 2 <= plane < 14:
                return jnp.zeros((8, 128), jnp.float32)
            place, part = 31 + (plane - 2) // 4, (plane - 2) % 4
            below = jnp.where(row >= 6, roll(got_below[place], 6 - 2 * part, 0), 0.0)
            return jnp.where(row < 2, roll(got_above[place], -2 * part, 0), below)
        if field == 0:
            if not 1 <= plane < 15:
                return jnp.ones((8, 128), jnp.float32)
            place, second = 24 + (plane - 1) // 2, (plane - 1) % 2
        else:
            place, second = 8 * (field - 1) + plane // 2, plane % 2
        above, below = got_above[place], got_below[place]
        if second:
            return jnp.where(front, roll(above, 4, 0), below)
        return jnp.where(front, above, roll(below, 4, 0))

    for field in range(5):
        own = [inner_faces[field], jnp.zeros((8, 128), jnp.float32)]
        for plane in range(16):
            cells = outer_rows(field, plane)
            outer[field, plane] = cells
            own[1] = gather_faces(cells, plane, own[1])
        faces[field, 0] = own[0]
        faces[field, 1] = own[1]
        even_spot = lane % 8 < 4
        right[field] = jnp.where(even_spot, own[0], roll(own[1], 4, 1))
        left[field] = jnp.where(even_spot, roll(own[0], -4, 1), own[1])


def place_blocks(owners_in, slots_in, placing, tags, owners, slots, arrived):
    copies = [
        pltpu.make_async_copy(source, target, arrived.at[number])
        for number, (source, target) in enumerate(((owners_in, owners), (slots_in, slots)))
    ]
    for copy in copies:
        copy.start()
    for copy in copies:
        copy.wait()
    row = lax.broadcasted_iota(jnp.int32, (64, 128), 0)
    block = lax.broadcasted_iota(jnp.int32, (64, 128), 1) // 2
    diagonal = lax.broadcasted_iota(jnp.int32, (64, 64), 0) == lax.broadcasted_iota(jnp.int32, (64, 64), 1)
    owner_column = jnp.sum(jnp.where(diagonal, owners[...].astype(jnp.float32), 0.0), axis=1, keepdims=True)
    slot_column = jnp.sum(jnp.where(diagonal, slots[...].astype(jnp.float32), 0.0), axis=1, keepdims=True)
    owner_row = jnp.sum(jnp.where(row == block, owner_column, 0.0), axis=0, keepdims=True)
    slot = jnp.sum(jnp.where(row == block, slot_column, 0.0), axis=0, keepdims=True)
    earlier = (owner_column == owner_row) & (row < block)
    owner = owner_row.astype(jnp.int32)
    rank = jnp.sum(jnp.where(earlier, 1.0, 0.0), axis=0, keepdims=True).astype(jnp.int32)
    position = rank * OWNERS + lax.rem(owner, SPAN_Z) * SPAN_Y + lax.div(owner, SPAN_Z)
    rows = lax.broadcasted_iota(jnp.int32, (128, 128), 0)
    placing[...] = (rows == position).astype(jnp.float32)
    tags[...] = jnp.broadcast_to(0.5 * (slot + 1.0), (16, 128))


def pick(chosen, values, contract):
    chosen = chosen.astype(jnp.bfloat16)
    total = None
    for _ in range(3):
        part = values.astype(jnp.bfloat16)
        values = values - part.astype(jnp.float32)
        product = lax.dot_general(chosen, part, (contract, ((), ())), preferred_element_type=jnp.float32)
        total = product if total is None else total + product
    return total


def wale(doubled):
    (g00, g01, g02), (g10, g11, g12), (g20, g21, g22) = doubled
    s01, s02, s12 = g01 + g10, g02 + g20, g12 + g21
    q0, q1, q2 = g00 * g00, g11 * g11, g22 * g22
    strain = 0.25 * ((q0 + q1 + q2) + 0.5 * (s01 * s01 + s02 * s02 + s12 * s12))
    p01, p02, p12 = g01 * g10, g02 * g20, g12 * g21
    d0, d1, d2 = q0 + (p01 + p02), q1 + (p01 + p12), q2 + (p02 + p12)
    third = (d0 + d1 + d2) * (1.0 / 3.0)
    d0, d1, d2 = d0 - third, d1 - third, d2 - third
    d01 = (g00 + g11) * s01 + (g02 * g21 + g12 * g20)
    d02 = (g00 + g22) * s02 + (g01 * g12 + g21 * g10)
    d12 = (g11 + g22) * s12 + (g10 * g02 + g20 * g01)
    deviator = 0.0625 * ((d0 * d0 + d1 * d1 + d2 * d2) + 0.5 * (d01 * d01 + d02 * d02 + d12 * d12))
    root = jnp.sqrt(deviator)
    eddy = (WALE_COEFF * WALE_COEFF) * deviator * root / (
        strain * strain * jnp.sqrt(strain) + deviator * jnp.sqrt(root) + WALE_FLOOR
    )
    return 0.5 + 3.0 * (BASE_VISCOSITY + eddy)


def collide(momentum, speed, stress, relaxation):
    retained = 1.0 - 1.0 / relaxation
    post = []
    for column, (one, two) in enumerate(((0, 0), (1, 1), (2, 2), (0, 1), (0, 2), (1, 2))):
        balance = momentum[one] * speed[two]
        post.append(balance + retained * (stress[column] - balance))
    return post


def leaving(density, momentum, post):
    t36 = density * (1.0 / 36.0) - (post[0] + post[1] + post[2]) * (1.0 / 24.0)
    az, ay, ax = (0.125 * post[k] for k in range(3))
    rzy, rzx, ryx = (0.25 * post[k] for k in range(3, 6))
    nz, ny, nx = ((1.0 / 12.0) * momentum[k] for k in range(3))
    bz, by, bx = t36 + az, t36 + ay, t36 + ax

    def edges(base, cross, one, two):
        plus, minus = base + cross, base - cross
        both, apart = one + two, one - two
        return plus + both, plus - both, minus + apart, minus - apart

    def up(value):
        return roll(value, 1, 0)

    def down(value):
        return roll(value, -1, 0)

    zpp, zmm, zpm, zmp = edges(bz + ay, rzy, nz, ny)
    y_zp = (up(zpp), down(zpm))
    y_zm = (up(zmp), down(zmm))
    xpp, xmm, xpm, xmp = edges(bz + ax, rzx, nz, nx)
    ypp, ymm, ypm, ymp = edges(by + ax, ryx, ny, nx)
    y_plus, y_minus = up(2.0 * (by + ny)), down(2.0 * (by - ny))
    ypp, ymp = up(ypp), down(ymp)
    ypm, ymm = up(ypm), down(ymm)
    x_plus, x_minus = 2.0 * (bx + nx), 2.0 * (bx - nx)
    syy_plus, syy_minus = ypp + ymp, ypm + ymm
    right = (x_plus + syy_plus, ypp - ymp, syy_plus, xpp, xmp)
    left = (x_minus + syy_minus, ypm - ymm, syy_minus, xpm, xmm)
    stay = (12.0 * t36, y_plus, y_minus, 2.0 * (bz + nz), y_zp, 2.0 * (bz - nz), y_zm)
    return stay, right, left


def plane_sums(stay, right, left):
    rest, y_plus, y_minus, z_plus, y_zp, z_minus, y_zm = stay
    syy = y_plus + y_minus
    sxx = right[0] + left[0]
    sums = [
        (rest + syy) + sxx,
        (y_plus - y_minus) + (right[1] + left[1]),
        right[0] - left[0],
        syy + (right[2] + left[2]),
        sxx,
        right[1] - left[1],
    ]
    for face, (one, two), plus, minus in ((z_plus, y_zp, right[3], left[3]), (z_minus, y_zm, right[4], left[4])):
        yy, xx = one + two, plus + minus
        sums += [face + (yy + xx), one - two, plus - minus, yy, xx]
    return sums


def gather_state(here, below, above, fluid):
    density = here[0] + (below[0] + above[0])
    third = density * (1.0 / 3.0)
    momentum = [
        fluid * (below[0] - above[0]),
        fluid * (here[1] + (below[1] + above[1])),
        fluid * (here[2] + (below[2] + above[2])),
    ]
    stress = [
        fluid * ((below[0] + above[0]) - third),
        fluid * ((here[3] + (below[3] + above[3])) - third),
        fluid * ((here[4] + (below[4] + above[4])) - third),
        fluid * (below[1] - above[1]),
        fluid * (below[2] - above[2]),
        fluid * here[5],
    ]
    return density, momentum, stress, third


PAIRS = ((0, 0), (1, 1), (2, 2), (0, 1), (0, 2), (1, 2))


def first_state(member):
    density = member(0)
    speed = [member(1 + k) for k in range(3)]
    momentum = [density * speed[k] for k in range(3)]
    stress = [momentum[one] * speed[two] for one, two in PAIRS]
    return density, speed, momentum, stress


def row_differences(speed):
    return [roll(value, -1, 0) - roll(value, 1, 0) for value in speed]


def lane_differences(speed):
    return [roll(value, -1, 1) - roll(value, 1, 1) for value in speed]


def step_one(planes, outer, state, sums):
    def cells(number, plane):
        return jnp.concatenate([planes[number, plane], outer[number, plane]], axis=0)

    for plane in range(1, 15):
        density, speed, momentum, stress = first_state(lambda number: cells(number, plane))
        dz = [cells(1 + k, plane + 1) - cells(1 + k, plane - 1) for k in range(3)]
        dy = row_differences(speed)
        dx = lane_differences(speed)
        relaxation = wale([[dz[k], dy[k], dx[k]] for k in range(3)])
        stay, right, left = leaving(density, momentum, collide(momentum, speed, stress, relaxation))
        right = [roll(value, 1, 1) for value in right]
        left = [roll(value, -1, 1) for value in left]
        for k, value in enumerate(plane_sums(stay, right, left)):
            sums[k, plane] = value
    for plane in range(2, 14):
        density, momentum, stress, _ = gather_state(
            [sums[k, plane] for k in range(6)],
            [sums[6 + k, plane - 1] for k in range(5)],
            [sums[11 + k, plane + 1] for k in range(5)],
            cells(4, plane),
        )
        for k, value in enumerate([density] + momentum + stress):
            state[k, plane - 2] = value


def step_two(
    planes, state_one, faces, from_left, from_right, placing, tags, moments_out, relaxation_out, outgoing,
    state, sums, strip, strip_sums, edge, pooled, moments, relaxations, left_sems,
):
    lane = lax.broadcasted_iota(jnp.int32, (16, 128), 1)
    first_lane, last_lane = lane == 0, lane == 127
    first_two, last_two = lane < 2, lane >= 126
    quarter = lax.broadcasted_iota(jnp.int32, (8, 128), 1) % 16 // 4

    for field in range(5):
        got_right, got_left = from_right[field], from_left[field]
        for half in range(2):
            for part in range(2):
                own = faces[field, part]
                turn = 8 * half + 4 * part
                cells = jnp.where(quarter == 0, roll(own, -8 * half, 1), roll(own, 8 - 8 * half, 1))
                cells = jnp.where(quarter == 1, roll(got_right, 4 - turn, 1), cells)
                strip[field, half, 8 * part : 8 * part + 8] = jnp.where(
                    quarter == 2, roll(got_left, 8 - turn, 1), cells
                )

    def strip_above(ref, number, half):
        return ref[number, 1] if half == 0 else roll(ref[number, 0], -16, 1)

    def strip_below(ref, number, half):
        return ref[number, 0] if half == 1 else roll(ref[number, 1], 16, 1)

    def strip_pass(step, half):
        if step == 0:
            density, speed, momentum, stress = first_state(lambda number: strip[number, half])
        else:
            density = strip[0, half]
            speed = [strip[1 + k, half] for k in range(3)]
            momentum = [strip[5 + k, half] for k in range(3)]
            stress = [strip[8 + k, half] for k in range(6)]
        dz = [strip_above(strip, 1 + k, half) - strip_below(strip, 1 + k, half) for k in range(3)]
        dy = row_differences(speed)
        dx = lane_differences(speed)
        relaxation = wale([[dz[k], dy[k], dx[k]] for k in range(3)])
        return leaving(density, momentum, collide(momentum, speed, stress, relaxation))

    for half in range(2):
        stay, right, left = strip_pass(0, half)
        right = [roll(value, 1, 1) for value in right]
        left = [roll(value, -1, 1) for value in left]
        for k, value in enumerate(plane_sums(stay, right, left)):
            strip_sums[k, half] = value
    for half in range(2):
        density, momentum, stress, _ = gather_state(
            [strip_sums[k, half] for k in range(6)],
            [strip_below(strip_sums, 6 + k, half) for k in range(5)],
            [strip_above(strip_sums, 11 + k, half) for k in range(5)],
            strip[4, half],
        )
        inverse = 1.0 / density
        strip[0, half] = density
        for k in range(3):
            strip[1 + k, half] = momentum[k] * inverse
            strip[5 + k, half] = momentum[k]
        for k in range(6):
            strip[8 + k, half] = stress[k]

    for plane in range(2, 14):
        half, turn = plane % 2, plane // 2 * 16
        members = []
        for k, number in enumerate((0, 5, 6, 7, 8, 9, 10, 11, 12, 13)):
            value = jnp.where(first_two, roll(strip[number, half], -12 - turn, 1), state_one[k, plane - 2])
            members.append(jnp.where(last_two, roll(strip[number, half], 124 - turn, 1), value))
        inverse = 1.0 / members[0]
        for k in range(3):
            members.append(members[1 + k] * inverse)
        for k in range(13):
            state[k, plane] = members[k]

    for half in range(2):
        _, right, left = strip_pass(1, half)
        for k in range(5):
            edge[k, half] = right[k]
            edge[5 + k, half] = left[k]

    for plane in range(3, 13):
        half, turn = plane % 2, plane // 2 * 16

        def from_left_lane(value, ref, number):
            return jnp.where(first_lane, roll(ref[number, half], 117 - turn, 1), roll(value, 1, 1))

        def from_right_lane(value, ref, number):
            return jnp.where(last_lane, roll(ref[number, half], 123 - turn, 1), roll(value, -1, 1))

        density = state[0, plane]
        momentum = [state[1 + k, plane] for k in range(3)]
        stress = [state[4 + k, plane] for k in range(6)]
        speed = [state[10 + k, plane] for k in range(3)]
        dz = [state[10 + k, plane + 1] - state[10 + k, plane - 1] for k in range(3)]
        dy = row_differences(speed)
        dx = [
            from_right_lane(speed[k], strip, 1 + k) - from_left_lane(speed[k], strip, 1 + k)
            for k in range(3)
        ]
        relaxation = wale([[dz[k], dy[k], dx[k]] for k in range(3)])
        stay, right, left = leaving(density, momentum, collide(momentum, speed, stress, relaxation))
        right = [from_left_lane(value, edge, k) for k, value in enumerate(right)]
        left = [from_right_lane(value, edge, 5 + k) for k, value in enumerate(left)]
        for k, value in enumerate(plane_sums(stay, right, left)):
            sums[k, plane] = value[0:8]
        if 4 <= plane < 12:
            relaxations[plane - 4] = relaxation[0:8]
    copies = [pltpu.make_async_copy(relaxations, relaxation_out, left_sems.at[4])]
    copies[0].start()

    for pair in range(4):
        total = None
        for low in (2 * pair, 2 * pair + 1):
            plane = low + 4
            density, momentum, stress, third = gather_state(
                [sums[k, plane] for k in range(6)],
                [sums[6 + k, plane - 1] for k in range(5)],
                [sums[11 + k, plane + 1] for k in range(5)],
                planes[4, plane],
            )
            members = [density] + momentum + [stress[k] + third for k in range(3)] + stress[3:]
            for k in range(10):
                moments[k, low] = members[k]
            total = members if total is None else [one + two for one, two in zip(total, members)]
        for k in range(10):
            pooled[k * 32 + pair * 8 : k * 32 + pair * 8 + 8, :] = total[k]
        done = pl.ds(2 * pair, 2)
        copies.append(pltpu.make_async_copy(moments.at[:, done], moments_out.at[:, done], left_sems.at[pair]))
        copies[-1].start()

    blocks = 0.125 * (pooled[pl.ds(0, 160, stride=2), :] + pooled[pl.ds(1, 160, stride=2), :])
    payload = jnp.concatenate(
        [blocks, jnp.zeros((32, 128), jnp.float32), tags[...], jnp.zeros((48, 128), jnp.float32)], axis=0
    )
    placed = pick(placing[...], payload, ((1,), (1,)))
    outgoing[:, 0:128] = placed[0:OWNERS, 0:128]
    outgoing[:, 128:256] = placed[0:OWNERS, 128:256] + roll(placed[OWNERS:, 128:256], 32, 1)
    outgoing[:, 256:384] = placed[OWNERS:, 0:128]
    for copy in copies:
        copy.wait()


def sum_slots(arrived, coarse):
    slot = lax.broadcasted_iota(jnp.int32, (2 * OWNERS, SLOTS), 1).astype(jnp.float32)
    shared = arrived[:, 128:256]
    tag = jnp.concatenate([shared[:, 64:65], shared[:, 96:97]], axis=0)
    blocks = jnp.concatenate(
        [
            jnp.concatenate([arrived[:, 0:128], arrived[:, 256:384]], axis=0),
            jnp.concatenate([shared, roll(shared, -32, 1)], axis=0),
        ],
        axis=1,
    )
    total = pick((tag == slot + 1.0).astype(jnp.float32), blocks, ((0,), (0,)))
    coarse[...] = total[:, 0:160]


def call(kernel, outs, name, scratch=(), in_hbm=0, out_spaces=None):
    extra = {"in_specs": [pl.BlockSpec(memory_space=pltpu.HBM)] * in_hbm} if in_hbm else {}
    if out_spaces:
        extra["out_specs"] = tuple(pl.BlockSpec(memory_space=space) for space in out_spaces)
    return pl.pallas_call(
        kernel,
        out_shape=outs,
        scratch_shapes=list(scratch),
        name=name,
        compiler_params=pltpu.CompilerParams(vmem_limit_bytes=48 * 1024 * 1024),
        **extra,
    )


def per_device(density, velocity, solid, owner_map, slot_map):
    placing, tags = call(
        place_blocks,
        (f32(128, 128), f32(16, 128)),
        "place_blocks",
        (pltpu.VMEM((1, 64), jnp.int32), pltpu.VMEM((1, 64), jnp.int32), pltpu.SemaphoreType.DMA((2,))),
        2,
    )(owner_map.reshape(1, 64), slot_map.reshape(1, 64))
    scalars = jnp.concatenate([density[None], 1.0 - solid[None].astype(jnp.float32)])
    near, far = call(pack_vertical, (f32(17, 8, 128),) * 2, "pack_vertical")(scalars, velocity)
    near, far = swap(near, far, "gz")
    planes, high, low = call(
        pack_spanwise, (f32(5, 16, 8, 128), f32(34, 8, 128), f32(34, 8, 128)), "pack_spanwise"
    )(scalars, velocity, far, near, placing)
    above = from_upper(low, "gy")
    below = from_lower(high, "gy")
    (inner_faces,) = call(pack_inner, (f32(5, 8, 128),), "pack_inner")(planes)
    outer, faces, right, left = call(
        pack_streamwise,
        (f32(5, 16, 8, 128), f32(5, 2, 8, 128), f32(5, 8, 128), f32(5, 8, 128)),
        "pack_streamwise",
    )(inner_faces, above, below)
    right, left = from_lower(right, "gx"), from_upper(left, "gx")
    state = call(
        step_one, f32(10, 12, 16, 128), "step_one", (pltpu.VMEM((16, 16, 16, 128), jnp.float32),)
    )(planes, outer)
    moments, relaxation, outgoing = call(
        step_two,
        (f32(10, 8, 8, 128), f32(8, 8, 128), f32(OWNERS, 384)),
        "step_two",
        (
            pltpu.VMEM((13, 16, 16, 128), jnp.float32),
            pltpu.VMEM((16, 16, 8, 128), jnp.float32),
            pltpu.VMEM((14, 2, 16, 128), jnp.float32),
            pltpu.VMEM((16, 2, 16, 128), jnp.float32),
            pltpu.VMEM((10, 2, 16, 128), jnp.float32),
            pltpu.VMEM((320, 128), jnp.float32),
            pltpu.VMEM((10, 8, 8, 128), jnp.float32),
            pltpu.VMEM((8, 8, 128), jnp.float32),
            pltpu.SemaphoreType.DMA((5,)),
        ),
        out_spaces=(pltpu.HBM, pltpu.HBM, pltpu.VMEM),
    )(planes, state, faces, right, left, placing, tags)
    arrived = lax.all_to_all(
        outgoing.reshape(OWNERS, 1, 384), ("gz", "gy"), split_axis=0, concat_axis=0, tiled=True
    )
    coarse = call(sum_slots, f32(SLOTS, 160), "sum_slots")(arrived.reshape(OWNERS, 384))
    return moments, relaxation, coarse.reshape(1, 1, 1, SLOTS, 160)


def solution(mesh):
    return jax.shard_map(
        per_device,
        mesh=mesh,
        in_specs=(
            P("gz", "gy", "gx"),
            P(None, "gz", "gy", "gx"),
            P("gz", "gy", "gx"),
            P("gx", "gy", "gz", None, None),
            P("gx", "gy", "gz", None, None),
        ),
        out_specs=(P(None, "gz", "gy", "gx"), P("gz", "gy", "gx"), P("gx", "gy", "gz", None, None)),
        check_vma=False,
    )
```
